32 devices in a mesh: dp: 8 (over z, y), fsdp: 4 (over x, core).
Axes of the slice: x: 2, y: 2, z: 4, core: 2. Of those that a mesh axis runs over, the one named last changes fastest.
Arguments:
- frames: bfloat16 [2, 32, 256, 1024], P(None, ('dp', 'fsdp')), may hold values from -6 to 6
- skip: bfloat16 [2, 32, 256, 1024], P(None, ('dp', 'fsdp')), may hold values from -6 to 6
- cotangent: bfloat16 [2, 32, 256, 1024], P(None, ('dp', 'fsdp')), may hold values from -6 to 6
- segment_ids: int32 [2, 32, 256], P(None, ('dp', 'fsdp')), may hold values from 0 to 3, never falling along the last dimension, each value on 1 to 128 neighbouring positions
- row_lengths: int32 [2, 32], P(None, ('dp', 'fsdp')), may hold values from 128 to 256
- w_skip: bfloat16 [2048, 1024], P(('dp', 'fsdp')), may hold values from -0.125 to 0.125
- b_skip: bfloat16 [1024], P(('dp', 'fsdp')), may hold values from -1.1953125 to 1.1953125
- gain_one: bfloat16 [1024], P(('dp', 'fsdp')), may hold values from 0.25 to 1.75
- w_qkv: bfloat16 [1024, 3072], P(('dp', 'fsdp')), may hold values from -0.1875 to 0.1875
- w_out: bfloat16 [1024, 1024], P(('dp', 'fsdp')), may hold values from -0.5 to 0.5
- gain_two: bfloat16 [1024], P(('dp', 'fsdp')), may hold values from 0.25 to 1.75
- w_up: bfloat16 [1024, 4096], P(('dp', 'fsdp')), may hold values from -0.1875 to 0.1875
- b_up: bfloat16 [4096], P(('dp', 'fsdp')), may hold values from -1.1953125 to 1.1953125
- w_down: bfloat16 [4096, 1024], P(('dp', 'fsdp')), may hold values from -0.09375 to 0.09375
- b_down: bfloat16 [1024], P(('dp', 'fsdp')), may hold values from -1.1953125 to 1.1953125
Outputs:
- output: bfloat16 [2, 32, 256, 1024], P(None, ('dp', 'fsdp'))
- frames_grad: float32 [2, 32, 256, 1024], P(None, ('dp', 'fsdp'))
- skip_grad: float32 [2, 32, 256, 1024], P(None, ('dp', 'fsdp'))
- w_skip_grad: float32 [2048, 1024], P(('dp', 'fsdp'))
- b_skip_grad: float32 [1024], P(('dp', 'fsdp'))
- gain_one_grad: float32 [1024], P(('dp', 'fsdp'))
- w_qkv_grad: float32 [1024, 3072], P(('dp', 'fsdp'))
- w_out_grad: float32 [1024, 1024], P(('dp', 'fsdp'))
- gain_two_grad: float32 [1024], P(('dp', 'fsdp'))
- w_up_grad: float32 [1024, 4096], P(('dp', 'fsdp'))
- b_up_grad: float32 [4096], P(('dp', 'fsdp'))
- w_down_grad: float32 [4096, 1024], P(('dp', 'fsdp'))
- b_down_grad: float32 [1024], P(('dp', 'fsdp'))
The draws below stay inside these ranges and needn't reach their ends.
All inputs are finite; a program needn't handle non-finite values.
Results may differ from the reference program's by a relative error of at most 0.012.
Values may be sent and summed in bfloat16 or wider, within the bound.
No kernel may reach another device: no remote copies, remote signals or barrier semaphores. Data moves between devices by JAX's collectives and lax.ppermute only.
A program may use at most 256 MiB of HBM per device.

```python
import math
import jax
import jax.numpy as jnp
import numpy as np
from jax import lax

D = 1024
HEADS = 16
HEAD = 64
FF = 4096
ROW = 256
MICRO = 2
SEGS = 4
ROWS = 32


def set_ends(values, rng, smallest, largest):
    place = [jax.random.randint(jax.random.fold_in(rng, axis), (), 0, length) for axis, length in enumerate(values.shape)]
    longest = values.shape.index(max(values.shape))
    neighbour = place[:longest] + [(place[longest] + 1) % values.shape[longest]] + place[longest + 1:]
    return values.at[tuple(place)].set(smallest).at[tuple(neighbour)].set(largest)


def steps_of(stream_key, extent, shards, least, high):
    factor_of = 1.0
    for axis_at, shards_of in shards:
        draws = jax.random.uniform(jax.random.fold_in(jax.random.fold_in(stream_key, 6), axis_at), (shards_of,), jnp.float32, least / len(shards), high / len(shards))
        factor_of = factor_of * jnp.repeat(jnp.exp(draws), extent[axis_at] // shards_of).reshape((-1,) + (1,) * (len(extent) - 1 - axis_at))
    return factor_of


def split_up(amount, total, limit, skew):
    portions = [(1 << 20) // math.isqrt(standing ** skew) + 1 for standing in range(2, amount + 1)]
    spare, holding = total - limit - (amount - 1), [1] * (amount - 1)
    while spare > 0:
        candidates = [i for i in range(amount - 1) if holding[i] < limit]
        pool, budget = sum([portions[i] for i in candidates]), spare
        for i in candidates:
            extra = min(limit - holding[i], max(1, budget * portions[i] // pool), spare)
            holding[i] = holding[i] + extra
            spare = spare - extra
    return np.array([limit] + holding)


def uneven(key, count, total, most, skew):
    if count == 2:
        one = jax.random.randint(key, (), max(1, total - most), min(most, total - 1) + 1)
        return jnp.stack([one, total - one])
    sizes = jnp.asarray(split_up(count, total, most, skew), jnp.int32)
    pairs = (count - 1) // 2
    donor, receiver = sizes[1:1 + 2 * pairs:2], sizes[2:2 + 2 * pairs:2]
    slack = jnp.minimum(donor - 1, most - receiver)
    shifted = jax.random.randint(jax.random.fold_in(key, 1), (pairs,), 0, 1 << 20) % (slack + 1)
    sizes = sizes.at[1:1 + 2 * pairs:2].set(donor - shifted).at[2:2 + 2 * pairs:2].set(receiver + shifted)
    return sizes[jax.random.permutation(jax.random.fold_in(key, 2), count)]


def centred(rng, shape, spread, limit, shards=(), kind=jnp.bfloat16):
    level = steps_of(rng, shape, shards, -0.22, 0.18) if shards else 1.0
    entries = jax.random.normal(rng, shape, jnp.float32) * spread * level
    return jnp.minimum(jnp.maximum(entries, -limit), limit).astype(kind)


def setup_inputs(seed: int = 0) -> dict:
    seeds = jax.random.split(jax.random.key(seed), 16)
    frames = centred(seeds[0], (MICRO, ROWS, ROW, D), 1.0, 6.0, ((1, 32),))
    skip = centred(seeds[1], (MICRO, ROWS, ROW, D), 1.0, 6.0, ((1, 32),))
    cotangent = centred(seeds[2], (MICRO, ROWS, ROW, D), 1.0, 6.0, ((1, 32),))
    segment_ids = jax.vmap(lambda own: jnp.searchsorted(jnp.cumsum(uneven(own, SEGS, ROW, ROW // 2, 0)), jnp.arange(ROW), side="right"))(jax.random.split(seeds[3], MICRO * ROWS)).reshape((MICRO, ROWS, ROW)).astype(jnp.int32)
    row_lengths = set_ends(jax.random.randint(seeds[4], (MICRO, ROWS), ROW // 2, ROW + 1), jax.random.fold_in(seeds[4], 1), ROW // 2, ROW).astype(jnp.int32)
    w_skip = centred(seeds[5], (2 * D, D), (2 * D) ** -0.5, 0.125, ((0, 32),))
    b_skip = centred(seeds[6], (D,), 0.2, 1.1953125, ((0, 32),))
    gain_one = jnp.clip(1.0 + 0.15 * jax.random.normal(seeds[7], (D,), jnp.float32), 0.25, 1.75).astype(jnp.bfloat16)
    w_qkv = centred(seeds[8], (D, 3 * D), D ** -0.5, 0.1875, ((0, 32),))
    w_out = centred(seeds[9], (D, D), (D // 8) ** -0.5, 0.5, ((0, 32),))
    gain_two = jnp.clip(1.0 + 0.15 * jax.random.normal(seeds[10], (D,), jnp.float32), 0.25, 1.75).astype(jnp.bfloat16)
    w_up = centred(seeds[11], (D, FF), D ** -0.5, 0.1875, ((0, 32),))
    b_up = centred(seeds[12], (FF,), 0.2, 1.1953125, ((0, 32),))
    w_down = centred(seeds[13], (FF, D), FF ** -0.5, 0.09375, ((0, 32),))
    b_down = centred(seeds[14], (D,), 0.2, 1.1953125, ((0, 32),))
    return {"frames": frames, "skip": skip, "cotangent": cotangent, "segment_ids": segment_ids, "row_lengths": row_lengths, "w_skip": w_skip, "b_skip": b_skip, "gain_one": gain_one, "w_qkv": w_qkv, "w_out": w_out, "gain_two": gain_two, "w_up": w_up, "b_up": b_up, "w_down": w_down, "b_down": b_down}


@jax.custom_vjp
def low(v):
    return lax.optimization_barrier(v.astype(jnp.bfloat16)).astype(jnp.float32)

@jax.custom_vjp
def low_back(v):
    return v

def low_keep(v):
    return (low(v), None)

def low_pass(kept, grad):
    return (grad,)

def back_keep(v):
    return (v, None)

def back_low(kept, grad):
    return (low(grad),)
low.defvjp(low_keep, low_pass)
low_back.defvjp(back_keep, back_low)
EPSILON = 1e-06

def gelu_tanh(values):
    return 0.5 * values * (1.0 + jnp.tanh(0.7978845608028654 * (values + 0.044715 * values * values * values)))

def rotary_tables(length, head):
    half = head // 2
    indices = jnp.arange(half, dtype=jnp.float32)
    freqs = jnp.exp(indices * (-2.0 * math.log(10000.0) / head))
    angles = jnp.arange(length, dtype=jnp.float32)[:, None] * freqs[None, :]
    return (jnp.cos(angles), jnp.sin(angles))

def rotate(values, cosine, sine):
    half = values.shape[-1] // 2
    first = values[..., :half]
    second = values[..., half:]
    cosine = cosine[:, None, :]
    sine = sine[:, None, :]
    return jnp.concatenate([first * cosine - second * sine, second * cosine + first * sine], axis=-1)

def product(form, left, right):
    return jnp.einsum(form, left, right, precision=lax.Precision.HIGHEST)

def forward_layer(frame_rows, skip_rows, params, segments, lengths):
    w_skip, b_skip, gain_one, w_qkv, w_out, gain_two, w_up, b_up, w_down, b_down = params
    group = frame_rows.shape[0]
    length = frame_rows.shape[1]
    joined = jnp.concatenate([frame_rows, skip_rows], axis=2)
    hidden = low_back(product('gri,io->gro', joined, w_skip)) + b_skip
    scale_one = lax.rsqrt(lax.optimization_barrier(jnp.mean(hidden * hidden, axis=2, keepdims=True)) + EPSILON)
    normed_one = low(hidden * scale_one * gain_one)
    mixed = low_back(product('gri,io->gro', normed_one, w_qkv))
    layout = (group, length, HEADS, HEAD)
    cosine, sine = rotary_tables(length, HEAD)
    query = low(jax.vmap(lambda rows: rotate(rows, cosine, sine))(mixed[:, :, :D].reshape(layout)))
    keys = low(jax.vmap(lambda rows: rotate(rows, cosine, sine))(mixed[:, :, D:2 * D].reshape(layout)))
    values = low(mixed[:, :, 2 * D:].reshape(layout))
    scores = low_back(product('gqhe,gkhe->ghqk', query, keys) * HEAD ** (-0.5))
    positions = jnp.arange(length)
    same = segments[:, :, None] == segments[:, None, :]
    valid = positions[None, None, :] < lengths[:, None, None]
    diagonal = (positions[:, None] == positions[None, :])[None]
    allowed = same & valid | diagonal
    masked = jnp.where(allowed[:, None], scores, -1e+30)
    highest = lax.optimization_barrier(jnp.max(masked, axis=3, keepdims=True))
    exponent = jnp.exp(masked - highest)
    probs = low(exponent / lax.optimization_barrier(jnp.sum(exponent, axis=3, keepdims=True)))
    attended = low(low_back(product('ghqk,gkhe->gqhe', probs, values))).reshape(group, length, D)
    middle = hidden + low_back(product('gri,io->gro', attended, w_out))
    scale_two = lax.rsqrt(lax.optimization_barrier(jnp.mean(middle * middle, axis=2, keepdims=True)) + EPSILON)
    normed_two = low(middle * scale_two * gain_two)
    inner = low_back(product('gri,io->gro', normed_two, w_up)) + b_up
    activated = low(gelu_tanh(inner))
    return middle + (low_back(product('gri,io->gro', activated, w_down)) + b_down)

def reference(frames, skip, cotangent, segment_ids, row_lengths, w_skip, b_skip, gain_one, w_qkv, w_out, gain_two, w_up, b_up, w_down, b_down):
    params = tuple((weight.astype(jnp.float32) for weight in (w_skip, b_skip, gain_one, w_qkv, w_out, gain_two, w_up, b_up, w_down, b_down)))
    group = math.gcd(ROWS, max(1, 4096 // ROW))
    blocks = MICRO * ROWS // group

    def blocked(array):
        return array.reshape((blocks, group) + array.shape[2:])
    pieces = (blocked(frames.astype(jnp.float32)), blocked(skip.astype(jnp.float32)), blocked(cotangent.astype(jnp.float32)), blocked(segment_ids), blocked(row_lengths))

    def advance(totals, piece):
        frame_rows, skip_rows, cot_rows, segments, lengths = piece

        def apply_layer(first, second, weights):
            return forward_layer(first, second, weights, segments, lengths)
        result, backward = jax.vjp(apply_layer, frame_rows, skip_rows, params)
        frame_grad, skip_grad, param_grads = backward(cot_rows)
        totals = tuple((total + addend for total, addend in zip(totals, param_grads)))
        return (totals, (result.astype(jnp.bfloat16), frame_grad, skip_grad))
    starting = tuple((jnp.zeros(weight.shape, jnp.float32) for weight in params))
    totals, (results, frame_grads, skip_grads) = lax.scan(advance, starting, pieces)
    layout = (MICRO, ROWS, ROW, D)
    return (results.reshape(layout), frame_grads.reshape(layout), skip_grads.reshape(layout), totals[0], totals[1], totals[2], totals[3], totals[4], totals[5], totals[6], totals[7], totals[8], totals[9])
```

```python
import functools
import math

import jax
import jax.numpy as jnp
from jax import lax
from jax.experimental import pallas as pl
from jax.experimental.pallas import tpu as pltpu
from jax.sharding import PartitionSpec as P

HEADS = 16
HEAD = 64
EPSILON = 1e-06
AXES = ("dp", "fsdp")
F32 = jnp.float32
BF16 = jnp.bfloat16


def dot(left, right, kind=F32):
    return jnp.dot(left, right, preferred_element_type=F32).astype(kind)


def against(left, right):
    return lax.dot_general(left, right, (((1,), (1,)), ((), ())), preferred_element_type=F32)


def contract(left, right):
    return lax.dot_general(left, right, (((0,), (0,)), ((), ())), preferred_element_type=F32)


def wide_tables(length):
    half = HEAD // 2
    indices = jnp.arange(half, dtype=F32)
    freqs = jnp.exp(indices * (-2.0 * math.log(10000.0) / HEAD))
    angles = jnp.arange(length, dtype=F32)[:, None] * freqs[None, :]
    cosine, sine = jnp.cos(angles), jnp.sin(angles)
    return (
        jnp.concatenate([cosine] * 4, axis=1),
        jnp.concatenate([-sine, sine, -sine, sine], axis=1),
    )


def swap_halves(values):
    half = HEAD // 2
    lane = lax.broadcasted_iota(jnp.int32, values.shape, 1)
    ahead = pltpu.roll(values, 2 * HEAD - half, 1)
    behind = pltpu.roll(values, half, 1)
    return jnp.where(lax.rem(lane, HEAD) < half, ahead, behind)


def allowed_of(column_ref, row_ref):
    length = row_ref.shape[-1]
    rows = lax.broadcasted_iota(jnp.int32, (length, length), 0)
    columns = lax.broadcasted_iota(jnp.int32, (length, length), 1)
    return (column_ref[0] == row_ref[0]) | (rows == columns)


def head_part(values, which):
    lane = lax.broadcasted_iota(jnp.int32, values.shape, 1)
    return jnp.where((lane >= HEAD) == (which == 1), values, jnp.zeros_like(values))


def attend_kernel(q_ref, k_ref, v_ref, cos_ref, sin_ref, column_ref, row_ref, qo_ref, ko_ref, vo_ref, a_ref, lse_ref):
    pair = pl.program_id(1)
    cosine, sine = cos_ref[...], sin_ref[...]
    raw_q, raw_k = q_ref[...], k_ref[...]
    query = (raw_q * cosine + swap_halves(raw_q) * sine).astype(BF16)
    key = (raw_k * cosine + swap_halves(raw_k) * sine).astype(BF16)
    value = v_ref[...].astype(BF16)
    qo_ref[...] = query
    ko_ref[...] = key
    vo_ref[...] = value
    allowed = allowed_of(column_ref, row_ref)
    total = jnp.zeros(value.shape, F32)
    lane = lax.broadcasted_iota(jnp.int32, lse_ref.shape, 1)

    @pl.when(pair == 0)
    def _():
        lse_ref[...] = jnp.zeros_like(lse_ref)

    marks = lse_ref[...]
    for which in range(2):
        scores = against(head_part(query, which), key) * HEAD ** (-0.5)
        masked = jnp.where(allowed, scores, -1e30)
        highest = jnp.max(masked, axis=1, keepdims=True)
        exponent = jnp.exp(masked - highest)
        summed = jnp.sum(exponent, axis=1, keepdims=True)
        probs = (exponent / summed).astype(BF16)
        total += dot(probs, head_part(value, which))
        marks = jnp.where(lane == 2 * pair + which, highest + jnp.log(summed), marks)
    lse_ref[...] = marks
    a_ref[...] = total.astype(BF16)


def attend(mixed, tables, column, row, rows, length):
    width = HEADS * HEAD
    pairs = HEADS // 2
    wide = 2 * HEAD
    place = lambda shift: pl.BlockSpec((length, wide), lambda r, p, s=shift: (r, p + s))
    table = pl.BlockSpec((length, wide), lambda r, p: (0, 0))
    narrow = jax.ShapeDtypeStruct((rows * length, width), BF16)
    return pl.pallas_call(
        attend_kernel,
        grid=(rows, pairs),
        in_specs=[
            place(0),
            place(pairs),
            place(2 * pairs),
            table,
            table,
            pl.BlockSpec((1, length, 1), lambda r, p: (r, 0, 0)),
            pl.BlockSpec((1, 1, length), lambda r, p: (r, 0, 0)),
        ],
        out_specs=[place(0)] * 4 + [pl.BlockSpec((length, wide), lambda r, p: (r, 0))],
        out_shape=[narrow] * 4 + [jax.ShapeDtypeStruct((rows * length, wide), F32)],
        cost_estimate=pl.CostEstimate(flops=rows * HEADS * length * length * 512, bytes_accessed=rows * length * width * 24, transcendentals=rows * HEADS * length * length),
    )(mixed, mixed, mixed, *tables, column, row)


def attend_back_kernel(q_ref, k_ref, v_ref, g_ref, lse_ref, cos_ref, sin_ref, column_ref, row_ref, gq_ref, gk_ref, gv_ref):
    pair = pl.program_id(1)
    cosine, sine = cos_ref[...], sin_ref[...]
    query, key, value, grad = q_ref[...], k_ref[...], v_ref[...], g_ref[...]
    allowed = allowed_of(column_ref, row_ref)
    lse = lse_ref[...]
    lane = lax.broadcasted_iota(jnp.int32, lse.shape, 1)
    scale = HEAD ** (-0.5)
    grad_q = jnp.zeros(query.shape, F32)
    grad_k = jnp.zeros(query.shape, F32)
    grad_v = jnp.zeros(query.shape, F32)
    for which in range(2):
        own_query = head_part(query, which)
        own_grad = head_part(grad, which)
        mark = jnp.sum(jnp.where(lane == 2 * pair + which, lse, 0.0), axis=1, keepdims=True)
        scores = against(own_query, key) * scale
        probs = jnp.exp(jnp.where(allowed, scores, -1e30) - mark)
        grad_probs = against(own_grad, value)
        inside = jnp.sum(grad_probs * probs, axis=1, keepdims=True)
        grad_scores = (probs * (grad_probs - inside)).astype(BF16)
        grad_v += contract(probs.astype(BF16), own_grad)
        grad_q += dot(grad_scores, head_part(key, which))
        grad_k += contract(grad_scores, own_query)
    grad_q = grad_q * scale
    grad_k = grad_k * scale
    gq_ref[...] = (grad_q * cosine - swap_halves(grad_q) * sine).astype(BF16)
    gk_ref[...] = (grad_k * cosine - swap_halves(grad_k) * sine).astype(BF16)
    gv_ref[...] = grad_v.astype(BF16)


def attend_back(query, key, value, grad, lse, tables, column, row, rows, length):
    width = HEADS * HEAD
    pairs = HEADS // 2
    wide = 2 * HEAD
    place = pl.BlockSpec((length, wide), lambda r, p: (r, p))
    table = pl.BlockSpec((length, wide), lambda r, p: (0, 0))
    narrow = jax.ShapeDtypeStruct((rows * length, width), BF16)
    return pl.pallas_call(
        attend_back_kernel,
        grid=(rows, pairs),
        in_specs=[place] * 4
        + [
            pl.BlockSpec((length, wide), lambda r, p: (r, 0)),
            table,
            table,
            pl.BlockSpec((1, length, 1), lambda r, p: (r, 0, 0)),
            pl.BlockSpec((1, 1, length), lambda r, p: (r, 0, 0)),
        ],
        out_specs=[place] * 3,
        out_shape=[narrow] * 3,
        cost_estimate=pl.CostEstimate(flops=rows * HEADS * length * length * 1280, bytes_accessed=rows * length * width * 14, transcendentals=rows * HEADS * length * length),
    )(query, key, value, grad, lse, *tables, column, row)


def gelu_parts(values):
    cube = values * values
    arch = jnp.tanh(0.7978845608028654 * (values + 0.044715 * values * cube))
    slope = 0.5 * (1.0 + arch) + 0.5 * values * (1.0 - arch * arch) * (0.7978845608028654 * (1.0 + 3.0 * 0.044715 * cube))
    return 0.5 * values * (1.0 + arch), slope


def norm_back(grad_normed, unit, scale, gain):
    scaled = grad_normed * gain
    return scale * (scaled - unit * jnp.mean(scaled * unit, axis=1, keepdims=True))


def pairs_of(move):
    pairs = []
    for z in range(4):
        for y in range(2):
            for x in range(2):
                for c in range(2):
                    there = move(z, y, x, c)
                    if there is not None:
                        source = ((z * 2 + y) * 2 + x) * 2 + c
                        target = ((there[0] * 2 + there[1]) * 2 + there[2]) * 2 + there[3]
                        pairs.append((source, target))
    return pairs


OTHER_CORE = pairs_of(lambda z, y, x, c: (z, y, x, 1 - c))
FIRST = pairs_of(lambda z, y, x, c: (z, 1 - y, x, c) if c == 0 else (z, y, 1 - x, c))
SECOND = pairs_of(lambda z, y, x, c: (z, y, 1 - x, c) if c == 0 else (z, 1 - y, x, c))
INWARD = pairs_of(lambda z, y, x, c: {0: (1, y, x, c), 3: (2, y, x, c)}.get(z))
MIDDLE = pairs_of(lambda z, y, x, c: {1: (2, y, x, c), 2: (1, y, x, c)}.get(z))
NEAR = pairs_of(lambda z, y, x, c: (z ^ 1, y, x, c))
Z_ORDER = ((3, 2, 1, 0), (3, 2, 0, 1), (0, 1, 3, 2), (0, 1, 2, 3))


def send(values, pairs):
    return lax.ppermute(values, AXES, pairs)


def block_order(place, late_plane, core):
    z, y, x = place
    levels = jnp.asarray(Z_ORDER, jnp.int32)[z]
    own_first = jnp.where(core == 0, y, x)
    own_second = jnp.where(core == 0, x, y)
    index = jnp.arange(16)
    if late_plane:
        first, slot, second = index // 8, index // 2 % 4, index % 2
    else:
        first, second, slot = index // 8, index // 4 % 2, index % 4
    level = jnp.sum(jnp.where(slot[:, None] == jnp.arange(4)[None, :], levels[None, :], 0), axis=1)
    first = jnp.where(first == 1, own_first, 1 - own_first)
    second = jnp.where(second == 1, own_second, 1 - own_second)
    at_y = jnp.where(core == 0, first, second)
    at_x = jnp.where(core == 0, second, first)
    return ((level * 2 + at_y) * 2 + at_x) * 2 + core


def both_orders(place, core, late_plane):
    return jnp.concatenate([block_order(place, late_plane, 1 - core), block_order(place, late_plane, core)])


def plus(left, right, kind=BF16):
    return (left.astype(F32) + right.astype(F32)).astype(kind)


def reduce(values, late_plane):
    half = values.shape[0] // 2
    kept = plus(values[half:], send(values[:half], FIRST))
    if not late_plane:
        half //= 2
        kept = plus(kept[half:], send(kept[:half], SECOND))
    half //= 2
    far = plus(kept[:half], send(kept[:half], INWARD))
    near = plus(kept[half:], send(far, MIDDLE))
    half //= 2
    if not late_plane:
        return plus(near[half:], send(near[:half], NEAR), F32)
    kept = plus(near[half:], send(near[:half], NEAR))
    half //= 2
    return plus(kept[half:], send(kept[:half], SECOND), F32)


def picked(values, order):
    columns = values.shape[1]
    block = columns // 32
    column = jnp.arange(columns)
    source = jnp.repeat(order, block) * block + column % block
    choice = (column[:, None] == source[None, :]).astype(BF16)
    return dot(values, choice, BF16)


def copy_kernel(order_ref, in_ref, out_ref):
    out_ref[...] = in_ref[...]


def picked_wide(values, order):
    rows, columns = values.shape
    block = columns // 32
    return pl.pallas_call(
        copy_kernel,
        grid_spec=pltpu.PrefetchScalarGridSpec(
            num_scalar_prefetch=1,
            grid=(32,),
            in_specs=[pl.BlockSpec((rows, block), lambda i, order: (0, order[i]))],
            out_specs=pl.BlockSpec((rows, block), lambda i, order: (0, i)),
        ),
        out_shape=jax.ShapeDtypeStruct(values.shape, values.dtype),
        cost_estimate=pl.CostEstimate(flops=0, bytes_accessed=4 * rows * columns, transcendentals=0),
    )(order, values)


def paired(values):
    half = values.shape[1] // 2
    return jnp.concatenate([values[:, half:], send(values[:, :half], OTHER_CORE)])


def with_other(values):
    return jnp.concatenate([values, send(values, OTHER_CORE)])


def on_device(
    known,
    frames,
    skip,
    cotangent,
    segment_ids,
    row_lengths,
    w_skip,
    b_skip,
    gain_one,
    w_qkv,
    w_out,
    gain_two,
    w_up,
    b_up,
    w_down,
    b_down,
):
    micro, rows, length, width = frames.shape
    count = micro * rows
    tokens = count * length
    devices = width // gain_one.shape[0]
    hidden_width = w_up.shape[1]

    vectors = jnp.concatenate([b_skip, gain_one, gain_two, b_down, b_up])
    part = w_skip.shape[0]
    lines = -(-vectors.shape[0] // width)
    lines = -(-lines // 8) * 8
    padded = jnp.pad(vectors, (0, lines * width - vectors.shape[0])).reshape(lines, width)
    all_skip = lax.all_gather(jnp.concatenate([w_skip, padded]), AXES, axis=0, tiled=False)
    all_qkv = lax.all_gather(jnp.concatenate([w_qkv, w_out], axis=1), AXES, axis=0, tiled=True)
    all_up = lax.all_gather(w_up, AXES, axis=0, tiled=True)
    all_down = lax.all_gather(w_down, AXES, axis=0, tiled=True)
    full_skip = all_skip[:, :part].reshape(devices * part, width)
    flat = all_skip[:, part:].reshape(devices, lines * width)
    small = width // devices
    spread = lambda at, size: flat[:, at : at + size].reshape(1, devices * size).astype(F32)
    bias_skip, gain_1, gain_2, bias_down = (spread(i * small, small) for i in range(4))
    bias_up = spread(4 * small, hidden_width // devices)
    full_qkv = all_qkv[:, : 3 * width]
    full_out = all_qkv[:, 3 * width :]

    frames = frames.reshape(tokens, width)
    skip = skip.reshape(tokens, width)
    grad_low = cotangent.reshape(tokens, width)
    grad_out = grad_low.astype(F32)
    segments = segment_ids.reshape(count, length)
    lengths = row_lengths.reshape(count, 1)
    reach = jnp.where(jnp.arange(length)[None, :] < lengths, segments, -1)
    column, row = segments[:, :, None], reach[:, None, :]
    tables = wide_tables(length)

    joined = jnp.concatenate([frames, skip], axis=1)
    hidden = dot(joined, full_skip) + bias_skip
    scale_one = lax.rsqrt(jnp.mean(hidden * hidden, axis=1, keepdims=True) + EPSILON)
    unit_one = hidden * scale_one
    normed_one = (unit_one * gain_1).astype(BF16)
    mixed = dot(normed_one, full_qkv)
    query, key, value, attended, lse = attend(mixed, tables, column, row, count, length)
    middle = hidden + dot(attended, full_out)
    scale_two = lax.rsqrt(jnp.mean(middle * middle, axis=1, keepdims=True) + EPSILON)
    unit_two = middle * scale_two
    normed_two = (unit_two * gain_2).astype(BF16)
    inner = dot(normed_two, all_up) + bias_up
    activated, slope = gelu_parts(inner)
    activated = activated.astype(BF16)
    output = (middle + (dot(activated, all_down) + bias_down)).astype(BF16)

    grad_inner = against(grad_low, all_down) * slope
    inner_low = grad_inner.astype(BF16)
    grad_normed_two = against(inner_low, all_up)
    grad_middle = grad_out + norm_back(grad_normed_two, unit_two, scale_two, gain_2)
    middle_low = grad_middle.astype(BF16)
    grad_attended = against(middle_low, full_out).astype(BF16)
    grad_mixed = jnp.concatenate(attend_back(query, key, value, grad_attended, lse, tables, column, row, count, length), axis=1)
    grad_normed_one = against(grad_mixed, full_qkv)
    grad_hidden = grad_middle + norm_back(grad_normed_one, unit_one, scale_one, gain_1)
    hidden_low = grad_hidden.astype(BF16)
    grad_joined = against(hidden_low, full_skip)

    total = lambda values: jnp.sum(values, axis=0)
    vector_grads = (
        total(grad_hidden),
        total(grad_normed_one * unit_one),
        total(grad_normed_two * unit_two),
        total(grad_out),
        total(grad_inner),
    )

    if known:
        place = lax.axis_index("dp")
        at_x = lax.axis_index("fsdp")
        core = at_x % 2
        coords = (place // 2, place % 2, at_x // 2)
        late = both_orders(coords, core, True)
        early = both_orders(coords, core, False)
        g_down = contract(paired(picked_wide(activated, late)), with_other(grad_low)).astype(BF16)
        down_grad = reduce(g_down, True)
        g_up = contract(paired(picked(normed_two, late)), with_other(inner_low)).astype(BF16)
        up_grad = reduce(g_up, True)
        g_out = contract(paired(picked(attended, early)), with_other(middle_low)).astype(BF16)
        g_qkv = contract(paired(picked(normed_one, early)), with_other(grad_mixed)).astype(BF16)
        both_grad = reduce(jnp.concatenate([g_qkv, g_out], axis=1), False)
        qkv_grad, out_grad = both_grad[:, : 3 * width], both_grad[:, 3 * width :]
        g_skip = contract(paired(picked(joined, early)), with_other(hidden_low)).astype(BF16)
        by_block = jnp.concatenate([v.reshape(devices, -1) for v in vector_grads], axis=1)
        by_block = by_block + send(by_block, OTHER_CORE)
        choice = (early[16:, None] == jnp.arange(devices)[None, :]).astype(F32)
        by_block = jnp.dot(choice, by_block, precision=lax.Precision.HIGHEST).astype(BF16)
        by_block = jnp.pad(by_block, ((0, 0), (0, lines * width - by_block.shape[1])))
        g_last = jnp.concatenate([g_skip.reshape(16, part, width), by_block.reshape(16, lines, width)], axis=1)
        last = reduce(g_last.reshape(16 * (part + lines), width), False)
        skip_weight_grad = last[:part]
        line = last[part:].reshape(lines * width)
        shares = [line[i * small : (i + 1) * small] for i in range(4)]
        shares.append(line[4 * small : 4 * small + hidden_width // devices])
    else:
        scatter = lambda values: lax.psum_scatter(values, AXES, scatter_dimension=0, tiled=True)
        down_grad = scatter(contract(activated, grad_low))
        up_grad = scatter(contract(normed_two, inner_low))
        out_grad = scatter(contract(attended, middle_low))
        qkv_grad = scatter(contract(normed_one, grad_mixed))
        skip_weight_grad = scatter(contract(joined, hidden_low))
        shares = [scatter(v) for v in vector_grads]

    shape = (micro, rows, length, width)
    return (
        output.reshape(shape),
        grad_joined[:, :width].reshape(shape),
        grad_joined[:, width:].reshape(shape),
        skip_weight_grad,
        shares[0],
        shares[1],
        qkv_grad,
        out_grad,
        shares[2],
        up_grad,
        shares[4],
        down_grad,
        shares[3],
    )


def solution(mesh):
    known = mesh.shape["dp"] == 8 and mesh.shape["fsdp"] == 4
    tokens = P(None, AXES, None, None)
    weight = P(AXES, None)
    vector = P(AXES)
    return jax.shard_map(
        functools.partial(on_device, known),
        mesh=mesh,
        in_specs=(
            tokens,
            tokens,
            tokens,
            P(None, AXES, None),
            P(None, AXES),
            weight,
            vector,
            vector,
            weight,
            weight,
            vector,
            weight,
            vector,
            weight,
            vector,
        ),
        out_specs=(
            tokens,
            tokens,
            tokens,
            weight,
            vector,
            vector,
            weight,
            weight,
            vector,
            weight,
            vector,
            weight,
            vector,
        ),
        check_vma=False,
    )
```

```python
import functools
import math

import jax
import jax.numpy as jnp
from jax import lax
from jax.experimental import pallas as pl
from jax.experimental.pallas import tpu as pltpu
from jax.sharding import PartitionSpec as P

HEADS = 16
HEAD = 64
EPSILON = 1e-06
AXES = ("dp", "fsdp")
F32 = jnp.float32
BF16 = jnp.bfloat16
VMEM = pltpu.CompilerParams(vmem_limit_bytes=48 << 20)


def dot(left, right, kind=F32):
    return jnp.dot(left, right, preferred_element_type=F32).astype(kind)


def against(left, right):
    return lax.dot_general(left, right, (((1,), (1,)), ((), ())), preferred_element_type=F32)


def contract(left, right):
    return lax.dot_general(left, right, (((0,), (0,)), ((), ())), preferred_element_type=F32)


def wide_tables(length):
    half = HEAD // 2
    indices = jnp.arange(half, dtype=F32)
    freqs = jnp.exp(indices * (-2.0 * math.log(10000.0) / HEAD))
    angles = jnp.arange(length, dtype=F32)[:, None] * freqs[None, :]
    cosine, sine = jnp.cos(angles), jnp.sin(angles)
    return (
        jnp.concatenate([cosine] * 4, axis=1),
        jnp.concatenate([-sine, sine, -sine, sine], axis=1),
    )


def swap_halves(values):
    half = HEAD // 2
    lane = lax.broadcasted_iota(jnp.int32, values.shape, 1)
    ahead = pltpu.roll(values, 2 * HEAD - half, 1)
    behind = pltpu.roll(values, half, 1)
    return jnp.where(lax.rem(lane, HEAD) < half, ahead, behind)


def allowed_of(column_ref, row_ref):
    length = row_ref.shape[-1]
    rows = lax.broadcasted_iota(jnp.int32, (length, length), 0)
    columns = lax.broadcasted_iota(jnp.int32, (length, length), 1)
    return (column_ref[0] == row_ref[0]) | (rows == columns)


def head_part(values, which):
    lane = lax.broadcasted_iota(jnp.int32, values.shape, 1)
    return jnp.where((lane >= HEAD) == (which == 1), values, jnp.zeros_like(values))


WIDE = 2 * HEAD
GROUP = 2


def attend_kernel(q_ref, k_ref, v_ref, cos_ref, sin_ref, column_ref, row_ref, qo_ref, ko_ref, vo_ref, a_ref, lse_ref):
    cosine, sine = cos_ref[...], sin_ref[...]
    allowed = allowed_of(column_ref, row_ref)
    for pair in range(GROUP):
        lanes = slice(pair * WIDE, (pair + 1) * WIDE)
        raw_q, raw_k = q_ref[:, lanes], k_ref[:, lanes]
        query = ((raw_q * cosine + swap_halves(raw_q) * sine)).astype(BF16)
        key = (raw_k * cosine + swap_halves(raw_k) * sine).astype(BF16)
        value = v_ref[:, lanes].astype(BF16)
        qo_ref[:, lanes] = query
        ko_ref[:, lanes] = key
        vo_ref[:, lanes] = value
        total = jnp.zeros(value.shape, F32)
        for which in range(2):
            scores = against(key, head_part(query, which)) * HEAD ** (-0.5)
            masked = jnp.where(allowed, scores, -1e30)
            highest = jnp.max(masked, axis=0, keepdims=True)
            exponent = jnp.exp(masked - highest)
            summed = jnp.sum(exponent, axis=0, keepdims=True)
            probs = (exponent / summed).astype(BF16)
            total += contract(probs, head_part(value, which))
            lse_ref[0, 0, pl.ds(2 * pair + which, 1), :] = highest + jnp.log(summed)
        a_ref[:, lanes] = total.astype(BF16)


def attend(mixed, tables, column, row, rows, length):
    width = HEADS * HEAD
    steps = HEADS // 2 // GROUP
    wide = WIDE * GROUP
    place = lambda shift: pl.BlockSpec((length, wide), lambda r, p, s=shift: (r, p + s))
    table = pl.BlockSpec((length, WIDE), lambda r, p: (0, 0))
    narrow = jax.ShapeDtypeStruct((rows * length, width), BF16)
    return pl.pallas_call(
        attend_kernel,
        grid=(rows, steps),
        in_specs=[
            place(0),
            place(steps),
            place(2 * steps),
            table,
            table,
            pl.BlockSpec((1, length, 1), lambda r, p: (r, 0, 0)),
            pl.BlockSpec((1, 1, length), lambda r, p: (r, 0, 0)),
        ],
        out_specs=[place(0)] * 4 + [pl.BlockSpec((1, 1, 2 * GROUP, length), lambda r, p: (r, p, 0, 0))],
        out_shape=[narrow] * 4 + [jax.ShapeDtypeStruct((rows, steps, 2 * GROUP, length), F32)],
        compiler_params=VMEM,
        cost_estimate=pl.CostEstimate(flops=rows * HEADS * length * length * 512, bytes_accessed=rows * length * width * 24, transcendentals=rows * HEADS * length * length),
    )(mixed, mixed, mixed, *tables, column, row)


def attend_back_kernel(q_ref, k_ref, v_ref, g_ref, lse_ref, cos_ref, sin_ref, column_ref, row_ref, gq_ref, gk_ref, gv_ref):
    cosine, sine = cos_ref[...], sin_ref[...]
    allowed = allowed_of(column_ref, row_ref)
    scale = HEAD ** (-0.5)
    for pair in range(GROUP):
        lanes = slice(pair * WIDE, (pair + 1) * WIDE)
        query, key, value, grad = q_ref[:, lanes], k_ref[:, lanes], v_ref[:, lanes], g_ref[:, lanes]
        grad_q = jnp.zeros(query.shape, F32)
        grad_k = jnp.zeros(query.shape, F32)
        grad_v = jnp.zeros(query.shape, F32)
        for which in range(2):
            own_query = head_part(query, which)
            own_grad = head_part(grad, which)
            mark = lse_ref[0, 0, pl.ds(2 * pair + which, 1), :]
            scores = against(key, own_query) * scale
            probs = jnp.exp(jnp.where(allowed, scores, -1e30) - mark)
            grad_probs = against(value, own_grad)
            inside = jnp.sum(grad_probs * probs, axis=0, keepdims=True)
            grad_scores = (probs * (grad_probs - inside)).astype(BF16)
            grad_v += dot(probs.astype(BF16), own_grad)
            grad_k += dot(grad_scores, own_query)
            grad_q += contract(grad_scores, head_part(key, which))
        grad_q = grad_q * scale
        grad_k = grad_k * scale
        gq_ref[:, lanes] = (grad_q * cosine - swap_halves(grad_q) * sine).astype(BF16)
        gk_ref[:, lanes] = (grad_k * cosine - swap_halves(grad_k) * sine).astype(BF16)
        gv_ref[:, lanes] = grad_v.astype(BF16)


def attend_back(query, key, value, grad, lse, tables, column, row, rows, length):
    width = HEADS * HEAD
    steps = HEADS // 2 // GROUP
    place = pl.BlockSpec((length, WIDE * GROUP), lambda r, p: (r, p))
    table = pl.BlockSpec((length, WIDE), lambda r, p: (0, 0))
    narrow = jax.ShapeDtypeStruct((rows * length, width), BF16)
    return pl.pallas_call(
        attend_back_kernel,
        grid=(rows, steps),
        in_specs=[place] * 4
        + [
            pl.BlockSpec((1, 1, 2 * GROUP, length), lambda r, p: (r, p, 0, 0)),
            table,
            table,
            pl.BlockSpec((1, length, 1), lambda r, p: (r, 0, 0)),
            pl.BlockSpec((1, 1, length), lambda r, p: (r, 0, 0)),
        ],
        out_specs=[place] * 3,
        out_shape=[narrow] * 3,
        compiler_params=VMEM,
        cost_estimate=pl.CostEstimate(flops=rows * HEADS * length * length * 1280, bytes_accessed=rows * length * width * 14, transcendentals=rows * HEADS * length * length),
    )(query, key, value, grad, lse, *tables, column, row)


def gelu_parts(values):
    cube = values * values
    arch = jnp.tanh(0.7978845608028654 * (values + 0.044715 * values * cube))
    slope = 0.5 * (1.0 + arch) + 0.5 * values * (1.0 - arch * arch) * (0.7978845608028654 * (1.0 + 3.0 * 0.044715 * cube))
    return 0.5 * values * (1.0 + arch), slope


TILE = 512
BLOCK = 128


def up_kernel(mine_ref, other_ref, core_ref, x_ref, w_ref, b_ref, act_ref, slope_ref, own_ref, give_ref):
    activated, slope = gelu_parts(dot(x_ref[...], w_ref[...]) + b_ref[...])
    activated = activated.astype(BF16)
    act_ref[...] = activated
    slope_ref[...] = slope.astype(BF16)
    second = core_ref[0] == 1
    pairs = TILE // 2 // BLOCK
    for pair in range(pairs):
        low = activated[:, 2 * pair * BLOCK : (2 * pair + 1) * BLOCK]
        high = activated[:, (2 * pair + 1) * BLOCK : (2 * pair + 2) * BLOCK]
        index = pl.program_id(0) * pairs + pair
        own_ref[:, pl.ds(pl.multiple_of(mine_ref[index] * BLOCK, BLOCK), BLOCK)] = jnp.where(second, high, low)
        give_ref[:, pl.ds(pl.multiple_of(other_ref[index] * BLOCK, BLOCK), BLOCK)] = jnp.where(second, low, high)


def up_product(normed, weight, bias, mine, other, core):
    tokens, width = normed.shape
    columns = weight.shape[1]
    tall = pl.BlockSpec((tokens, TILE), lambda i, *_: (0, i))
    whole = pl.BlockSpec((tokens, columns // 2), lambda i, *_: (0, 0))
    return pl.pallas_call(
        up_kernel,
        grid_spec=pltpu.PrefetchScalarGridSpec(
            num_scalar_prefetch=3,
            grid=(columns // TILE,),
            in_specs=[
                pl.BlockSpec((tokens, width), lambda i, *_: (0, 0)),
                pl.BlockSpec((width, TILE), lambda i, *_: (0, i)),
                pl.BlockSpec((1, TILE), lambda i, *_: (0, i)),
            ],
            out_specs=[tall, tall, whole, whole],
        ),
        out_shape=[jax.ShapeDtypeStruct((tokens, n), BF16) for n in (columns, columns, columns // 2, columns // 2)],
        compiler_params=VMEM,
        cost_estimate=pl.CostEstimate(flops=2 * tokens * width * columns, bytes_accessed=2 * (width * columns + 3 * tokens * columns), transcendentals=tokens * columns),
    )(mine, other, core, normed, weight, bias)


def inner_kernel(g_ref, w_ref, slope_ref, low_ref, sum_ref):
    grad_inner = against(g_ref[...], w_ref[...]) * slope_ref[...].astype(F32)
    low_ref[...] = grad_inner.astype(BF16)
    sum_ref[...] = jnp.sum(grad_inner, axis=0, keepdims=True)


def inner_back(grad_low, weight, slope):
    tokens, width = grad_low.shape
    columns = weight.shape[0]
    tall = pl.BlockSpec((tokens, TILE), lambda i: (0, i))
    return pl.pallas_call(
        inner_kernel,
        grid=(columns // TILE,),
        in_specs=[
            pl.BlockSpec((tokens, width), lambda i: (0, 0)),
            pl.BlockSpec((TILE, width), lambda i: (i, 0)),
            tall,
        ],
        out_specs=[tall, pl.BlockSpec((1, TILE), lambda i: (0, i))],
        out_shape=[jax.ShapeDtypeStruct((tokens, columns), BF16), jax.ShapeDtypeStruct((1, columns), F32)],
        compiler_params=VMEM,
        cost_estimate=pl.CostEstimate(flops=2 * tokens * width * columns, bytes_accessed=2 * (width * columns + 2 * tokens * columns), transcendentals=0),
    )(grad_low, weight, slope)


def pair_kernel(x_ref, xs_ref, g_ref, gs_ref, out_ref):
    out_ref[...] = (contract(x_ref[...], g_ref[...]) + contract(xs_ref[...], gs_ref[...])).astype(BF16)


def pair_product(x, x_other, g, g_other):
    tokens, rows = x.shape
    columns = g.shape[1]
    if rows > columns:
        steps = rows // TILE
        x_spec = pl.BlockSpec((tokens, TILE), lambda i: (0, i))
        g_spec = pl.BlockSpec((tokens, columns), lambda i: (0, 0))
        out_spec = pl.BlockSpec((TILE, columns), lambda i: (i, 0))
    else:
        tile = min(2 * TILE, columns // 2)
        steps = columns // tile
        x_spec = pl.BlockSpec((tokens, rows), lambda i: (0, 0))
        g_spec = pl.BlockSpec((tokens, tile), lambda i: (0, i))
        out_spec = pl.BlockSpec((rows, tile), lambda i: (0, i))
    return pl.pallas_call(
        pair_kernel,
        grid=(steps,),
        in_specs=[x_spec, x_spec, g_spec, g_spec],
        out_specs=out_spec,
        out_shape=jax.ShapeDtypeStruct((rows, columns), BF16),
        compiler_params=VMEM,
        cost_estimate=pl.CostEstimate(flops=4 * tokens * rows * columns, bytes_accessed=4 * tokens * (rows + columns) + 2 * rows * columns, transcendentals=0),
    )(x, x_other, g, g_other)


def norm_back(grad_normed, unit, scale, gain):
    scaled = grad_normed * gain
    return scale * (scaled - unit * jnp.mean(scaled * unit, axis=1, keepdims=True))


def pairs_of(move):
    pairs = []
    for z in range(4):
        for y in range(2):
            for x in range(2):
                for c in range(2):
                    there = move(z, y, x, c)
                    if there is not None:
                        source = ((z * 2 + y) * 2 + x) * 2 + c
                        target = ((there[0] * 2 + there[1]) * 2 + there[2]) * 2 + there[3]
                        pairs.append((source, target))
    return pairs


OTHER_CORE = pairs_of(lambda z, y, x, c: (z, y, x, 1 - c))
FIRST = pairs_of(lambda z, y, x, c: (z, 1 - y, x, c) if c == 0 else (z, y, 1 - x, c))
SECOND = pairs_of(lambda z, y, x, c: (z, y, 1 - x, c) if c == 0 else (z, 1 - y, x, c))
INWARD = pairs_of(lambda z, y, x, c: {0: (1, y, x, c), 3: (2, y, x, c)}.get(z))
MIDDLE = pairs_of(lambda z, y, x, c: {1: (2, y, x, c), 2: (1, y, x, c)}.get(z))
NEAR = pairs_of(lambda z, y, x, c: (z ^ 1, y, x, c))
Z_ORDER = ((3, 2, 1, 0), (3, 2, 0, 1), (0, 1, 3, 2), (0, 1, 2, 3))


def send(values, pairs):
    return lax.ppermute(values, AXES, pairs)


def block_order(place, late_plane, core):
    z, y, x = place
    levels = jnp.asarray(Z_ORDER, jnp.int32)[z]
    own_first = jnp.where(core == 0, y, x)
    own_second = jnp.where(core == 0, x, y)
    index = jnp.arange(16)
    if late_plane:
        first, slot, second = index // 8, index // 2 % 4, index % 2
    else:
        first, second, slot = index // 8, index // 4 % 2, index % 4
    level = jnp.sum(jnp.where(slot[:, None] == jnp.arange(4)[None, :], levels[None, :], 0), axis=1)
    first = jnp.where(first == 1, own_first, 1 - own_first)
    second = jnp.where(second == 1, own_second, 1 - own_second)
    at_y = jnp.where(core == 0, first, second)
    at_x = jnp.where(core == 0, second, first)
    return ((level * 2 + at_y) * 2 + at_x) * 2 + core


def both_orders(place, core, late_plane):
    return jnp.concatenate([block_order(place, late_plane, 1 - core), block_order(place, late_plane, core)])


def plus(left, right, kind=BF16):
    return (left.astype(F32) + right.astype(F32)).astype(kind)


OUTWARD = pairs_of(lambda z, y, x, c: {1: (0, y, x, c), 2: (3, y, x, c)}.get(z))


def collect(block, late_plane, inner):
    kept = block
    if late_plane:
        kept = jnp.concatenate([send(kept, SECOND), kept])
    near = jnp.concatenate([send(kept, NEAR), kept])
    far = send(near, MIDDLE)
    far = jnp.where(inner, far, send(far, OUTWARD))
    kept = jnp.concatenate([far, near])
    if not late_plane:
        kept = jnp.concatenate([send(kept, SECOND), kept])
    first = send(kept, FIRST)
    return first, kept, send(first, OTHER_CORE), send(kept, OTHER_CORE)


def place_kernel(order_ref, *refs):
    parts, out_ref, sems = refs[:4], refs[4], refs[5]
    block = out_ref.shape[0] // 32
    copies = []
    for index in range(32):
        part = parts[(2 + index // 8) % 4]
        target = out_ref.at[pl.ds(pl.multiple_of(order_ref[index] * block, block), block)]
        copies.append(pltpu.make_async_copy(part.at[pl.ds(index % 8 * block, block)], target, sems.at[index]))
        copies[-1].start()
    for copy in copies:
        copy.wait()


def placed(parts, order):
    rows, columns = parts[0].shape
    return pl.pallas_call(
        place_kernel,
        grid_spec=pltpu.PrefetchScalarGridSpec(
            num_scalar_prefetch=1,
            grid=(1,),
            in_specs=[pl.BlockSpec((rows, columns), lambda i, order: (0, 0))] * 4,
            out_specs=pl.BlockSpec(memory_space=pl.ANY),
            scratch_shapes=[pltpu.SemaphoreType.DMA((32,))],
        ),
        out_shape=jax.ShapeDtypeStruct((4 * rows, columns), parts[0].dtype),
        compiler_params=VMEM,
        cost_estimate=pl.CostEstimate(flops=0, bytes_accessed=16 * rows * columns, transcendentals=0),
    )(order, *parts)


def after(value, *others):
    return lax.optimization_barrier((value,) + others)[0]


class Summing:
    def __init__(self, values, late_plane):
        self.kept = values
        self.far = None
        self.steps = [FIRST, INWARD, MIDDLE, NEAR, SECOND] if late_plane else [FIRST, SECOND, INWARD, MIDDLE, NEAR]

    def step(self):
        pairs = self.steps.pop(0)
        kept, half = self.kept, self.kept.shape[0] // 2
        if pairs is INWARD:
            self.far = plus(kept[:half], send(kept[:half], pairs))
            self.kept = kept[half:]
        elif pairs is MIDDLE:
            self.kept = plus(kept, send(self.far, pairs))
            self.far = None
        else:
            self.kept = plus(kept[half:], send(kept[:half], pairs), BF16 if self.steps else F32)
        return self.kept if self.far is None else self.far

    def finish(self):
        while self.steps:
            self.step()
        return self.kept


def picked(values, order):
    columns = values.shape[1]
    block = columns // 32
    column = jnp.arange(columns)
    source = jnp.repeat(order, block) * block + column % block
    choice = (column[:, None] == source[None, :]).astype(BF16)
    return dot(values, choice, BF16)


def swapped(values):
    return send(values, OTHER_CORE)


def halves(values):
    half = values.shape[1] // 2
    return values[:, :half], values[:, half:]


def on_device(
    known,
    frames,
    skip,
    cotangent,
    segment_ids,
    row_lengths,
    w_skip,
    b_skip,
    gain_one,
    w_qkv,
    w_out,
    gain_two,
    w_up,
    b_up,
    w_down,
    b_down,
):
    micro, rows, length, width = frames.shape
    count = micro * rows
    tokens = count * length
    devices = width // gain_one.shape[0]
    hidden_width = w_up.shape[1]

    vectors = jnp.concatenate([b_skip, gain_one, gain_two, b_down, b_up])
    part = w_skip.shape[0]
    lines = -(-vectors.shape[0] // width)
    lines = -(-lines // 8) * 8
    padded = jnp.pad(vectors, (0, lines * width - vectors.shape[0])).reshape(lines, width)
    own_skip = jnp.concatenate([w_skip, padded])
    own_qkv = jnp.concatenate([w_qkv, w_out], axis=1)
    if known:
        place = lax.axis_index("dp")
        at_x = lax.axis_index("fsdp")
        core = at_x % 2
        coords = (place // 2, place % 2, at_x // 2)
        late = both_orders(coords, core, True)
        early = both_orders(coords, core, False)
        inner_chip = (coords[0] == 1) | (coords[0] == 2)
        all_up = lax.all_gather(w_up, AXES, axis=0, tiled=True)
        all_down = lax.all_gather(w_down, AXES, axis=0, tiled=True)
        all_skip = placed(collect(own_skip, True, inner_chip), late).reshape(devices, part + lines, width)
        all_qkv = placed(collect(own_qkv, False, inner_chip), early)
    else:
        all_skip = lax.all_gather(own_skip, AXES, axis=0, tiled=False)
        all_qkv = lax.all_gather(own_qkv, AXES, axis=0, tiled=True)
        all_up = lax.all_gather(w_up, AXES, axis=0, tiled=True)
        all_down = lax.all_gather(w_down, AXES, axis=0, tiled=True)
    full_skip = all_skip[:, :part].reshape(devices * part, width)
    flat = all_skip[:, part:].reshape(devices, lines * width)
    small = width // devices
    spread = lambda at, size: flat[:, at : at + size].reshape(1, devices * size).astype(F32)
    bias_skip, gain_1, gain_2, bias_down = (spread(i * small, small) for i in range(4))
    bias_up = spread(4 * small, hidden_width // devices)
    full_qkv = all_qkv[:, : 3 * width]
    full_out = all_qkv[:, 3 * width :]

    frames = frames.reshape(tokens, width)
    skip = skip.reshape(tokens, width)
    grad_low = cotangent.reshape(tokens, width)
    grad_out = grad_low.astype(F32)
    segments = segment_ids.reshape(count, length)
    lengths = row_lengths.reshape(count, 1)
    reach = jnp.where(jnp.arange(length)[None, :] < lengths, segments, -1)
    column, row = reach[:, :, None], segments[:, None, :]
    tables = wide_tables(length)

    joined = jnp.concatenate([frames, skip], axis=1)
    hidden = dot(joined, full_skip) + bias_skip
    scale_one = lax.rsqrt(jnp.mean(hidden * hidden, axis=1, keepdims=True) + EPSILON)
    unit_one = hidden * scale_one
    normed_one = (unit_one * gain_1).astype(BF16)
    mixed = dot(normed_one, full_qkv)
    query, key, value, attended, lse = attend(mixed, tables, column, row, count, length)
    middle = hidden + dot(attended, full_out)
    scale_two = lax.rsqrt(jnp.mean(middle * middle, axis=1, keepdims=True) + EPSILON)
    unit_two = middle * scale_two
    normed_two = (unit_two * gain_2).astype(BF16)
    total = lambda values: jnp.sum(values, axis=0)
    back = functools.partial(attend_back, query, key, value, lse=lse, tables=tables, column=column, row=row, rows=count, length=length)

    if known:
        ends = lambda order: jnp.sum(jnp.where(order[None, :] // 2 == jnp.arange(16)[:, None], jnp.arange(16)[None, :], 0), axis=1).astype(jnp.int32)
        give_joined, own_joined = halves(picked(joined, early))
        joined_other = swapped(give_joined)
        grad_other = swapped(grad_low)
        give_one, own_one = halves(picked(normed_one, early))
        give_attended, own_attended = halves(picked(attended, early))
        give_two, own_two = halves(picked(normed_two, late))
        one_other, attended_other, two_other = swapped(give_one), swapped(give_attended), swapped(give_two)

        activated, slope, own_active, give_active = up_product(
            normed_two, all_up, bias_up, ends(late[16:]), ends(late[:16]), core.reshape(1)
        )
        active_other = swapped(give_active)
        inner_low, inner_sum = inner_back(grad_low, all_down, slope)
        inner_other = swapped(inner_low)
        g_down = pair_product(own_active, active_other, grad_low, grad_other)
        down = Summing(g_down, True)
        inner_low = after(inner_low, g_down)
        grad_normed_two = against(inner_low, all_up)
        g_up = pair_product(own_two, two_other, after(inner_low, grad_normed_two), inner_other)
        up = Summing(g_up, True)
        grad_middle = grad_out + norm_back(after(grad_normed_two, g_up), unit_two, scale_two, gain_2)
        middle_low = grad_middle.astype(BF16)
        middle_other = swapped(middle_low)
        grad_attended = against(middle_low, full_out).astype(BF16)
        grad_mixed = jnp.concatenate(back(grad=after(grad_attended, down.step())), axis=1)
        mixed_other = swapped(grad_mixed)
        g_out = pair_product(own_attended, attended_other, after(middle_low, up.step(), down.step()), middle_other)
        grad_normed_one = against(grad_mixed, full_qkv)
        g_qkv = pair_product(own_one, one_other, after(grad_mixed, g_out), mixed_other)
        both = Summing(jnp.concatenate([g_qkv, g_out], axis=1), False)
        grad_normed_one = after(grad_normed_one, up.step(), down.step())
        grad_hidden = grad_middle + norm_back(grad_normed_one, unit_one, scale_one, gain_1)
        hidden_low = grad_hidden.astype(BF16)
        g_skip = pair_product(own_joined, joined_other, hidden_low, swapped(hidden_low))
        vector_grads = (total(grad_hidden), total(grad_normed_one * unit_one), total(grad_normed_two * unit_two), total(grad_out), inner_sum[0])
        by_block = jnp.concatenate([v.reshape(devices, -1) for v in vector_grads], axis=1)
        by_block = by_block + swapped(by_block)
        choice = (early[16:, None] == jnp.arange(devices)[None, :]).astype(F32)
        by_block = jnp.dot(choice, by_block, precision=lax.Precision.HIGHEST).astype(BF16)
        by_block = jnp.pad(by_block, ((0, 0), (0, lines * width - by_block.shape[1])))
        g_last = jnp.concatenate([g_skip.reshape(16, part, width), by_block.reshape(16, lines, width)], axis=1)
        tail = Summing(g_last.reshape(16 * (part + lines), width), False)
        grad_joined = against(after(hidden_low, g_last, both.step(), up.step(), down.step()), full_skip)
        output = (middle + (dot(after(activated, grad_joined, tail.step(), both.step()), all_down) + bias_down)).astype(BF16)
        down_grad = down.finish()
        up_grad = up.finish()
        both_grad = both.finish()
        last = tail.finish()
        qkv_grad, out_grad = both_grad[:, : 3 * width], both_grad[:, 3 * width :]
        skip_weight_grad = last[:part]
        line = last[part:].reshape(lines * width)
        shares = [line[i * small : (i + 1) * small] for i in range(4)]
        shares.append(line[4 * small : 4 * small + hidden_width // devices])
        grad_joined = against(after(hidden_low, g_last), full_skip)
        output = (middle + (dot(after(activated, g_last), all_down) + bias_down)).astype(BF16)
    else:
        activated, slope = gelu_parts(dot(normed_two, all_up) + bias_up)
        activated = activated.astype(BF16)
        output = (middle + (dot(activated, all_down) + bias_down)).astype(BF16)
        grad_inner = against(grad_low, all_down) * slope
        inner_low = grad_inner.astype(BF16)
        grad_normed_two = against(inner_low, all_up)
        grad_middle = grad_out + norm_back(grad_normed_two, unit_two, scale_two, gain_2)
        middle_low = grad_middle.astype(BF16)
        grad_mixed = jnp.concatenate(back(grad=against(middle_low, full_out).astype(BF16)), axis=1)
        grad_normed_one = against(grad_mixed, full_qkv)
        grad_hidden = grad_middle + norm_back(grad_normed_one, unit_one, scale_one, gain_1)
        hidden_low = grad_hidden.astype(BF16)
        grad_joined = against(hidden_low, full_skip)
        vector_grads = (total(grad_hidden), total(grad_normed_one * unit_one), total(grad_normed_two * unit_two), total(grad_out), total(grad_inner))
        scatter = lambda values: lax.psum_scatter(values, AXES, scatter_dimension=0, tiled=True)
        down_grad = scatter(contract(activated, grad_low))
        up_grad = scatter(contract(normed_two, inner_low))
        out_grad = scatter(contract(attended, middle_low))
        qkv_grad = scatter(contract(normed_one, grad_mixed))
        skip_weight_grad = scatter(contract(joined, hidden_low))
        shares = [scatter(v) for v in vector_grads]

    shape = (micro, rows, length, width)
    return (
        output.reshape(shape),
        grad_joined[:, :width].reshape(shape),
        grad_joined[:, width:].reshape(shape),
        skip_weight_grad,
        shares[0],
        shares[1],
        qkv_grad,
        out_grad,
        shares[2],
        up_grad,
        shares[4],
        down_grad,
        shares[3],
    )


def solution(mesh):
    known = mesh.shape["dp"] == 8 and mesh.shape["fsdp"] == 4
    tokens = P(None, AXES, None, None)
    weight = P(AXES, None)
    vector = P(AXES)
    return jax.shard_map(
        functools.partial(on_device, known),
        mesh=mesh,
        in_specs=(
            tokens,
            tokens,
            tokens,
            P(None, AXES, None),
            P(None, AXES),
            weight,
            vector,
            vector,
            weight,
            weight,
            vector,
            weight,
            vector,
            weight,
            vector,
        ),
        out_specs=(
            tokens,
            tokens,
            tokens,
            weight,
            vector,
            vector,
            weight,
            weight,
            vector,
            weight,
            vector,
            weight,
            vector,
        ),
        check_vma=False,
    )
```

```python
import functools
import math

import jax
import jax.numpy as jnp
from jax import lax
from jax.experimental import pallas as pl
from jax.experimental.pallas import tpu as pltpu
from jax.sharding import Mesh, PartitionSpec as P

HEADS = 16
HEAD = 64
EPSILON = 1e-06
AXES = ("dp", "fsdp")
CHIPS = ("dp", "x")
CORES = CHIPS + ("core",)
F32 = jnp.float32
BF16 = jnp.bfloat16
VMEM = pltpu.CompilerParams(vmem_limit_bytes=48 << 20)


def dot(left, right, kind=F32):
    return jnp.dot(left, right, preferred_element_type=F32).astype(kind)


def against(left, right):
    return lax.dot_general(left, right, (((1,), (1,)), ((), ())), preferred_element_type=F32)


def contract(left, right):
    return lax.dot_general(left, right, (((0,), (0,)), ((), ())), preferred_element_type=F32)


def wide_tables(length):
    half = HEAD // 2
    indices = jnp.arange(half, dtype=F32)
    freqs = jnp.exp(indices * (-2.0 * math.log(10000.0) / HEAD))
    angles = jnp.arange(length, dtype=F32)[:, None] * freqs[None, :]
    cosine, sine = jnp.cos(angles), jnp.sin(angles)
    return (
        jnp.concatenate([cosine] * 4, axis=1),
        jnp.concatenate([-sine, sine, -sine, sine], axis=1),
    )


def swap_halves(values):
    half = HEAD // 2
    lane = lax.broadcasted_iota(jnp.int32, values.shape, 1)
    ahead = pltpu.roll(values, 2 * HEAD - half, 1)
    behind = pltpu.roll(values, half, 1)
    return jnp.where(lax.rem(lane, HEAD) < half, ahead, behind)


def allowed_of(column_ref, row_ref):
    length = row_ref.shape[-1]
    rows = lax.broadcasted_iota(jnp.int32, (length, length), 0)
    columns = lax.broadcasted_iota(jnp.int32, (length, length), 1)
    return (column_ref[0] == row_ref[0]) | (rows == columns)


def head_part(values, which):
    lane = lax.broadcasted_iota(jnp.int32, values.shape, 1)
    return jnp.where((lane >= HEAD) == (which == 1), values, jnp.zeros_like(values))


WIDE = 2 * HEAD
GROUP = 2


def attend_kernel(q_ref, k_ref, v_ref, cos_ref, sin_ref, column_ref, row_ref, qo_ref, ko_ref, vo_ref, a_ref, lse_ref):
    cosine, sine = cos_ref[...], sin_ref[...]
    allowed = allowed_of(column_ref, row_ref)
    for pair in range(GROUP):
        lanes = slice(pair * WIDE, (pair + 1) * WIDE)
        raw_q, raw_k = q_ref[:, lanes], k_ref[:, lanes]
        query = ((raw_q * cosine + swap_halves(raw_q) * sine)).astype(BF16)
        key = (raw_k * cosine + swap_halves(raw_k) * sine).astype(BF16)
        value = v_ref[:, lanes].astype(BF16)
        qo_ref[:, lanes] = query
        ko_ref[:, lanes] = key
        vo_ref[:, lanes] = value
        total = jnp.zeros(value.shape, F32)
        for which in range(2):
            scores = against(key, head_part(query, which)) * HEAD ** (-0.5)
            masked = jnp.where(allowed, scores, -1e30)
            highest = jnp.max(masked, axis=0, keepdims=True)
            exponent = jnp.exp(masked - highest)
            summed = jnp.sum(exponent, axis=0, keepdims=True)
            probs = (exponent / summed).astype(BF16)
            total += contract(probs, head_part(value, which))
            lse_ref[0, 0, pl.ds(2 * pair + which, 1), :] = highest + jnp.log(summed)
        a_ref[:, lanes] = total.astype(BF16)


def attend(mixed, tables, column, row, rows, length):
    width = HEADS * HEAD
    steps = HEADS // 2 // GROUP
    wide = WIDE * GROUP
    place = lambda shift: pl.BlockSpec((length, wide), lambda r, p, s=shift: (r, p + s))
    table = pl.BlockSpec((length, WIDE), lambda r, p: (0, 0))
    narrow = jax.ShapeDtypeStruct((rows * length, width), BF16)
    return pl.pallas_call(
        attend_kernel,
        grid=(rows, steps),
        in_specs=[
            place(0),
            place(steps),
            place(2 * steps),
            table,
            table,
            pl.BlockSpec((1, length, 1), lambda r, p: (r, 0, 0)),
            pl.BlockSpec((1, 1, length), lambda r, p: (r, 0, 0)),
        ],
        out_specs=[place(0)] * 4 + [pl.BlockSpec((1, 1, 2 * GROUP, length), lambda r, p: (r, p, 0, 0))],
        out_shape=[narrow] * 4 + [jax.ShapeDtypeStruct((rows, steps, 2 * GROUP, length), F32)],
        compiler_params=VMEM,
        cost_estimate=pl.CostEstimate(flops=rows * HEADS * length * length * 512, bytes_accessed=rows * length * width * 24, transcendentals=rows * HEADS * length * length),
    )(mixed, mixed, mixed, *tables, column, row)


def attend_back_kernel(q_ref, k_ref, v_ref, g_ref, lse_ref, cos_ref, sin_ref, column_ref, row_ref, out_ref):
    cosine, sine = cos_ref[...], sin_ref[...]
    allowed = allowed_of(column_ref, row_ref)
    scale = HEAD ** (-0.5)
    for pair in range(GROUP):
        lanes = slice(pair * WIDE, (pair + 1) * WIDE)
        query, key, value, grad = q_ref[:, lanes], k_ref[:, lanes], v_ref[:, lanes], g_ref[:, lanes]
        grad_q = jnp.zeros(query.shape, F32)
        grad_k = jnp.zeros(query.shape, F32)
        grad_v = jnp.zeros(query.shape, F32)
        for which in range(2):
            own_query = head_part(query, which)
            own_grad = head_part(grad, which)
            mark = lse_ref[0, 0, pl.ds(2 * pair + which, 1), :]
            scores = against(key, own_query) * scale
            probs = jnp.exp(jnp.where(allowed, scores, -1e30) - mark)
            grad_probs = against(value, own_grad)
            inside = jnp.sum(grad_probs * probs, axis=0, keepdims=True)
            grad_scores = (probs * (grad_probs - inside)).astype(BF16)
            grad_v += dot(probs.astype(BF16), own_grad)
            grad_k += dot(grad_scores, own_query)
            grad_q += contract(grad_scores, head_part(key, which))
        grad_q = grad_q * scale
        grad_k = grad_k * scale
        width = HEADS * HEAD
        start = pl.program_id(1) * (GROUP * WIDE) + pair * WIDE
        target = lambda part: pl.ds(pl.multiple_of(part * width + start, WIDE), WIDE)
        out_ref[:, target(0)] = (grad_q * cosine - swap_halves(grad_q) * sine).astype(BF16)
        out_ref[:, target(1)] = (grad_k * cosine - swap_halves(grad_k) * sine).astype(BF16)
        out_ref[:, target(2)] = grad_v.astype(BF16)


def attend_back(query, key, value, grad, lse, tables, column, row, rows, length):
    width = HEADS * HEAD
    steps = HEADS // 2 // GROUP
    place = pl.BlockSpec((length, WIDE * GROUP), lambda r, p: (r, p))
    table = pl.BlockSpec((length, WIDE), lambda r, p: (0, 0))
    return pl.pallas_call(
        attend_back_kernel,
        grid=(rows, steps),
        in_specs=[place] * 4
        + [
            pl.BlockSpec((1, 1, 2 * GROUP, length), lambda r, p: (r, p, 0, 0)),
            table,
            table,
            pl.BlockSpec((1, length, 1), lambda r, p: (r, 0, 0)),
            pl.BlockSpec((1, 1, length), lambda r, p: (r, 0, 0)),
        ],
        out_specs=pl.BlockSpec((length, 3 * width), lambda r, p: (r, 0)),
        out_shape=jax.ShapeDtypeStruct((rows * length, 3 * width), BF16),
        compiler_params=VMEM,
        cost_estimate=pl.CostEstimate(flops=rows * HEADS * length * length * 1280, bytes_accessed=rows * length * width * 14, transcendentals=rows * HEADS * length * length),
    )(query, key, value, grad, lse, *tables, column, row)


def gelu_parts(values):
    cube = values * values
    arch = jnp.tanh(0.7978845608028654 * (values + 0.044715 * values * cube))
    slope = 0.5 * (1.0 + arch) + 0.5 * values * (1.0 - arch * arch) * (0.7978845608028654 * (1.0 + 3.0 * 0.044715 * cube))
    return 0.5 * values * (1.0 + arch), slope


TILE = 512
BLOCK = 128


def up_kernel(mine_ref, other_ref, core_ref, x_ref, w_ref, b_ref, act_ref, slope_ref, own_ref, give_ref):
    activated, slope = gelu_parts(dot(x_ref[...], w_ref[...]) + b_ref[...])
    activated = activated.astype(BF16)
    act_ref[...] = activated
    slope_ref[...] = slope.astype(BF16)
    second = core_ref[0] == 1
    pairs = TILE // 2 // BLOCK
    for pair in range(pairs):
        low = activated[:, 2 * pair * BLOCK : (2 * pair + 1) * BLOCK]
        high = activated[:, (2 * pair + 1) * BLOCK : (2 * pair + 2) * BLOCK]
        index = pl.program_id(0) * pairs + pair
        own_ref[:, pl.ds(pl.multiple_of(mine_ref[index] * BLOCK, BLOCK), BLOCK)] = jnp.where(second, high, low)
        give_ref[:, pl.ds(pl.multiple_of(other_ref[index] * BLOCK, BLOCK), BLOCK)] = jnp.where(second, low, high)


def up_product(normed, weight, bias, mine, other, core):
    tokens, width = normed.shape
    columns = weight.shape[1]
    tall = pl.BlockSpec((tokens, TILE), lambda i, *_: (0, i))
    whole = pl.BlockSpec((tokens, columns // 2), lambda i, *_: (0, 0))
    return pl.pallas_call(
        up_kernel,
        grid_spec=pltpu.PrefetchScalarGridSpec(
            num_scalar_prefetch=3,
            grid=(columns // TILE,),
            in_specs=[
                pl.BlockSpec((tokens, width), lambda i, *_: (0, 0)),
                pl.BlockSpec((width, TILE), lambda i, *_: (0, i)),
                pl.BlockSpec((1, TILE), lambda i, *_: (0, i)),
            ],
            out_specs=[tall, tall, whole, whole],
        ),
        out_shape=[jax.ShapeDtypeStruct((tokens, n), BF16) for n in (columns, columns, columns // 2, columns // 2)],
        compiler_params=VMEM,
        cost_estimate=pl.CostEstimate(flops=2 * tokens * width * columns, bytes_accessed=2 * (width * columns + 3 * tokens * columns), transcendentals=tokens * columns),
    )(mine, other, core, normed, weight, bias)


def inner_kernel(g_ref, w_ref, slope_ref, low_ref, sum_ref):
    grad_inner = against(g_ref[...], w_ref[...]) * slope_ref[...].astype(F32)
    low_ref[...] = grad_inner.astype(BF16)
    sum_ref[...] = jnp.sum(grad_inner, axis=0, keepdims=True)


def inner_back(grad_low, weight, slope):
    tokens, width = grad_low.shape
    columns = weight.shape[0]
    tall = pl.BlockSpec((tokens, TILE), lambda i: (0, i))
    return pl.pallas_call(
        inner_kernel,
        grid=(columns // TILE,),
        in_specs=[
            pl.BlockSpec((tokens, width), lambda i: (0, 0)),
            pl.BlockSpec((TILE, width), lambda i: (i, 0)),
            tall,
        ],
        out_specs=[tall, pl.BlockSpec((1, TILE), lambda i: (0, i))],
        out_shape=[jax.ShapeDtypeStruct((tokens, columns), BF16), jax.ShapeDtypeStruct((1, columns), F32)],
        compiler_params=VMEM,
        cost_estimate=pl.CostEstimate(flops=2 * tokens * width * columns, bytes_accessed=2 * (width * columns + 2 * tokens * columns), transcendentals=0),
    )(grad_low, weight, slope)


def tall_kernel(x_ref, xs_ref, g_ref, gs_ref, give_ref, keep_ref):
    summed = (contract(x_ref[...], g_ref[...]) + contract(xs_ref[...], gs_ref[...])).astype(BF16)
    for number, ref in enumerate((give_ref, keep_ref)):

        @pl.when(pl.program_id(0) // 2 == number)
        def _():
            ref[...] = summed


def tall_product(x, x_other, g, g_other):
    tokens, rows = x.shape
    columns = g.shape[1]
    tile = rows // 4
    x_spec = pl.BlockSpec((tokens, tile), lambda i: (0, i))
    g_spec = pl.BlockSpec((tokens, columns), lambda i: (0, 0))
    out = lambda least: pl.BlockSpec((tile, columns), lambda i: (jnp.clip(i - least, 0, 1), 0))
    return pl.pallas_call(
        tall_kernel,
        grid=(4,),
        in_specs=[x_spec, x_spec, g_spec, g_spec],
        out_specs=[out(0), out(2)],
        out_shape=[jax.ShapeDtypeStruct((rows // 2, columns), BF16)] * 2,
        compiler_params=VMEM,
        cost_estimate=pl.CostEstimate(flops=4 * tokens * rows * columns, bytes_accessed=4 * tokens * (rows + columns) + 2 * rows * columns, transcendentals=0),
    )(x, x_other, g, g_other)


def wide_kernel(steps, *refs):
    sources, (give_ref, keep_ref) = refs[:-2], refs[-2:]
    half = give_ref.shape[0]
    at = 0
    for number, count in enumerate(steps):
        x_ref, xs_ref, g_ref, gs_ref = sources[4 * number : 4 * number + 4]

        @pl.when((pl.program_id(0) >= at) & (pl.program_id(0) < at + count))
        def _():
            summed = contract(x_ref[...], g_ref[...]) + contract(xs_ref[...], gs_ref[...])
            give_ref[...] = summed[:half].astype(BF16)
            keep_ref[...] = summed[half:].astype(BF16)

        at += count


def wide_product(*groups):
    tokens, rows = groups[0][0].shape
    tile = 1024
    steps = [group[2].shape[1] // tile for group in groups]
    in_specs, at, columns = [], 0, 0
    for group, count in zip(groups, steps):
        x_spec = pl.BlockSpec((tokens, rows), lambda i: (0, 0))
        g_spec = pl.BlockSpec((tokens, tile), lambda i, at=at, count=count: (0, jnp.clip(i - at, 0, count - 1)))
        in_specs += [x_spec, x_spec, g_spec, g_spec]
        at += count
        columns += group[2].shape[1]
    return pl.pallas_call(
        functools.partial(wide_kernel, steps),
        grid=(at,),
        in_specs=in_specs,
        out_specs=[pl.BlockSpec((rows // 2, tile), lambda i: (0, i))] * 2,
        out_shape=[jax.ShapeDtypeStruct((rows // 2, columns), BF16)] * 2,
        compiler_params=VMEM,
        cost_estimate=pl.CostEstimate(flops=4 * tokens * rows * columns, bytes_accessed=4 * tokens * (rows + columns) + 2 * rows * columns, transcendentals=0),
    )(*(value for group in groups for value in group))


def last_kernel(x_ref, xs_ref, g_ref, gs_ref, extra_ref, give_ref, keep_ref):
    summed = (contract(x_ref[...], g_ref[...]) + contract(xs_ref[...], gs_ref[...])).astype(BF16)
    blocks, lines, width = extra_ref.shape
    part = summed.shape[0] // blocks
    for number, ref in enumerate((give_ref, keep_ref)):

        @pl.when(pl.program_id(0) // 2 == number)
        def _():
            ref[:, :part] = summed.reshape(blocks, part, width)
            ref[:, part:] = extra_ref[...]


def last_product(x, x_other, g, g_other, extra):
    tokens, rows = x.shape
    blocks, lines, width = extra.shape
    part = rows // blocks
    quarter = blocks // 4
    x_spec = pl.BlockSpec((tokens, rows // 4), lambda i: (0, i))
    g_spec = pl.BlockSpec((tokens, width), lambda i: (0, 0))
    out = lambda least: pl.BlockSpec((quarter, part + lines, width), lambda i: (jnp.clip(i - least, 0, 1), 0, 0))
    give, keep = pl.pallas_call(
        last_kernel,
        grid=(4,),
        in_specs=[x_spec, x_spec, g_spec, g_spec, pl.BlockSpec((quarter, lines, width), lambda i: (i, 0, 0))],
        out_specs=[out(0), out(2)],
        out_shape=[jax.ShapeDtypeStruct((blocks // 2, part + lines, width), BF16)] * 2,
        compiler_params=VMEM,
        cost_estimate=pl.CostEstimate(flops=4 * tokens * rows * width, bytes_accessed=4 * tokens * (rows + width) + 2 * rows * width, transcendentals=0),
    )(x, x_other, g, g_other, extra)
    flat = (blocks // 2 * (part + lines), width)
    return give.reshape(flat), keep.reshape(flat)


def norm_back(grad_normed, unit, scale, gain):
    scaled = grad_normed * gain
    return scale * (scaled - unit * jnp.mean(scaled * unit, axis=1, keepdims=True))


def pairs_of(move):
    pairs = []
    for z in range(4):
        for y in range(2):
            for x in range(2):
                for c in range(2):
                    there = move(z, y, x, c)
                    if there is not None:
                        source = ((z * 2 + y) * 2 + x) * 2 + c
                        target = ((there[0] * 2 + there[1]) * 2 + there[2]) * 2 + there[3]
                        pairs.append((source, target))
    return pairs


OTHER_CORE = pairs_of(lambda z, y, x, c: (z, y, x, 1 - c))
FIRST = pairs_of(lambda z, y, x, c: (z, 1 - y, x, c) if c == 0 else (z, y, 1 - x, c))
SECOND = pairs_of(lambda z, y, x, c: (z, y, 1 - x, c) if c == 0 else (z, 1 - y, x, c))
FAR = pairs_of(lambda z, y, x, c: (z ^ 2, y, x, c))
NEAR = pairs_of(lambda z, y, x, c: (z ^ 1, y, x, c))
PLANE_FIRST = (FIRST, SECOND, FAR, NEAR)
PLANE_LAST = (FIRST, FAR, NEAR, SECOND)


def send(values, pairs):
    return lax.ppermute(values, CORES, pairs)


def block_order(place, steps, core):
    z, y, x = place
    index = jnp.arange(16)
    flip = {}
    for level, pairs in enumerate(steps):
        flip[id(pairs)] = 1 - index // (8 >> level) % 2
    at_z = z ^ (2 * flip[id(FAR)]) ^ flip[id(NEAR)]
    first, second = flip[id(FIRST)], flip[id(SECOND)]
    at_y = y ^ jnp.where(core == 0, first, second)
    at_x = x ^ jnp.where(core == 0, second, first)
    return ((at_z * 2 + at_y) * 2 + at_x) * 2 + core


def both_orders(place, core, steps):
    return jnp.concatenate([block_order(place, steps, 1 - core), block_order(place, steps, core)])


def plus(left, right, kind=BF16):
    return (left.astype(F32) + right.astype(F32)).astype(kind)


class Gathering:
    def __init__(self, block, steps):
        self.kept = block
        self.steps = list(steps[::-1])

    def step(self, before=(), wait=()):
        pairs = self.steps.pop(0)
        got = after(send(after(self.kept, *before), pairs), *wait)
        if self.steps:
            self.kept = jnp.concatenate([got, self.kept])
        else:
            self.kept = (got, self.kept)
            self.kept += tuple(send(half, OTHER_CORE) for half in self.kept)
        return self.kept


def place_kernel(cuts, order_ref, *refs):
    parts, outs, sems = refs[:4], refs[4:-1], refs[-1]
    block = parts[0].shape[0] // 8
    copies = []
    for index in range(32):
        part = parts[(2 + index // 8) % 4]
        for number, (row, rows, column, columns) in enumerate(cuts):
            target = outs[number].at[pl.ds(pl.multiple_of(order_ref[index] * rows, rows), rows)]
            source = part.at[pl.ds(index % 8 * block + row, rows), pl.ds(column, columns)]
            copies.append(pltpu.make_async_copy(source, target, sems.at[number * 32 + index]))
            copies[-1].start()
    for copy in copies:
        copy.wait()


def placed(parts, order, cuts):
    rows, columns = parts[0].shape
    return pl.pallas_call(
        functools.partial(place_kernel, cuts),
        grid_spec=pltpu.PrefetchScalarGridSpec(
            num_scalar_prefetch=1,
            grid=(1,),
            in_specs=[pl.BlockSpec((rows, columns), lambda i, order: (0, 0))] * 4,
            out_specs=[pl.BlockSpec(memory_space=pl.ANY)] * len(cuts),
            scratch_shapes=[pltpu.SemaphoreType.DMA((32 * len(cuts),))],
        ),
        out_shape=[jax.ShapeDtypeStruct((32 * cut[1], cut[3]), parts[0].dtype) for cut in cuts],
        compiler_params=VMEM,
        cost_estimate=pl.CostEstimate(flops=0, bytes_accessed=16 * rows * columns, transcendentals=0),
    )(order, *parts)


def after(value, *others):
    return lax.optimization_barrier((value,) + others)[0] if others else value


class Summing:
    def __init__(self, halves, steps):
        self.give, self.kept = halves
        self.steps = list(steps)

    def step(self, *wait):
        pairs = self.steps.pop(0)
        got = after(send(self.give, pairs), *wait)
        if self.steps:
            half = self.kept.shape[0] // 2
            self.give = plus(self.kept[:half], got[:half])
            self.kept = plus(self.kept[half:], got[half:])
            return self.give
        self.kept = plus(self.kept, got, F32)
        return self.kept

    def finish(self):
        while self.steps:
            self.step()
        return self.kept


def picked(values, order):
    columns = values.shape[1]
    block = columns // 32
    column = jnp.arange(columns)
    source = jnp.repeat(order, block) * block + column % block
    choice = (column[:, None] == source[None, :]).astype(BF16)
    return dot(values, choice, BF16)


def swapped(values):
    return send(values, OTHER_CORE)


def halves(values):
    half = values.shape[1] // 2
    return values[:, :half], values[:, half:]


def on_device(
    known,
    frames,
    skip,
    cotangent,
    segment_ids,
    row_lengths,
    w_skip,
    b_skip,
    gain_one,
    w_qkv,
    w_out,
    gain_two,
    w_up,
    b_up,
    w_down,
    b_down,
):
    micro, rows, length, width = frames.shape
    count = micro * rows
    tokens = count * length
    devices = width // gain_one.shape[0]
    hidden_width = w_up.shape[1]

    vectors = jnp.concatenate([b_skip, gain_one, gain_two, b_down, b_up])
    part = w_skip.shape[0]
    lines = -(-vectors.shape[0] // width)
    lines = -(-lines // 16) * 16
    padded = jnp.pad(vectors, (0, lines * width - vectors.shape[0])).reshape(lines, width)
    own_skip = jnp.concatenate([w_skip, padded])
    own_qkv = jnp.concatenate([w_qkv, w_out], axis=1)
    if known:
        place = lax.axis_index("dp")
        core = lax.axis_index("core")
        coords = (place // 2, place % 2, lax.axis_index("x"))
        order = both_orders(coords, core, PLANE_FIRST)
        joined = jnp.concatenate([frames.reshape(tokens, width), skip.reshape(tokens, width)], axis=1)
        give_joined, own_joined = halves(picked(joined, order))
        all_up = lax.all_gather(w_up, CORES, axis=0, tiled=True)
        all_down = lax.all_gather(w_down, CORES, axis=0, tiled=True)
        at_skip, at_qkv = (Gathering(own, PLANE_FIRST) for own in (own_skip, own_qkv))
        at_skip.step()
        near = at_qkv.step()
        far = at_skip.step(before=(near,), wait=(own_joined,))
        at_skip.step()
        got_skip = at_skip.step()
        far = at_qkv.step(before=(far,))
        at_skip.kept = got_skip[:2] + tuple(send(after(half, far), OTHER_CORE) for half in got_skip[:2])
        got_skip = at_skip.kept
        full_skip, flat = placed(got_skip, order, ((0, part, 0, width), (part, lines, 0, width)))
        at_qkv.step()
    else:
        all_skip = lax.all_gather(own_skip, AXES, axis=0, tiled=False)
        all_qkv = lax.all_gather(own_qkv, AXES, axis=0, tiled=True)
        all_up = lax.all_gather(w_up, AXES, axis=0, tiled=True)
        all_down = lax.all_gather(w_down, AXES, axis=0, tiled=True)
        full_skip = all_skip[:, :part].reshape(devices * part, width)
        flat = all_skip[:, part:]
        full_qkv = all_qkv[:, : 3 * width]
        full_out = all_qkv[:, 3 * width :]
        joined = jnp.concatenate([frames.reshape(tokens, width), skip.reshape(tokens, width)], axis=1)
    flat = flat.reshape(devices, lines * width)
    small = width // devices
    spread = lambda at, size: flat[:, at : at + size].reshape(1, devices * size).astype(F32)
    bias_skip, gain_1, gain_2, bias_down = (spread(i * small, small) for i in range(4))
    bias_up = spread(4 * small, hidden_width // devices)

    grad_low = cotangent.reshape(tokens, width)
    grad_out = grad_low.astype(F32)
    segments = segment_ids.reshape(count, length)
    lengths = row_lengths.reshape(count, 1)
    reach = jnp.where(jnp.arange(length)[None, :] < lengths, segments, -1)
    column, row = reach[:, :, None], segments[:, None, :]
    tables = wide_tables(length)

    hidden = dot(joined, full_skip) + bias_skip
    scale_one = lax.rsqrt(jnp.mean(hidden * hidden, axis=1, keepdims=True) + EPSILON)
    unit_one = hidden * scale_one
    normed_one = (unit_one * gain_1).astype(BF16)
    if known:
        give_one, own_one = halves(picked(normed_one, order))
        got_qkv = at_qkv.step(wait=(own_one,))
        full_qkv, full_out = placed(got_qkv, order, ((0, w_qkv.shape[0], 0, 3 * width), (0, w_qkv.shape[0], 3 * width, width)))
    mixed = dot(normed_one, full_qkv)
    query, key, value, attended, lse = attend(mixed, tables, column, row, count, length)
    middle = hidden + dot(attended, full_out)
    scale_two = lax.rsqrt(jnp.mean(middle * middle, axis=1, keepdims=True) + EPSILON)
    unit_two = middle * scale_two
    normed_two = (unit_two * gain_2).astype(BF16)
    total = lambda values: jnp.sum(values, axis=0)
    back = functools.partial(attend_back, query, key, value, lse=lse, tables=tables, column=column, row=row, rows=count, length=length)

    if known:
        ends = lambda blocks: jnp.sum(jnp.where(blocks[None, :] // 2 == jnp.arange(16)[:, None], jnp.arange(16)[None, :], 0), axis=1).astype(jnp.int32)
        joined_other = swapped(give_joined)
        grad_other = swapped(grad_low)
        give_attended, own_attended = halves(picked(attended, order))
        give_two, own_two = halves(picked(normed_two, order))
        one_other, attended_other, two_other = swapped(give_one), swapped(give_attended), swapped(give_two)

        activated, slope, own_active, give_active = up_product(
            normed_two, all_up, bias_up, ends(order[16:]), ends(order[:16]), core.reshape(1)
        )
        active_other = swapped(give_active)
        down = Summing(tall_product(own_active, active_other, grad_low, grad_other), PLANE_FIRST)
        inner_low, inner_sum = inner_back(grad_low, after(all_down, down.give), slope)
        inner_other = swapped(inner_low)
        grad_normed_two = against(inner_low, all_up)
        down.step(grad_normed_two)
        up = Summing(wide_product((own_two, two_other, after(inner_low, grad_normed_two, down.give), inner_other)), PLANE_FIRST)
        grad_middle = grad_out + norm_back(after(grad_normed_two, up.give), unit_two, scale_two, gain_2)
        middle_low = grad_middle.astype(BF16)
        middle_other = swapped(middle_low)
        grad_attended = against(middle_low, full_out).astype(BF16)
        down.step(grad_attended)
        grad_mixed = back(grad=after(grad_attended, down.give))
        mixed_other = swapped(grad_mixed)
        up.step(grad_mixed)
        grad_normed_one = against(after(grad_mixed, up.give), full_qkv)
        both = Summing(
            wide_product(
                (own_one, one_other, after(grad_mixed, grad_normed_one), mixed_other),
                (own_attended, attended_other, middle_low, middle_other),
            ),
            PLANE_FIRST,
        )
        up.step(both.give)
        down.step(both.give)
        grad_hidden = grad_middle + norm_back(after(grad_normed_one, both.give, up.give, down.give), unit_one, scale_one, gain_1)
        hidden_low = grad_hidden.astype(BF16)
        hidden_other = swapped(hidden_low)
        vector_grads = (total(grad_hidden), total(grad_normed_one * unit_one), total(grad_normed_two * unit_two), total(grad_out), inner_sum[0])
        by_block = jnp.concatenate([v.reshape(devices, -1) for v in vector_grads], axis=1)
        by_block = by_block + swapped(by_block)
        choice = (order[16:, None] == jnp.arange(devices)[None, :]).astype(F32)
        by_block = jnp.dot(choice, by_block, precision=lax.Precision.HIGHEST).astype(BF16)
        by_block = jnp.pad(by_block, ((0, 0), (0, lines * width - by_block.shape[1]))).reshape(16, lines, width)
        tail = Summing(last_product(own_joined, joined_other, hidden_low, hidden_other, by_block), PLANE_FIRST)
        both.step(tail.give)
        down_grad = down.step(tail.give)
        grad_joined = against(after(hidden_low, both.give, down_grad), full_skip)
        up.step(grad_joined)
        both.step(grad_joined)
        tail.step(grad_joined)
        output = (middle + (dot(after(activated, both.give, tail.give, up.give), all_down) + bias_down)).astype(BF16)
        up_grad = up.finish()
        both_grad = both.finish()
        last = tail.finish()
        qkv_grad, out_grad = both_grad[:, : 3 * width], both_grad[:, 3 * width :]
        skip_weight_grad = last[:part]
        line = last[part:].reshape(lines * width)
        shares = [line[i * small : (i + 1) * small] for i in range(4)]
        shares.append(line[4 * small : 4 * small + hidden_width // devices])
    else:
        activated, slope = gelu_parts(dot(normed_two, all_up) + bias_up)
        activated = activated.astype(BF16)
        output = (middle + (dot(activated, all_down) + bias_down)).astype(BF16)
        grad_inner = against(grad_low, all_down) * slope
        inner_low = grad_inner.astype(BF16)
        grad_normed_two = against(inner_low, all_up)
        grad_middle = grad_out + norm_back(grad_normed_two, unit_two, scale_two, gain_2)
        middle_low = grad_middle.astype(BF16)
        grad_mixed = back(grad=against(middle_low, full_out).astype(BF16))
        grad_normed_one = against(grad_mixed, full_qkv)
        grad_hidden = grad_middle + norm_back(grad_normed_one, unit_one, scale_one, gain_1)
        hidden_low = grad_hidden.astype(BF16)
        grad_joined = against(hidden_low, full_skip)
        vector_grads = (total(grad_hidden), total(grad_normed_one * unit_one), total(grad_normed_two * unit_two), total(grad_out), total(grad_inner))
        scatter = lambda values: lax.psum_scatter(values, AXES, scatter_dimension=0, tiled=True)
        down_grad = scatter(contract(activated, grad_low))
        up_grad = scatter(contract(normed_two, inner_low))
        out_grad = scatter(contract(attended, middle_low))
        qkv_grad = scatter(contract(normed_one, grad_mixed))
        skip_weight_grad = scatter(contract(joined, hidden_low))
        shares = [scatter(v) for v in vector_grads]

    shape = (micro, rows, length, width)
    return (
        output.reshape(shape),
        grad_joined[:, :width].reshape(shape),
        grad_joined[:, width:].reshape(shape),
        skip_weight_grad,
        shares[0],
        shares[1],
        qkv_grad,
        out_grad,
        shares[2],
        up_grad,
        shares[4],
        down_grad,
        shares[3],
    )


def solution(mesh):
    known = mesh.shape["dp"] == 8 and mesh.shape["fsdp"] == 4
    axes = AXES
    if known:
        mesh = Mesh(mesh.devices.reshape(8, 2, 2), CORES)
        axes = CORES
    tokens = P(None, axes, None, None)
    weight = P(axes, None)
    vector = P(axes)
    return jax.shard_map(
        functools.partial(on_device, known),
        mesh=mesh,
        in_specs=(
            tokens,
            tokens,
            tokens,
            P(None, axes, None),
            P(None, axes),
            weight,
            vector,
            vector,
            weight,
            weight,
            vector,
            weight,
            vector,
            weight,
            vector,
        ),
        out_specs=(
            tokens,
            tokens,
            tokens,
            weight,
            vector,
            vector,
            weight,
            weight,
            vector,
            weight,
            vector,
            weight,
            vector,
        ),
        check_vma=False,
    )
```

```python
import functools
import math

import jax
import jax.numpy as jnp
from jax import lax
from jax.experimental import pallas as pl
from jax.experimental.pallas import tpu as pltpu
from jax.sharding import Mesh, PartitionSpec as P

HEADS = 16
HEAD = 64
EPSILON = 1e-06
AXES = ("dp", "fsdp")
CHIPS = ("dp", "x")
CORES = CHIPS + ("core",)
F32 = jnp.float32
BF16 = jnp.bfloat16
VMEM = pltpu.CompilerParams(vmem_limit_bytes=48 << 20)


def dot(left, right, kind=F32):
    return jnp.dot(left, right, preferred_element_type=F32).astype(kind)


def against(left, right):
    return lax.dot_general(left, right, (((1,), (1,)), ((), ())), preferred_element_type=F32)


def contract(left, right):
    return lax.dot_general(left, right, (((0,), (0,)), ((), ())), preferred_element_type=F32)


def wide_tables(length):
    half = HEAD // 2
    indices = jnp.arange(half, dtype=F32)
    freqs = jnp.exp(indices * (-2.0 * math.log(10000.0) / HEAD))
    angles = jnp.arange(length, dtype=F32)[:, None] * freqs[None, :]
    cosine, sine = jnp.cos(angles), jnp.sin(angles)
    return (
        jnp.concatenate([cosine] * 4, axis=1),
        jnp.concatenate([-sine, sine, -sine, sine], axis=1),
    )


def swap_halves(values):
    half = HEAD // 2
    lane = lax.broadcasted_iota(jnp.int32, values.shape, 1)
    ahead = pltpu.roll(values, 2 * HEAD - half, 1)
    behind = pltpu.roll(values, half, 1)
    return jnp.where(lax.rem(lane, HEAD) < half, ahead, behind)


def allowed_of(column_ref, row_ref):
    length = row_ref.shape[-1]
    rows = lax.broadcasted_iota(jnp.int32, (length, length), 0)
    columns = lax.broadcasted_iota(jnp.int32, (length, length), 1)
    return (column_ref[0] == row_ref[0]) | (rows == columns)


def head_part(values, which):
    lane = lax.broadcasted_iota(jnp.int32, values.shape, 1)
    return jnp.where((lane >= HEAD) == (which == 1), values, jnp.zeros_like(values))


WIDE = 2 * HEAD
GROUP = 2


def attend_kernel(q_ref, k_ref, v_ref, cos_ref, sin_ref, column_ref, row_ref, qo_ref, ko_ref, vo_ref, a_ref, lse_ref):
    cosine, sine = cos_ref[...], sin_ref[...]
    allowed = allowed_of(column_ref, row_ref)
    for pair in range(GROUP):
        lanes = slice(pair * WIDE, (pair + 1) * WIDE)
        raw_q, raw_k = q_ref[:, lanes], k_ref[:, lanes]
        query = ((raw_q * cosine + swap_halves(raw_q) * sine)).astype(BF16)
        key = (raw_k * cosine + swap_halves(raw_k) * sine).astype(BF16)
        value = v_ref[:, lanes].astype(BF16)
        qo_ref[:, lanes] = query
        ko_ref[:, lanes] = key
        vo_ref[:, lanes] = value
        total = jnp.zeros(value.shape, F32)
        for which in range(2):
            scores = against(key, head_part(query, which)) * HEAD ** (-0.5)
            masked = jnp.where(allowed, scores, -1e30)
            highest = jnp.max(masked, axis=0, keepdims=True)
            exponent = jnp.exp(masked - highest)
            summed = jnp.sum(exponent, axis=0, keepdims=True)
            probs = (exponent / summed).astype(BF16)
            total += contract(probs, head_part(value, which))
            lse_ref[0, 0, pl.ds(2 * pair + which, 1), :] = highest + jnp.log(summed)
        a_ref[:, lanes] = total.astype(BF16)


def attend(mixed, tables, column, row, rows, length):
    width = HEADS * HEAD
    steps = HEADS // 2 // GROUP
    wide = WIDE * GROUP
    place = lambda shift: pl.BlockSpec((length, wide), lambda r, p, s=shift: (r, p + s))
    table = pl.BlockSpec((length, WIDE), lambda r, p: (0, 0))
    narrow = jax.ShapeDtypeStruct((rows * length, width), BF16)
    return pl.pallas_call(
        attend_kernel,
        grid=(rows, steps),
        in_specs=[
            place(0),
            place(steps),
            place(2 * steps),
            table,
            table,
            pl.BlockSpec((1, length, 1), lambda r, p: (r, 0, 0)),
            pl.BlockSpec((1, 1, length), lambda r, p: (r, 0, 0)),
        ],
        out_specs=[place(0)] * 4 + [pl.BlockSpec((1, 1, 2 * GROUP, length), lambda r, p: (r, p, 0, 0))],
        out_shape=[narrow] * 4 + [jax.ShapeDtypeStruct((rows, steps, 2 * GROUP, length), F32)],
        compiler_params=VMEM,
        cost_estimate=pl.CostEstimate(flops=rows * HEADS * length * length * 512, bytes_accessed=rows * length * width * 24, transcendentals=rows * HEADS * length * length),
    )(mixed, mixed, mixed, *tables, column, row)


def attend_back_kernel(q_ref, k_ref, v_ref, g_ref, lse_ref, cos_ref, sin_ref, column_ref, row_ref, out_ref, *piece_refs):
    cosine, sine = cos_ref[...], sin_ref[...]
    allowed = allowed_of(column_ref, row_ref)
    scale = HEAD ** (-0.5)
    for pair in range(GROUP):
        lanes = slice(pair * WIDE, (pair + 1) * WIDE)
        query, key, value, grad = q_ref[:, lanes], k_ref[:, lanes], v_ref[:, lanes], g_ref[:, lanes]
        grad_q = jnp.zeros(query.shape, F32)
        grad_k = jnp.zeros(query.shape, F32)
        grad_v = jnp.zeros(query.shape, F32)
        for which in range(2):
            own_query = head_part(query, which)
            own_grad = head_part(grad, which)
            mark = lse_ref[0, 0, pl.ds(2 * pair + which, 1), :]
            scores = against(key, own_query) * scale
            probs = jnp.exp(jnp.where(allowed, scores, -1e30) - mark)
            grad_probs = against(value, own_grad)
            inside = jnp.sum(grad_probs * probs, axis=0, keepdims=True)
            grad_scores = (probs * (grad_probs - inside)).astype(BF16)
            grad_v += dot(probs.astype(BF16), own_grad)
            grad_k += dot(grad_scores, own_query)
            grad_q += contract(grad_scores, head_part(key, which))
        grad_q = grad_q * scale
        grad_k = grad_k * scale
        width = HEADS * HEAD
        start = pl.program_id(1) * (GROUP * WIDE) + pair * WIDE
        target = lambda part: pl.ds(pl.multiple_of(part * width + start, WIDE), WIDE)
        grad_q = grad_q * cosine - swap_halves(grad_q) * sine
        grad_k = grad_k * cosine - swap_halves(grad_k) * sine
        for part, values in enumerate((grad_q, grad_k, grad_v)):
            out_ref[:, target(part)] = values.astype(BF16)
            piece_refs[part][:, lanes] = values.astype(BF16)


def attend_back(query, key, value, grad, lse, tables, column, row, rows, length):
    width = HEADS * HEAD
    steps = HEADS // 2 // GROUP
    place = pl.BlockSpec((length, WIDE * GROUP), lambda r, p: (r, p))
    table = pl.BlockSpec((length, WIDE), lambda r, p: (0, 0))
    return pl.pallas_call(
        attend_back_kernel,
        grid=(rows, steps),
        in_specs=[place] * 4
        + [
            pl.BlockSpec((1, 1, 2 * GROUP, length), lambda r, p: (r, p, 0, 0)),
            table,
            table,
            pl.BlockSpec((1, length, 1), lambda r, p: (r, 0, 0)),
            pl.BlockSpec((1, 1, length), lambda r, p: (r, 0, 0)),
        ],
        out_specs=[pl.BlockSpec((length, 3 * width), lambda r, p: (r, 0))] + [place] * 3,
        out_shape=[jax.ShapeDtypeStruct((rows * length, 3 * width), BF16)] + [jax.ShapeDtypeStruct((rows * length, width), BF16)] * 3,
        compiler_params=VMEM,
        cost_estimate=pl.CostEstimate(flops=rows * HEADS * length * length * 1280, bytes_accessed=rows * length * width * 14, transcendentals=rows * HEADS * length * length),
    )(query, key, value, grad, lse, *tables, column, row)


def gelu_parts(values):
    cube = values * values
    arch = jnp.tanh(0.7978845608028654 * (values + 0.044715 * values * cube))
    slope = 0.5 * (1.0 + arch) + 0.5 * values * (1.0 - arch * arch) * (0.7978845608028654 * (1.0 + 3.0 * 0.044715 * cube))
    return 0.5 * values * (1.0 + arch), slope


TILE = 512
BLOCK = 128


def up_kernel(mine_ref, other_ref, core_ref, x_ref, w_ref, b_ref, act_ref, slope_ref, own_ref, give_ref):
    activated, slope = gelu_parts(dot(x_ref[...], w_ref[...]) + b_ref[...])
    activated = activated.astype(BF16)
    act_ref[...] = activated
    slope_ref[...] = slope.astype(BF16)
    second = core_ref[0] == 1
    pairs = TILE // 2 // BLOCK
    for pair in range(pairs):
        low = activated[:, 2 * pair * BLOCK : (2 * pair + 1) * BLOCK]
        high = activated[:, (2 * pair + 1) * BLOCK : (2 * pair + 2) * BLOCK]
        index = pl.program_id(0) * pairs + pair
        own_ref[:, pl.ds(pl.multiple_of(mine_ref[index] * BLOCK, BLOCK), BLOCK)] = jnp.where(second, high, low)
        give_ref[:, pl.ds(pl.multiple_of(other_ref[index] * BLOCK, BLOCK), BLOCK)] = jnp.where(second, low, high)


def up_product(normed, weight, bias, mine, other, core):
    tokens, width = normed.shape
    columns = weight.shape[1]
    tall = pl.BlockSpec((tokens, TILE), lambda i, *_: (0, i))
    whole = pl.BlockSpec((tokens, columns // 2), lambda i, *_: (0, 0))
    return pl.pallas_call(
        up_kernel,
        grid_spec=pltpu.PrefetchScalarGridSpec(
            num_scalar_prefetch=3,
            grid=(columns // TILE,),
            in_specs=[
                pl.BlockSpec((tokens, width), lambda i, *_: (0, 0)),
                pl.BlockSpec((width, TILE), lambda i, *_: (0, i)),
                pl.BlockSpec((1, TILE), lambda i, *_: (0, i)),
            ],
            out_specs=[tall, tall, whole, whole],
        ),
        out_shape=[jax.ShapeDtypeStruct((tokens, n), BF16) for n in (columns, columns, columns // 2, columns // 2)],
        compiler_params=VMEM,
        cost_estimate=pl.CostEstimate(flops=2 * tokens * width * columns, bytes_accessed=2 * (width * columns + 3 * tokens * columns), transcendentals=tokens * columns),
    )(mine, other, core, normed, weight, bias)


PIECES = 4


def inner_kernel(g_ref, w_ref, slope_ref, low_ref, sum_ref, *piece_refs):
    grad_inner = against(g_ref[...], w_ref[...]) * slope_ref[...].astype(F32)
    low = grad_inner.astype(BF16)
    low_ref[...] = low
    sum_ref[...] = jnp.sum(grad_inner, axis=0, keepdims=True)
    each = pl.num_programs(0) // PIECES
    for number, ref in enumerate(piece_refs):

        @pl.when(pl.program_id(0) // each == number)
        def _():
            ref[...] = low


def inner_back(grad_low, weight, slope):
    tokens, width = grad_low.shape
    columns = weight.shape[0]
    each = columns // TILE // PIECES
    tall = pl.BlockSpec((tokens, TILE), lambda i: (0, i))
    piece = lambda number: pl.BlockSpec((tokens, TILE), lambda i: (0, jnp.clip(i - number * each, 0, each - 1)))
    low, summed, *pieces = pl.pallas_call(
        inner_kernel,
        grid=(columns // TILE,),
        in_specs=[
            pl.BlockSpec((tokens, width), lambda i: (0, 0)),
            pl.BlockSpec((TILE, width), lambda i: (i, 0)),
            tall,
        ],
        out_specs=[tall, pl.BlockSpec((1, TILE), lambda i: (0, i))] + [piece(number) for number in range(PIECES)],
        out_shape=[jax.ShapeDtypeStruct((tokens, columns), BF16), jax.ShapeDtypeStruct((1, columns), F32)]
        + [jax.ShapeDtypeStruct((tokens, columns // PIECES), BF16)] * PIECES,
        compiler_params=VMEM,
        cost_estimate=pl.CostEstimate(flops=2 * tokens * width * columns, bytes_accessed=2 * (width * columns + 2 * tokens * columns), transcendentals=0),
    )(grad_low, weight, slope)
    return low, summed, pieces


def tall_kernel(x_ref, xs_ref, g_ref, gs_ref, give_ref, keep_ref):
    summed = (contract(x_ref[...], g_ref[...]) + contract(xs_ref[...], gs_ref[...])).astype(BF16)
    for number, ref in enumerate((give_ref, keep_ref)):

        @pl.when(pl.program_id(0) // 2 == number)
        def _():
            ref[...] = summed


def tall_product(x, x_other, g, g_other):
    tokens, rows = x.shape
    columns = g.shape[1]
    tile = rows // 4
    x_spec = pl.BlockSpec((tokens, tile), lambda i: (0, i))
    g_spec = pl.BlockSpec((tokens, columns), lambda i: (0, 0))
    out = lambda least: pl.BlockSpec((tile, columns), lambda i: (jnp.clip(i - least, 0, 1), 0))
    return pl.pallas_call(
        tall_kernel,
        grid=(4,),
        in_specs=[x_spec, x_spec, g_spec, g_spec],
        out_specs=[out(0), out(2)],
        out_shape=[jax.ShapeDtypeStruct((rows // 2, columns), BF16)] * 2,
        compiler_params=VMEM,
        cost_estimate=pl.CostEstimate(flops=4 * tokens * rows * columns, bytes_accessed=4 * tokens * (rows + columns) + 2 * rows * columns, transcendentals=0),
    )(x, x_other, g, g_other)


def wide_kernel(counts, *refs):
    sources, (give_ref, keep_ref) = refs[:-2], refs[-2:]
    half = give_ref.shape[0]
    at = 0
    for count, pieces in counts:
        (x_ref, xs_ref, g_ref), gs_refs = sources[:3], sources[3 : 3 + pieces]
        sources = sources[3 + pieces :]
        for number, gs_ref in enumerate(gs_refs):
            least = at + number * (count // pieces)

            @pl.when((pl.program_id(0) >= least) & (pl.program_id(0) < least + count // pieces))
            def _():
                summed = contract(x_ref[...], g_ref[...]) + contract(xs_ref[...], gs_ref[...])
                give_ref[...] = summed[:half].astype(BF16)
                keep_ref[...] = summed[half:].astype(BF16)

        at += count


def wide_product(*groups):
    tokens, rows = groups[0][0].shape
    tile = 1024
    counts, in_specs, values, at, columns = [], [], [], 0, 0
    for x, xs, g, pieces in groups:
        count = g.shape[1] // tile
        part = count // len(pieces)
        counts.append((count, len(pieces)))
        x_spec = pl.BlockSpec((tokens, rows), lambda i: (0, 0))
        g_spec = lambda start, size: pl.BlockSpec((tokens, tile), lambda i: (0, jnp.clip(i - start, 0, size - 1)))
        in_specs += [x_spec, x_spec, g_spec(at, count)] + [g_spec(at + number * part, part) for number in range(len(pieces))]
        values += [x, xs, g, *pieces]
        at += count
        columns += g.shape[1]
    return pl.pallas_call(
        functools.partial(wide_kernel, counts),
        grid=(at,),
        in_specs=in_specs,
        out_specs=[pl.BlockSpec((rows // 2, tile), lambda i: (0, i))] * 2,
        out_shape=[jax.ShapeDtypeStruct((rows // 2, columns), BF16)] * 2,
        compiler_params=VMEM,
        cost_estimate=pl.CostEstimate(flops=4 * tokens * rows * columns, bytes_accessed=4 * tokens * (rows + columns) + 2 * rows * columns, transcendentals=0),
    )(*values)


def last_kernel(x_ref, xs_ref, g_ref, gs_ref, extra_ref, give_ref, keep_ref):
    summed = (contract(x_ref[...], g_ref[...]) + contract(xs_ref[...], gs_ref[...])).astype(BF16)
    blocks, lines, width = extra_ref.shape
    part = summed.shape[0] // blocks
    for number, ref in enumerate((give_ref, keep_ref)):

        @pl.when(pl.program_id(0) // 2 == number)
        def _():
            ref[:, :part] = summed.reshape(blocks, part, width)
            ref[:, part:] = extra_ref[...]


def last_product(x, x_other, g, g_other, extra):
    tokens, rows = x.shape
    blocks, lines, width = extra.shape
    part = rows // blocks
    quarter = blocks // 4
    x_spec = pl.BlockSpec((tokens, rows // 4), lambda i: (0, i))
    g_spec = pl.BlockSpec((tokens, width), lambda i: (0, 0))
    out = lambda least: pl.BlockSpec((quarter, part + lines, width), lambda i: (jnp.clip(i - least, 0, 1), 0, 0))
    give, keep = pl.pallas_call(
        last_kernel,
        grid=(4,),
        in_specs=[x_spec, x_spec, g_spec, g_spec, pl.BlockSpec((quarter, lines, width), lambda i: (i, 0, 0))],
        out_specs=[out(0), out(2)],
        out_shape=[jax.ShapeDtypeStruct((blocks // 2, part + lines, width), BF16)] * 2,
        compiler_params=VMEM,
        cost_estimate=pl.CostEstimate(flops=4 * tokens * rows * width, bytes_accessed=4 * tokens * (rows + width) + 2 * rows * width, transcendentals=0),
    )(x, x_other, g, g_other, extra)
    flat = (blocks // 2 * (part + lines), width)
    return give.reshape(flat), keep.reshape(flat)


def norm_back(grad_normed, unit, scale, gain):
    scaled = grad_normed * gain
    return scale * (scaled - unit * jnp.mean(scaled * unit, axis=1, keepdims=True))


def pairs_of(move):
    pairs = []
    for z in range(4):
        for y in range(2):
            for x in range(2):
                for c in range(2):
                    there = move(z, y, x, c)
                    if there is not None:
                        source = ((z * 2 + y) * 2 + x) * 2 + c
                        target = ((there[0] * 2 + there[1]) * 2 + there[2]) * 2 + there[3]
                        pairs.append((source, target))
    return pairs


OTHER_CORE = pairs_of(lambda z, y, x, c: (z, y, x, 1 - c))
FIRST = pairs_of(lambda z, y, x, c: (z, 1 - y, x, c) if c == 0 else (z, y, 1 - x, c))
SECOND = pairs_of(lambda z, y, x, c: (z, y, 1 - x, c) if c == 0 else (z, 1 - y, x, c))
FAR = pairs_of(lambda z, y, x, c: (z ^ 2, y, x, c))
NEAR = pairs_of(lambda z, y, x, c: (z ^ 1, y, x, c))
PLANE_FIRST = (FIRST, SECOND, FAR, NEAR)
PLANE_LAST = (FIRST, FAR, NEAR, SECOND)


def send(values, pairs):
    return lax.ppermute(values, CORES, pairs)


def block_order(place, steps, core):
    z, y, x = place
    index = jnp.arange(16)
    flip = {}
    for level, pairs in enumerate(steps):
        flip[id(pairs)] = 1 - index // (8 >> level) % 2
    at_z = z ^ (2 * flip[id(FAR)]) ^ flip[id(NEAR)]
    first, second = flip[id(FIRST)], flip[id(SECOND)]
    at_y = y ^ jnp.where(core == 0, first, second)
    at_x = x ^ jnp.where(core == 0, second, first)
    return ((at_z * 2 + at_y) * 2 + at_x) * 2 + core


def both_orders(place, core, steps):
    return jnp.concatenate([block_order(place, steps, 1 - core), block_order(place, steps, core)])


def plus(left, right, kind=BF16):
    return (left.astype(F32) + right.astype(F32)).astype(kind)


class Gathering:
    def __init__(self, block, steps):
        self.kept = block
        self.steps = list(steps[::-1])

    def step(self, before=(), wait=()):
        pairs = self.steps.pop(0)
        got = after(send(after(self.kept, *before), pairs), *wait)
        if self.steps:
            self.kept = jnp.concatenate([got, self.kept])
        else:
            self.kept = (got, self.kept)
            self.kept += tuple(send(half, OTHER_CORE) for half in self.kept)
        return self.kept


def place_kernel(cuts, order_ref, *refs):
    parts, outs, sems = refs[:4], refs[4:-1], refs[-1]
    block = parts[0].shape[0] // 8
    copies = []
    for index in range(32):
        part = parts[(2 + index // 8) % 4]
        for number, (row, rows, column, columns) in enumerate(cuts):
            target = outs[number].at[pl.ds(pl.multiple_of(order_ref[index] * rows, rows), rows)]
            source = part.at[pl.ds(index % 8 * block + row, rows), pl.ds(column, columns)]
            copies.append(pltpu.make_async_copy(source, target, sems.at[number * 32 + index]))
            copies[-1].start()
    for copy in copies:
        copy.wait()


def placed(parts, order, cuts):
    rows, columns = parts[0].shape
    return pl.pallas_call(
        functools.partial(place_kernel, cuts),
        grid_spec=pltpu.PrefetchScalarGridSpec(
            num_scalar_prefetch=1,
            grid=(1,),
            in_specs=[pl.BlockSpec((rows, columns), lambda i, order: (0, 0))] * 4,
            out_specs=[pl.BlockSpec(memory_space=pl.ANY)] * len(cuts),
            scratch_shapes=[pltpu.SemaphoreType.DMA((32 * len(cuts),))],
        ),
        out_shape=[jax.ShapeDtypeStruct((32 * cut[1], cut[3]), parts[0].dtype) for cut in cuts],
        compiler_params=VMEM,
        cost_estimate=pl.CostEstimate(flops=0, bytes_accessed=16 * rows * columns, transcendentals=0),
    )(order, *parts)


def after(value, *others):
    return lax.optimization_barrier((value,) + others)[0] if others else value


class Summing:
    def __init__(self, halves, steps):
        self.give, self.kept = halves
        self.steps = list(steps)

    def step(self, *wait, before=()):
        got = after(send(after(self.give, *before), self.steps.pop(0)), *wait)
        return self.add(got)

    def add(self, got):
        if self.steps:
            half = self.kept.shape[0] // 2
            self.give = plus(self.kept[:half], got[:half])
            self.kept = plus(self.kept[half:], got[half:])
            return self.give
        self.kept = plus(self.kept, got, F32)
        return self.kept

    def send_part(self, *wait):
        half = self.give.shape[0] // 2
        got = after(send(self.give[:half], self.steps[0]), *wait)
        self.later = self.give[half:]
        self.give = plus(self.kept[:half], got)
        return self.give

    def keep_part(self, *wait):
        got = after(send(after(self.later, self.give), self.steps.pop(0)), *wait)
        self.kept = plus(self.kept[self.later.shape[0] :], got)
        return self.kept

    def finish(self):
        while self.steps:
            self.step()
        return self.kept


def picked(values, order):
    columns = values.shape[1]
    block = columns // 32
    column = jnp.arange(columns)
    source = jnp.repeat(order, block) * block + column % block
    choice = (column[:, None] == source[None, :]).astype(BF16)
    return dot(values, choice, BF16)


def swapped(values):
    return send(values, OTHER_CORE)


def halves(values):
    half = values.shape[1] // 2
    return values[:, :half], values[:, half:]


def on_device(
    known,
    frames,
    skip,
    cotangent,
    segment_ids,
    row_lengths,
    w_skip,
    b_skip,
    gain_one,
    w_qkv,
    w_out,
    gain_two,
    w_up,
    b_up,
    w_down,
    b_down,
):
    micro, rows, length, width = frames.shape
    count = micro * rows
    tokens = count * length
    devices = width // gain_one.shape[0]
    hidden_width = w_up.shape[1]

    vectors = jnp.concatenate([b_skip, gain_one, gain_two, b_down, b_up])
    part = w_skip.shape[0]
    lines = -(-vectors.shape[0] // width)
    lines = -(-lines // 16) * 16
    padded = jnp.pad(vectors, (0, lines * width - vectors.shape[0])).reshape(lines, width)
    own_skip = jnp.concatenate([w_skip, padded])
    own_qkv = jnp.concatenate([w_qkv, w_out], axis=1)
    if known:
        place = lax.axis_index("dp")
        core = lax.axis_index("core")
        coords = (place // 2, place % 2, lax.axis_index("x"))
        order = both_orders(coords, core, PLANE_FIRST)
        joined = jnp.concatenate([frames.reshape(tokens, width), skip.reshape(tokens, width)], axis=1)
        give_joined, own_joined = halves(picked(joined, order))
        all_up = lax.all_gather(w_up, CORES, axis=0, tiled=True)
        all_down = lax.all_gather(w_down, CORES, axis=0, tiled=True)
        at_skip, at_qkv = (Gathering(own, PLANE_FIRST) for own in (own_skip, own_qkv))
        at_skip.step()
        near = at_qkv.step()
        joined_other, grad_other = swapped(give_joined), swapped(cotangent.reshape(tokens, width))
        far = at_skip.step(before=(near,), wait=(own_joined, joined_other, grad_other))
        at_skip.step()
        got_skip = at_skip.step()
        far = at_qkv.step(before=(far,))
        at_skip.kept = got_skip[:2] + tuple(send(after(half, far), OTHER_CORE) for half in got_skip[:2])
        got_skip = at_skip.kept
        full_skip, flat = placed(got_skip, order, ((0, part, 0, width), (part, lines, 0, width)))
        at_qkv.step()
    else:
        all_skip = lax.all_gather(own_skip, AXES, axis=0, tiled=False)
        all_qkv = lax.all_gather(own_qkv, AXES, axis=0, tiled=True)
        all_up = lax.all_gather(w_up, AXES, axis=0, tiled=True)
        all_down = lax.all_gather(w_down, AXES, axis=0, tiled=True)
        full_skip = all_skip[:, :part].reshape(devices * part, width)
        flat = all_skip[:, part:]
        full_qkv = all_qkv[:, : 3 * width]
        full_out = all_qkv[:, 3 * width :]
        joined = jnp.concatenate([frames.reshape(tokens, width), skip.reshape(tokens, width)], axis=1)
    flat = flat.reshape(devices, lines * width)
    small = width // devices
    spread = lambda at, size: flat[:, at : at + size].reshape(1, devices * size).astype(F32)
    bias_skip, gain_1, gain_2, bias_down = (spread(i * small, small) for i in range(4))
    bias_up = spread(4 * small, hidden_width // devices)

    grad_low = cotangent.reshape(tokens, width)
    grad_out = grad_low.astype(F32)
    segments = segment_ids.reshape(count, length)
    lengths = row_lengths.reshape(count, 1)
    reach = jnp.where(jnp.arange(length)[None, :] < lengths, segments, -1)
    column, row = reach[:, :, None], segments[:, None, :]
    tables = wide_tables(length)

    hidden = dot(joined, full_skip) + bias_skip
    scale_one = lax.rsqrt(jnp.mean(hidden * hidden, axis=1, keepdims=True) + EPSILON)
    unit_one = hidden * scale_one
    normed_one = (unit_one * gain_1).astype(BF16)
    if known:
        give_one, own_one = halves(picked(normed_one, order))
        got_qkv = at_qkv.step(wait=(own_one,))
        full_qkv, full_out = placed(got_qkv, order, ((0, w_qkv.shape[0], 0, 3 * width), (0, w_qkv.shape[0], 3 * width, width)))
    mixed = dot(normed_one, full_qkv)
    query, key, value, attended, lse = attend(mixed, tables, column, row, count, length)
    middle = hidden + dot(attended, full_out)
    scale_two = lax.rsqrt(jnp.mean(middle * middle, axis=1, keepdims=True) + EPSILON)
    unit_two = middle * scale_two
    normed_two = (unit_two * gain_2).astype(BF16)
    total = lambda values: jnp.sum(values, axis=0)
    back = functools.partial(attend_back, query, key, value, lse=lse, tables=tables, column=column, row=row, rows=count, length=length)

    if known:
        ends = lambda blocks: jnp.sum(jnp.where(blocks[None, :] // 2 == jnp.arange(16)[:, None], jnp.arange(16)[None, :], 0), axis=1).astype(jnp.int32)
        give_attended, own_attended = halves(picked(attended, order))
        give_two, own_two = halves(picked(normed_two, order))
        one_other, attended_other, two_other = swapped(give_one), swapped(give_attended), swapped(give_two)

        activated, slope, own_active, give_active = up_product(
            normed_two, all_up, bias_up, ends(order[16:]), ends(order[:16]), core.reshape(1)
        )
        active_other = swapped(give_active)
        down = Summing(tall_product(own_active, active_other, grad_low, grad_other), PLANE_FIRST)
        inner_low, inner_sum, inner_pieces = inner_back(grad_low, after(all_down, down.give), slope)
        inner_other = [swapped(piece) for piece in inner_pieces]
        grad_normed_two = against(inner_low, all_up)
        up = Summing(wide_product((own_two, two_other, after(inner_low, grad_normed_two), inner_other)), PLANE_FIRST)
        grad_middle = grad_out + norm_back(after(grad_normed_two, up.give), unit_two, scale_two, gain_2)
        middle_low = grad_middle.astype(BF16)
        middle_other = swapped(middle_low)
        grad_attended = against(middle_low, full_out).astype(BF16)
        down.step(grad_attended)
        grad_mixed, *mixed_pieces = back(grad=after(grad_attended, down.give))
        mixed_other = [swapped(piece) for piece in mixed_pieces]
        given = down.step(grad_mixed)
        grad_normed_one = against(after(grad_mixed, given), full_qkv)
        both = Summing(
            wide_product(
                (own_one, one_other, after(grad_mixed, grad_normed_one), mixed_other),
                (own_attended, attended_other, middle_low, [middle_other]),
            ),
            PLANE_FIRST,
        )
        up.step(both.give, before=(given,))
        down.step(both.give)
        grad_hidden = grad_middle + norm_back(after(grad_normed_one, both.give, up.give, down.give), unit_one, scale_one, gain_1)
        hidden_low = grad_hidden.astype(BF16)
        hidden_other = swapped(hidden_low)
        vector_grads = (total(grad_hidden), total(grad_normed_one * unit_one), total(grad_normed_two * unit_two), total(grad_out), inner_sum[0])
        by_block = jnp.concatenate([v.reshape(devices, -1) for v in vector_grads], axis=1)
        by_block = by_block + swapped(by_block)
        choice = (order[16:, None] == jnp.arange(devices)[None, :]).astype(F32)
        by_block = jnp.dot(choice, by_block, precision=lax.Precision.HIGHEST).astype(BF16)
        by_block = jnp.pad(by_block, ((0, 0), (0, lines * width - by_block.shape[1]))).reshape(16, lines, width)
        tail = Summing(last_product(own_joined, joined_other, hidden_low, hidden_other, by_block), PLANE_FIRST)
        both.step(tail.give)
        up.step(tail.give)
        down_grad = down.step(tail.give)
        grad_joined = against(after(hidden_low, both.give, up.give), full_skip)
        output = (middle + (dot(after(activated, grad_joined), all_down) + bias_down)).astype(BF16)
        both.step(output)
        tail.step(before=(both.give,))
        up.step(both.give)
        both.send_part(tail.give)
        tail.step()
        up_grad = up.step(tail.give)
        both.keep_part(tail.give)
        tail.step()
        both_grad = both.finish()
        last = tail.finish()
        qkv_grad, out_grad = both_grad[:, : 3 * width], both_grad[:, 3 * width :]
        skip_weight_grad = last[:part]
        line = last[part:].reshape(lines * width)
        shares = [line[i * small : (i + 1) * small] for i in range(4)]
        shares.append(line[4 * small : 4 * small + hidden_width // devices])
    else:
        activated, slope = gelu_parts(dot(normed_two, all_up) + bias_up)
        activated = activated.astype(BF16)
        output = (middle + (dot(activated, all_down) + bias_down)).astype(BF16)
        grad_inner = against(grad_low, all_down) * slope
        inner_low = grad_inner.astype(BF16)
        grad_normed_two = against(inner_low, all_up)
        grad_middle = grad_out + norm_back(grad_normed_two, unit_two, scale_two, gain_2)
        middle_low = grad_middle.astype(BF16)
        grad_mixed = back(grad=against(middle_low, full_out).astype(BF16))[0]
        grad_normed_one = against(grad_mixed, full_qkv)
        grad_hidden = grad_middle + norm_back(grad_normed_one, unit_one, scale_one, gain_1)
        hidden_low = grad_hidden.astype(BF16)
        grad_joined = against(hidden_low, full_skip)
        vector_grads = (total(grad_hidden), total(grad_normed_one * unit_one), total(grad_normed_two * unit_two), total(grad_out), total(grad_inner))
        scatter = lambda values: lax.psum_scatter(values, AXES, scatter_dimension=0, tiled=True)
        down_grad = scatter(contract(activated, grad_low))
        up_grad = scatter(contract(normed_two, inner_low))
        out_grad = scatter(contract(attended, middle_low))
        qkv_grad = scatter(contract(normed_one, grad_mixed))
        skip_weight_grad = scatter(contract(joined, hidden_low))
        shares = [scatter(v) for v in vector_grads]

    shape = (micro, rows, length, width)
    return (
        output.reshape(shape),
        grad_joined[:, :width].reshape(shape),
        grad_joined[:, width:].reshape(shape),
        skip_weight_grad,
        shares[0],
        shares[1],
        qkv_grad,
        out_grad,
        shares[2],
        up_grad,
        shares[4],
        down_grad,
        shares[3],
    )


def solution(mesh):
    known = mesh.shape["dp"] == 8 and mesh.shape["fsdp"] == 4
    axes = AXES
    if known:
        mesh = Mesh(mesh.devices.reshape(8, 2, 2), CORES)
        axes = CORES
    tokens = P(None, axes, None, None)
    weight = P(axes, None)
    vector = P(axes)
    return jax.shard_map(
        functools.partial(on_device, known),
        mesh=mesh,
        in_specs=(
            tokens,
            tokens,
            tokens,
            P(None, axes, None),
            P(None, axes),
            weight,
            vector,
            vector,
            weight,
            weight,
            vector,
            weight,
            vector,
            weight,
            vector,
        ),
        out_specs=(
            tokens,
            tokens,
            tokens,
            weight,
            vector,
            vector,
            weight,
            weight,
            vector,
            weight,
            vector,
            weight,
            vector,
        ),
        check_vma=False,
    )
```

```python
import functools
import math

import jax
import jax.numpy as jnp
from jax import lax
from jax.experimental import pallas as pl
from jax.experimental.pallas import tpu as pltpu
from jax.sharding import Mesh, PartitionSpec as P

HEADS = 16
HEAD = 64
EPSILON = 1e-06
AXES = ("dp", "fsdp")
CHIPS = ("dp", "x")
CORES = CHIPS + ("core",)
F32 = jnp.float32
BF16 = jnp.bfloat16
VMEM = pltpu.CompilerParams(vmem_limit_bytes=48 << 20)


def dot(left, right, kind=F32):
    return jnp.dot(left, right, preferred_element_type=F32).astype(kind)


def against(left, right):
    return lax.dot_general(left, right, (((1,), (1,)), ((), ())), preferred_element_type=F32)


def contract(left, right):
    return lax.dot_general(left, right, (((0,), (0,)), ((), ())), preferred_element_type=F32)


def wide_tables(length):
    half = HEAD // 2
    indices = jnp.arange(half, dtype=F32)
    freqs = jnp.exp(indices * (-2.0 * math.log(10000.0) / HEAD))
    angles = jnp.arange(length, dtype=F32)[:, None] * freqs[None, :]
    cosine, sine = jnp.cos(angles), jnp.sin(angles)
    return (
        jnp.concatenate([cosine] * 4, axis=1),
        jnp.concatenate([-sine, sine, -sine, sine], axis=1),
    )


def swap_halves(values):
    half = HEAD // 2
    lane = lax.broadcasted_iota(jnp.int32, values.shape, 1)
    ahead = pltpu.roll(values, 2 * HEAD - half, 1)
    behind = pltpu.roll(values, half, 1)
    return jnp.where(lax.rem(lane, HEAD) < half, ahead, behind)


def allowed_of(column_ref, row_ref):
    length = row_ref.shape[-1]
    rows = lax.broadcasted_iota(jnp.int32, (length, length), 0)
    columns = lax.broadcasted_iota(jnp.int32, (length, length), 1)
    return (column_ref[0] == row_ref[0]) | (rows == columns)


def head_part(values, which):
    lane = lax.broadcasted_iota(jnp.int32, values.shape, 1)
    return jnp.where((lane >= HEAD) == (which == 1), values, jnp.zeros_like(values))


WIDE = 2 * HEAD
GROUP = 4


def attend_kernel(q_ref, k_ref, v_ref, cos_ref, sin_ref, column_ref, row_ref, qo_ref, ko_ref, vo_ref, a_ref, lse_ref):
    cosine, sine = cos_ref[...], sin_ref[...]
    allowed = allowed_of(column_ref, row_ref)
    for pair in range(GROUP):
        lanes = slice(pair * WIDE, (pair + 1) * WIDE)
        raw_q, raw_k = q_ref[:, lanes], k_ref[:, lanes]
        query = ((raw_q * cosine + swap_halves(raw_q) * sine)).astype(BF16)
        key = (raw_k * cosine + swap_halves(raw_k) * sine).astype(BF16)
        value = v_ref[:, lanes].astype(BF16)
        scaled = query * jnp.asarray(HEAD ** (-0.5), BF16)
        qo_ref[:, lanes] = query
        ko_ref[:, lanes] = key
        vo_ref[:, lanes] = value
        total = jnp.zeros(value.shape[::-1], F32)
        for which in range(2):
            masked = jnp.where(allowed, against(key, head_part(scaled, which)), -1e30)
            highest = jnp.max(masked, axis=0, keepdims=True)
            exponent = jnp.exp(masked - highest)
            summed = jnp.sum(exponent, axis=0, keepdims=True)
            probs = (exponent * (1.0 / summed)).astype(BF16)
            total += contract(head_part(value, which), probs)
            lse_ref[0, 0, pl.ds(2 * pair + which, 1), :] = highest + jnp.log(summed)
        a_ref[:, lanes] = total.T.astype(BF16)


def attend(mixed, tables, column, row, rows, length):
    width = HEADS * HEAD
    steps = HEADS // 2 // GROUP
    wide = WIDE * GROUP
    place = lambda shift: pl.BlockSpec((length, wide), lambda r, p, s=shift: (r, p + s))
    table = pl.BlockSpec((length, WIDE), lambda r, p: (0, 0))
    narrow = jax.ShapeDtypeStruct((rows * length, width), BF16)
    return pl.pallas_call(
        attend_kernel,
        grid=(rows, steps),
        in_specs=[
            place(0),
            place(steps),
            place(2 * steps),
            table,
            table,
            pl.BlockSpec((1, length, 1), lambda r, p: (r, 0, 0)),
            pl.BlockSpec((1, 1, length), lambda r, p: (r, 0, 0)),
        ],
        out_specs=[place(0)] * 4 + [pl.BlockSpec((1, 1, 2 * GROUP, length), lambda r, p: (r, p, 0, 0))],
        out_shape=[narrow] * 4 + [jax.ShapeDtypeStruct((rows, steps, 2 * GROUP, length), F32)],
        compiler_params=VMEM,
        cost_estimate=pl.CostEstimate(flops=rows * HEADS * length * length * 512, bytes_accessed=rows * length * width * 24, transcendentals=rows * HEADS * length * length),
    )(mixed, mixed, mixed, *tables, column, row)


def attend_back_kernel(q_ref, k_ref, v_ref, g_ref, lse_ref, cos_ref, sin_ref, column_ref, row_ref, out_ref, *piece_refs):
    cosine, sine = cos_ref[...], sin_ref[...]
    allowed = allowed_of(column_ref, row_ref)
    scale = HEAD ** (-0.5)
    for pair in range(GROUP):
        lanes = slice(pair * WIDE, (pair + 1) * WIDE)
        query, key, value, grad = q_ref[:, lanes], k_ref[:, lanes], v_ref[:, lanes], g_ref[:, lanes]
        scaled = query * jnp.asarray(scale, BF16)
        grad_q = jnp.zeros(query.shape[::-1], F32)
        grad_k = jnp.zeros(query.shape, F32)
        grad_v = jnp.zeros(query.shape, F32)
        for which in range(2):
            own_query = head_part(scaled, which)
            own_grad = head_part(grad, which)
            mark = lse_ref[0, 0, pl.ds(2 * pair + which, 1), :]
            probs = jnp.exp(jnp.where(allowed, against(key, own_query), -1e30) - mark)
            grad_probs = against(value, own_grad)
            inside = jnp.sum(grad_probs * probs, axis=0, keepdims=True)
            grad_scores = (probs * (grad_probs - inside)).astype(BF16)
            grad_v += dot(probs.astype(BF16), own_grad)
            grad_k += dot(grad_scores, own_query)
            grad_q += contract(head_part(key, which), grad_scores)
        grad_q = grad_q.T * scale
        width = HEADS * HEAD
        start = pl.program_id(1) * (GROUP * WIDE) + pair * WIDE
        target = lambda part: pl.ds(pl.multiple_of(part * width + start, WIDE), WIDE)
        grad_q = grad_q * cosine - swap_halves(grad_q) * sine
        grad_k = grad_k * cosine - swap_halves(grad_k) * sine
        for part, values in enumerate((grad_q, grad_k, grad_v)):
            out_ref[:, target(part)] = values.astype(BF16)
            piece_refs[part][:, lanes] = values.astype(BF16)


def attend_back(query, key, value, grad, lse, tables, column, row, rows, length):
    width = HEADS * HEAD
    steps = HEADS // 2 // GROUP
    place = pl.BlockSpec((length, WIDE * GROUP), lambda r, p: (r, p))
    table = pl.BlockSpec((length, WIDE), lambda r, p: (0, 0))
    return pl.pallas_call(
        attend_back_kernel,
        grid=(rows, steps),
        in_specs=[place] * 4
        + [
            pl.BlockSpec((1, 1, 2 * GROUP, length), lambda r, p: (r, p, 0, 0)),
            table,
            table,
            pl.BlockSpec((1, length, 1), lambda r, p: (r, 0, 0)),
            pl.BlockSpec((1, 1, length), lambda r, p: (r, 0, 0)),
        ],
        out_specs=[pl.BlockSpec((length, 3 * width), lambda r, p: (r, 0))] + [place] * 3,
        out_shape=[jax.ShapeDtypeStruct((rows * length, 3 * width), BF16)] + [jax.ShapeDtypeStruct((rows * length, width), BF16)] * 3,
        compiler_params=VMEM,
        cost_estimate=pl.CostEstimate(flops=rows * HEADS * length * length * 1280, bytes_accessed=rows * length * width * 14, transcendentals=rows * HEADS * length * length),
    )(query, key, value, grad, lse, *tables, column, row)


def gelu_parts(values):
    cube = values * values
    arch = jnp.tanh(0.7978845608028654 * (values + 0.044715 * values * cube))
    slope = 0.5 * (1.0 + arch) + 0.5 * values * (1.0 - arch * arch) * (0.7978845608028654 * (1.0 + 3.0 * 0.044715 * cube))
    return 0.5 * values * (1.0 + arch), slope


TILE = 1024
BLOCK = 128


def up_kernel(mine_ref, other_ref, core_ref, x_ref, w_ref, b_ref, act_ref, slope_ref, own_ref, give_ref):
    activated, slope = gelu_parts(dot(x_ref[...], w_ref[...]) + b_ref[...])
    activated = activated.astype(BF16)
    act_ref[...] = activated
    slope_ref[...] = slope.astype(BF16)
    second = core_ref[0] == 1
    pairs = TILE // 2 // BLOCK
    for pair in range(pairs):
        low = activated[:, 2 * pair * BLOCK : (2 * pair + 1) * BLOCK]
        high = activated[:, (2 * pair + 1) * BLOCK : (2 * pair + 2) * BLOCK]
        index = pl.program_id(0) * pairs + pair
        own_ref[:, pl.ds(pl.multiple_of(mine_ref[index] * BLOCK, BLOCK), BLOCK)] = jnp.where(second, high, low)
        give_ref[:, pl.ds(pl.multiple_of(other_ref[index] * BLOCK, BLOCK), BLOCK)] = jnp.where(second, low, high)


def up_product(normed, weight, bias, mine, other, core):
    tokens, width = normed.shape
    columns = weight.shape[1]
    tall = pl.BlockSpec((tokens, TILE), lambda i, *_: (0, i))
    whole = pl.BlockSpec((tokens, columns // 2), lambda i, *_: (0, 0))
    return pl.pallas_call(
        up_kernel,
        grid_spec=pltpu.PrefetchScalarGridSpec(
            num_scalar_prefetch=3,
            grid=(columns // TILE,),
            in_specs=[
                pl.BlockSpec((tokens, width), lambda i, *_: (0, 0)),
                pl.BlockSpec((width, TILE), lambda i, *_: (0, i)),
                pl.BlockSpec((1, TILE), lambda i, *_: (0, i)),
            ],
            out_specs=[tall, tall, whole, whole],
        ),
        out_shape=[jax.ShapeDtypeStruct((tokens, n), BF16) for n in (columns, columns, columns // 2, columns // 2)],
        compiler_params=VMEM,
        cost_estimate=pl.CostEstimate(flops=2 * tokens * width * columns, bytes_accessed=2 * (width * columns + 3 * tokens * columns), transcendentals=tokens * columns),
    )(mine, other, core, normed, weight, bias)


PIECES = 4


def inner_kernel(g_ref, w_ref, slope_ref, low_ref, sum_ref, *piece_refs):
    grad_inner = against(g_ref[...], w_ref[...]) * slope_ref[...].astype(F32)
    low = grad_inner.astype(BF16)
    low_ref[...] = low
    sum_ref[...] = jnp.sum(grad_inner, axis=0, keepdims=True)
    for number, ref in enumerate(piece_refs):

        @pl.when(pl.program_id(0) == number)
        def _():
            ref[...] = low


def inner_back(grad_low, weight, slope):
    tokens, width = grad_low.shape
    columns = weight.shape[0]
    tile = columns // PIECES
    tall = pl.BlockSpec((tokens, tile), lambda i: (0, i))
    low, summed, *pieces = pl.pallas_call(
        inner_kernel,
        grid=(PIECES,),
        in_specs=[
            pl.BlockSpec((tokens, width), lambda i: (0, 0)),
            pl.BlockSpec((tile, width), lambda i: (i, 0)),
            tall,
        ],
        out_specs=[tall, pl.BlockSpec((1, tile), lambda i: (0, i))] + [pl.BlockSpec((tokens, tile), lambda i: (0, 0))] * PIECES,
        out_shape=[jax.ShapeDtypeStruct((tokens, columns), BF16), jax.ShapeDtypeStruct((1, columns), F32)]
        + [jax.ShapeDtypeStruct((tokens, columns // PIECES), BF16)] * PIECES,
        compiler_params=VMEM,
        cost_estimate=pl.CostEstimate(flops=2 * tokens * width * columns, bytes_accessed=2 * (width * columns + 2 * tokens * columns), transcendentals=0),
    )(grad_low, weight, slope)
    return low, summed, pieces


def tall_kernel(x_ref, xs_ref, g_ref, gs_ref, give_ref, keep_ref):
    summed = (contract(x_ref[...], g_ref[...]) + contract(xs_ref[...], gs_ref[...])).astype(BF16)
    for number, ref in enumerate((give_ref, keep_ref)):

        @pl.when(pl.program_id(0) // 2 == number)
        def _():
            ref[...] = summed


def tall_product(x, x_other, g, g_other):
    tokens, rows = x.shape
    columns = g.shape[1]
    tile = rows // 4
    x_spec = pl.BlockSpec((tokens, tile), lambda i: (0, i))
    g_spec = pl.BlockSpec((tokens, columns), lambda i: (0, 0))
    out = lambda least: pl.BlockSpec((tile, columns), lambda i: (jnp.clip(i - least, 0, 1), 0))
    return pl.pallas_call(
        tall_kernel,
        grid=(4,),
        in_specs=[x_spec, x_spec, g_spec, g_spec],
        out_specs=[out(0), out(2)],
        out_shape=[jax.ShapeDtypeStruct((rows // 2, columns), BF16)] * 2,
        compiler_params=VMEM,
        cost_estimate=pl.CostEstimate(flops=4 * tokens * rows * columns, bytes_accessed=4 * tokens * (rows + columns) + 2 * rows * columns, transcendentals=0),
    )(x, x_other, g, g_other)


def wide_kernel(counts, *refs):
    sources, (give_ref, keep_ref) = refs[:-2], refs[-2:]
    half = give_ref.shape[0]
    at = 0
    for count, pieces in counts:
        (x_ref, xs_ref, g_ref), gs_refs = sources[:3], sources[3 : 3 + pieces]
        sources = sources[3 + pieces :]
        for number, gs_ref in enumerate(gs_refs):
            least = at + number * (count // pieces)

            @pl.when((pl.program_id(0) >= least) & (pl.program_id(0) < least + count // pieces))
            def _():
                summed = contract(x_ref[...], g_ref[...]) + contract(xs_ref[...], gs_ref[...])
                give_ref[...] = summed[:half].astype(BF16)
                keep_ref[...] = summed[half:].astype(BF16)

        at += count


def wide_product(*groups):
    tokens, rows = groups[0][0].shape
    tile = 1024
    counts, in_specs, values, at, columns = [], [], [], 0, 0
    for x, xs, g, pieces in groups:
        count = g.shape[1] // tile
        part = count // len(pieces)
        counts.append((count, len(pieces)))
        x_spec = pl.BlockSpec((tokens, rows), lambda i: (0, 0))
        g_spec = lambda start, size: pl.BlockSpec((tokens, tile), lambda i: (0, jnp.clip(i - start, 0, size - 1)))
        in_specs += [x_spec, x_spec, g_spec(at, count)] + [g_spec(at + number * part, part) for number in range(len(pieces))]
        values += [x, xs, g, *pieces]
        at += count
        columns += g.shape[1]
    return pl.pallas_call(
        functools.partial(wide_kernel, counts),
        grid=(at,),
        in_specs=in_specs,
        out_specs=[pl.BlockSpec((rows // 2, tile), lambda i: (0, i))] * 2,
        out_shape=[jax.ShapeDtypeStruct((rows // 2, columns), BF16)] * 2,
        compiler_params=VMEM,
        cost_estimate=pl.CostEstimate(flops=4 * tokens * rows * columns, bytes_accessed=4 * tokens * (rows + columns) + 2 * rows * columns, transcendentals=0),
    )(*values)


def last_kernel(x_ref, xs_ref, g_ref, gs_ref, extra_ref, give_ref, keep_ref):
    summed = (contract(x_ref[...], g_ref[...]) + contract(xs_ref[...], gs_ref[...])).astype(BF16)
    blocks, lines, width = extra_ref.shape
    part = summed.shape[0] // blocks
    for number, ref in enumerate((give_ref, keep_ref)):

        @pl.when(pl.program_id(0) // 2 == number)
        def _():
            ref[:, :part] = summed.reshape(blocks, part, width)
            ref[:, part:] = extra_ref[...]


def last_product(x, x_other, g, g_other, extra):
    tokens, rows = x.shape
    blocks, lines, width = extra.shape
    part = rows // blocks
    quarter = blocks // 4
    x_spec = pl.BlockSpec((tokens, rows // 4), lambda i: (0, i))
    g_spec = pl.BlockSpec((tokens, width), lambda i: (0, 0))
    out = lambda least: pl.BlockSpec((quarter, part + lines, width), lambda i: (jnp.clip(i - least, 0, 1), 0, 0))
    give, keep = pl.pallas_call(
        last_kernel,
        grid=(4,),
        in_specs=[x_spec, x_spec, g_spec, g_spec, pl.BlockSpec((quarter, lines, width), lambda i: (i, 0, 0))],
        out_specs=[out(0), out(2)],
        out_shape=[jax.ShapeDtypeStruct((blocks // 2, part + lines, width), BF16)] * 2,
        compiler_params=VMEM,
        cost_estimate=pl.CostEstimate(flops=4 * tokens * rows * width, bytes_accessed=4 * tokens * (rows + width) + 2 * rows * width, transcendentals=0),
    )(x, x_other, g, g_other, extra)
    flat = (blocks // 2 * (part + lines), width)
    return give.reshape(flat), keep.reshape(flat)


def norm_back(grad_normed, unit, scale, gain):
    scaled = grad_normed * gain
    return scale * (scaled - unit * jnp.mean(scaled * unit, axis=1, keepdims=True))


def pairs_of(move):
    pairs = []
    for z in range(4):
        for y in range(2):
            for x in range(2):
                for c in range(2):
                    there = move(z, y, x, c)
                    if there is not None:
                        source = ((z * 2 + y) * 2 + x) * 2 + c
                        target = ((there[0] * 2 + there[1]) * 2 + there[2]) * 2 + there[3]
                        pairs.append((source, target))
    return pairs


OTHER_CORE = pairs_of(lambda z, y, x, c: (z, y, x, 1 - c))
FIRST = pairs_of(lambda z, y, x, c: (z, 1 - y, x, c) if c == 0 else (z, y, 1 - x, c))
SECOND = pairs_of(lambda z, y, x, c: (z, y, 1 - x, c) if c == 0 else (z, 1 - y, x, c))
FAR = pairs_of(lambda z, y, x, c: (z ^ 2, y, x, c))
NEAR = pairs_of(lambda z, y, x, c: (z ^ 1, y, x, c))
PLANE_FIRST = (FIRST, SECOND, FAR, NEAR)
PLANE_LAST = (FIRST, FAR, NEAR, SECOND)


def send(values, pairs):
    return lax.ppermute(values, CORES, pairs)


def block_order(place, steps, core):
    z, y, x = place
    index = jnp.arange(16)
    flip = {}
    for level, pairs in enumerate(steps):
        flip[id(pairs)] = 1 - index // (8 >> level) % 2
    at_z = z ^ (2 * flip[id(FAR)]) ^ flip[id(NEAR)]
    first, second = flip[id(FIRST)], flip[id(SECOND)]
    at_y = y ^ jnp.where(core == 0, first, second)
    at_x = x ^ jnp.where(core == 0, second, first)
    return ((at_z * 2 + at_y) * 2 + at_x) * 2 + core


def both_orders(place, core, steps):
    return jnp.concatenate([block_order(place, steps, 1 - core), block_order(place, steps, core)])


def plus(left, right, kind=BF16):
    return (left.astype(F32) + right.astype(F32)).astype(kind)


class Gathering:
    def __init__(self, block, steps):
        self.kept = block
        self.steps = list(steps[::-1])

    def step(self, before=(), wait=()):
        pairs = self.steps.pop(0)
        got = after(send(after(self.kept, *before), pairs), *wait)
        if self.steps:
            self.kept = jnp.concatenate([got, self.kept])
        else:
            self.kept = (got, self.kept)
            self.kept += tuple(send(half, OTHER_CORE) for half in self.kept)
        return self.kept


def place_kernel(cuts, order_ref, *refs):
    parts, outs, sems = refs[:4], refs[4:-1], refs[-1]
    block = parts[0].shape[0] // 8
    copies = []
    for index in range(32):
        part = parts[(2 + index // 8) % 4]
        for number, (row, rows, column, columns) in enumerate(cuts):
            target = outs[number].at[pl.ds(pl.multiple_of(order_ref[index] * rows, rows), rows)]
            source = part.at[pl.ds(index % 8 * block + row, rows), pl.ds(column, columns)]
            copies.append(pltpu.make_async_copy(source, target, sems.at[number * 32 + index]))
            copies[-1].start()
    for copy in copies:
        copy.wait()


def placed(parts, order, cuts):
    rows, columns = parts[0].shape
    return pl.pallas_call(
        functools.partial(place_kernel, cuts),
        grid_spec=pltpu.PrefetchScalarGridSpec(
            num_scalar_prefetch=1,
            grid=(1,),
            in_specs=[pl.BlockSpec((rows, columns), lambda i, order: (0, 0))] * 4,
            out_specs=[pl.BlockSpec(memory_space=pl.ANY)] * len(cuts),
            scratch_shapes=[pltpu.SemaphoreType.DMA((32 * len(cuts),))],
        ),
        out_shape=[jax.ShapeDtypeStruct((32 * cut[1], cut[3]), parts[0].dtype) for cut in cuts],
        compiler_params=VMEM,
        cost_estimate=pl.CostEstimate(flops=0, bytes_accessed=16 * rows * columns, transcendentals=0),
    )(order, *parts)


def after(value, *others):
    return lax.optimization_barrier((value,) + others)[0] if others else value


class Summing:
    def __init__(self, halves, steps):
        self.give, self.kept = halves
        self.steps = list(steps)

    def step(self, *wait, before=()):
        got = after(send(after(self.give, *before), self.steps.pop(0)), *wait)
        return self.add(got)

    def add(self, got):
        if self.steps:
            half = self.kept.shape[0] // 2
            self.give = plus(self.kept[:half], got[:half])
            self.kept = plus(self.kept[half:], got[half:])
            return self.give
        self.kept = plus(self.kept, got, F32)
        return self.kept

    def send_part(self, *wait):
        half = self.give.shape[0] // 2
        got = after(send(self.give[:half], self.steps[0]), *wait)
        self.later = self.give[half:]
        self.give = plus(self.kept[:half], got)
        return self.give

    def keep_part(self, *wait):
        got = after(send(after(self.later, self.give), self.steps.pop(0)), *wait)
        self.kept = plus(self.kept[self.later.shape[0] :], got)
        return self.kept

    def finish(self):
        while self.steps:
            self.step()
        return self.kept


def picked(values, order):
    columns = values.shape[1]
    block = columns // 32
    column = jnp.arange(columns)
    source = jnp.repeat(order, block) * block + column % block
    choice = (column[:, None] == source[None, :]).astype(BF16)
    return dot(values, choice, BF16)


def swapped(values):
    return send(values, OTHER_CORE)


def halves(values):
    half = values.shape[1] // 2
    return values[:, :half], values[:, half:]


def on_device(
    known,
    frames,
    skip,
    cotangent,
    segment_ids,
    row_lengths,
    w_skip,
    b_skip,
    gain_one,
    w_qkv,
    w_out,
    gain_two,
    w_up,
    b_up,
    w_down,
    b_down,
):
    micro, rows, length, width = frames.shape
    count = micro * rows
    tokens = count * length
    devices = width // gain_one.shape[0]
    hidden_width = w_up.shape[1]

    vectors = jnp.concatenate([b_skip, gain_one, gain_two, b_down, b_up])
    part = w_skip.shape[0]
    lines = -(-vectors.shape[0] // width)
    lines = -(-lines // 16) * 16
    padded = jnp.pad(vectors, (0, lines * width - vectors.shape[0])).reshape(lines, width)
    own_skip = jnp.concatenate([w_skip, padded])
    own_qkv = jnp.concatenate([w_qkv, w_out], axis=1)
    if known:
        place = lax.axis_index("dp")
        core = lax.axis_index("core")
        coords = (place // 2, place % 2, lax.axis_index("x"))
        order = both_orders(coords, core, PLANE_FIRST)
        joined = jnp.concatenate([frames.reshape(tokens, width), skip.reshape(tokens, width)], axis=1)
        give_joined, own_joined = halves(picked(joined, order))
        all_up = lax.all_gather(w_up, CORES, axis=0, tiled=True)
        all_down = lax.all_gather(w_down, CORES, axis=0, tiled=True)
        at_skip, at_qkv = (Gathering(own, PLANE_FIRST) for own in (own_skip, own_qkv))
        at_skip.step()
        near = at_qkv.step()
        joined_other, grad_other = swapped(give_joined), swapped(cotangent.reshape(tokens, width))
        far = at_skip.step(before=(near,), wait=(own_joined, joined_other, grad_other))
        at_skip.step()
        got_skip = at_skip.step()
        far = at_qkv.step(before=(far,))
        at_skip.kept = got_skip[:2] + tuple(send(after(half, far), OTHER_CORE) for half in got_skip[:2])
        got_skip = at_skip.kept
        full_skip, flat = placed(got_skip, order, ((0, part, 0, width), (part, lines, 0, width)))
        at_qkv.step()
    else:
        all_skip = lax.all_gather(own_skip, AXES, axis=0, tiled=False)
        all_qkv = lax.all_gather(own_qkv, AXES, axis=0, tiled=True)
        all_up = lax.all_gather(w_up, AXES, axis=0, tiled=True)
        all_down = lax.all_gather(w_down, AXES, axis=0, tiled=True)
        full_skip = all_skip[:, :part].reshape(devices * part, width)
        flat = all_skip[:, part:]
        full_qkv = all_qkv[:, : 3 * width]
        full_out = all_qkv[:, 3 * width :]
        joined = jnp.concatenate([frames.reshape(tokens, width), skip.reshape(tokens, width)], axis=1)
    flat = flat.reshape(devices, lines * width)
    small = width // devices
    spread = lambda at, size: flat[:, at : at + size].reshape(1, devices * size).astype(F32)
    bias_skip, gain_1, gain_2, bias_down = (spread(i * small, small) for i in range(4))
    bias_up = spread(4 * small, hidden_width // devices)

    grad_low = cotangent.reshape(tokens, width)
    grad_out = grad_low.astype(F32)
    segments = segment_ids.reshape(count, length)
    lengths = row_lengths.reshape(count, 1)
    reach = jnp.where(jnp.arange(length)[None, :] < lengths, segments, -1)
    column, row = reach[:, :, None], segments[:, None, :]
    tables = wide_tables(length)

    hidden = dot(joined, full_skip) + bias_skip
    scale_one = lax.rsqrt(jnp.mean(hidden * hidden, axis=1, keepdims=True) + EPSILON)
    unit_one = hidden * scale_one
    normed_one = (unit_one * gain_1).astype(BF16)
    if known:
        give_one, own_one = halves(picked(normed_one, order))
        got_qkv = at_qkv.step(wait=(own_one,))
        full_qkv, full_out = placed(got_qkv, order, ((0, w_qkv.shape[0], 0, 3 * width), (0, w_qkv.shape[0], 3 * width, width)))
    mixed = dot(normed_one, full_qkv)
    query, key, value, attended, lse = attend(mixed, tables, column, row, count, length)
    middle = hidden + dot(attended, full_out)
    scale_two = lax.rsqrt(jnp.mean(middle * middle, axis=1, keepdims=True) + EPSILON)
    unit_two = middle * scale_two
    normed_two = (unit_two * gain_2).astype(BF16)
    total = lambda values: jnp.sum(values, axis=0)
    back = functools.partial(attend_back, query, key, value, lse=lse, tables=tables, column=column, row=row, rows=count, length=length)

    if known:
        ends = lambda blocks: jnp.sum(jnp.where(blocks[None, :] // 2 == jnp.arange(16)[:, None], jnp.arange(16)[None, :], 0), axis=1).astype(jnp.int32)
        give_attended, own_attended = halves(picked(attended, order))
        give_two, own_two = halves(picked(normed_two, order))
        one_other, attended_other, two_other = swapped(give_one), swapped(give_attended), swapped(give_two)

        activated, slope, own_active, give_active = up_product(
            normed_two, all_up, bias_up, ends(order[16:]), ends(order[:16]), core.reshape(1)
        )
        active_other = swapped(give_active)
        down = Summing(tall_product(own_active, active_other, grad_low, grad_other), PLANE_FIRST)
        inner_low, inner_sum, inner_pieces = inner_back(grad_low, after(all_down, down.give), slope)
        inner_other = [swapped(piece) for piece in inner_pieces]
        grad_normed_two = against(inner_low, all_up)
        up = Summing(wide_product((own_two, two_other, after(inner_low, grad_normed_two), inner_other)), PLANE_FIRST)
        down.step(up.give)
        grad_middle = grad_out + norm_back(after(grad_normed_two, down.give), unit_two, scale_two, gain_2)
        middle_low = grad_middle.astype(BF16)
        middle_other = swapped(middle_low)
        grad_attended = against(middle_low, full_out).astype(BF16)
        grad_mixed, *mixed_pieces = back(grad=after(grad_attended, down.give))
        mixed_other = [swapped(piece) for piece in mixed_pieces]
        down.step(grad_mixed)
        up.step(grad_mixed)
        both = Summing(
            wide_product(
                (own_one, one_other, after(grad_mixed, up.give, down.give), mixed_other),
                (own_attended, attended_other, middle_low, [middle_other]),
            ),
            PLANE_FIRST,
        )
        up.step(both.give)
        given = down.send_part(both.give)
        grad_normed_one = against(after(grad_mixed, both.give, up.give, given), full_qkv)
        both.send_part(grad_normed_one)
        down_kept = down.keep_part(grad_normed_one)
        grad_hidden = grad_middle + norm_back(after(grad_normed_one, both.give, down_kept), unit_one, scale_one, gain_1)
        hidden_low = grad_hidden.astype(BF16)
        hidden_other = swapped(hidden_low)
        vector_grads = (total(grad_hidden), total(grad_normed_one * unit_one), total(grad_normed_two * unit_two), total(grad_out), inner_sum[0])
        by_block = jnp.concatenate([v.reshape(devices, -1) for v in vector_grads], axis=1)
        by_block = by_block + swapped(by_block)
        choice = (order[16:, None] == jnp.arange(devices)[None, :]).astype(F32)
        by_block = jnp.dot(choice, by_block, precision=lax.Precision.HIGHEST).astype(BF16)
        by_block = jnp.pad(by_block, ((0, 0), (0, lines * width - by_block.shape[1]))).reshape(16, lines, width)
        tail = Summing(last_product(own_joined, joined_other, after(hidden_low, both.give), hidden_other, by_block), PLANE_FIRST)
        both_kept = both.keep_part(tail.give)
        down_grad = down.step(tail.give)
        grad_joined = against(after(hidden_low, both_kept, down_grad), full_skip)
        both.step(grad_joined)
        tail.step(both.give)
        up.step(both.give)
        both.send_part(tail.give)
        tail.step()
        up_grad = up.step(tail.give)
        output = (middle + (dot(after(activated, tail.give), all_down) + bias_down)).astype(BF16)
        both.keep_part(output)
        tail.step(output)
        both_grad = both.finish()
        last = tail.finish()
        qkv_grad, out_grad = both_grad[:, : 3 * width], both_grad[:, 3 * width :]
        skip_weight_grad = last[:part]
        line = last[part:].reshape(lines * width)
        shares = [line[i * small : (i + 1) * small] for i in range(4)]
        shares.append(line[4 * small : 4 * small + hidden_width // devices])
    else:
        activated, slope = gelu_parts(dot(normed_two, all_up) + bias_up)
        activated = activated.astype(BF16)
        output = (middle + (dot(activated, all_down) + bias_down)).astype(BF16)
        grad_inner = against(grad_low, all_down) * slope
        inner_low = grad_inner.astype(BF16)
        grad_normed_two = against(inner_low, all_up)
        grad_middle = grad_out + norm_back(grad_normed_two, unit_two, scale_two, gain_2)
        middle_low = grad_middle.astype(BF16)
        grad_mixed = back(grad=against(middle_low, full_out).astype(BF16))[0]
        grad_normed_one = against(grad_mixed, full_qkv)
        grad_hidden = grad_middle + norm_back(grad_normed_one, unit_one, scale_one, gain_1)
        hidden_low = grad_hidden.astype(BF16)
        grad_joined = against(hidden_low, full_skip)
        vector_grads = (total(grad_hidden), total(grad_normed_one * unit_one), total(grad_normed_two * unit_two), total(grad_out), total(grad_inner))
        scatter = lambda values: lax.psum_scatter(values, AXES, scatter_dimension=0, tiled=True)
        down_grad = scatter(contract(activated, grad_low))
        up_grad = scatter(contract(normed_two, inner_low))
        out_grad = scatter(contract(attended, middle_low))
        qkv_grad = scatter(contract(normed_one, grad_mixed))
        skip_weight_grad = scatter(contract(joined, hidden_low))
        shares = [scatter(v) for v in vector_grads]

    shape = (micro, rows, length, width)
    return (
        output.reshape(shape),
        grad_joined[:, :width].reshape(shape),
        grad_joined[:, width:].reshape(shape),
        skip_weight_grad,
        shares[0],
        shares[1],
        qkv_grad,
        out_grad,
        shares[2],
        up_grad,
        shares[4],
        down_grad,
        shares[3],
    )


def solution(mesh):
    known = mesh.shape["dp"] == 8 and mesh.shape["fsdp"] == 4
    axes = AXES
    if known:
        mesh = Mesh(mesh.devices.reshape(8, 2, 2), CORES)
        axes = CORES
    tokens = P(None, axes, None, None)
    weight = P(axes, None)
    vector = P(axes)
    return jax.shard_map(
        functools.partial(on_device, known),
        mesh=mesh,
        in_specs=(
            tokens,
            tokens,
            tokens,
            P(None, axes, None),
            P(None, axes),
            weight,
            vector,
            vector,
            weight,
            weight,
            vector,
            weight,
            vector,
            weight,
            vector,
        ),
        out_specs=(
            tokens,
            tokens,
            tokens,
            weight,
            vector,
            vector,
            weight,
            weight,
            vector,
            weight,
            vector,
            weight,
            vector,
        ),
        check_vma=False,
    )
```

```python
import functools
import math

import jax
import jax.numpy as jnp
from jax import lax
from jax.experimental import pallas as pl
from jax.experimental.pallas import tpu as pltpu
from jax.sharding import Mesh, PartitionSpec as P

HEADS = 16
HEAD = 64
EPSILON = 1e-06
AXES = ("dp", "fsdp")
CHIPS = ("dp", "x")
CORES = CHIPS + ("core",)
F32 = jnp.float32
BF16 = jnp.bfloat16
VMEM = pltpu.CompilerParams(vmem_limit_bytes=48 << 20)


def dot(left, right, kind=F32):
    return jnp.dot(left, right, preferred_element_type=F32).astype(kind)


def against(left, right):
    return lax.dot_general(left, right, (((1,), (1,)), ((), ())), preferred_element_type=F32)


def contract(left, right):
    return lax.dot_general(left, right, (((0,), (0,)), ((), ())), preferred_element_type=F32)


def wide_tables(length):
    half = HEAD // 2
    indices = jnp.arange(half, dtype=F32)
    freqs = jnp.exp(indices * (-2.0 * math.log(10000.0) / HEAD))
    angles = jnp.arange(length, dtype=F32)[:, None] * freqs[None, :]
    cosine, sine = jnp.cos(angles), jnp.sin(angles)
    return (
        jnp.concatenate([cosine] * 4, axis=1),
        jnp.concatenate([-sine, sine, -sine, sine], axis=1),
    )


def swap_halves(values):
    half = HEAD // 2
    lane = lax.broadcasted_iota(jnp.int32, values.shape, 1)
    ahead = pltpu.roll(values, 2 * HEAD - half, 1)
    behind = pltpu.roll(values, half, 1)
    return jnp.where(lax.rem(lane, HEAD) < half, ahead, behind)


def allowed_of(column_ref, row_ref):
    length = row_ref.shape[-1]
    rows = lax.broadcasted_iota(jnp.int32, (length, length), 0)
    columns = lax.broadcasted_iota(jnp.int32, (length, length), 1)
    return (column_ref[0] == row_ref[0]) | (rows == columns)


def head_part(values, which):
    lane = lax.broadcasted_iota(jnp.int32, values.shape, 1)
    return jnp.where((lane >= HEAD) == (which == 1), values, jnp.zeros_like(values))


WIDE = 2 * HEAD
GROUP = 8


def attend_kernel(q_ref, k_ref, v_ref, cos_ref, sin_ref, column_ref, row_ref, qo_ref, ko_ref, vo_ref, a_ref, lse_ref):
    cosine, sine = cos_ref[...], sin_ref[...]
    allowed = allowed_of(column_ref, row_ref)
    for pair in range(GROUP):
        lanes = slice(pair * WIDE, (pair + 1) * WIDE)
        raw_q, raw_k = q_ref[:, lanes], k_ref[:, lanes]
        query = ((raw_q * cosine + swap_halves(raw_q) * sine)).astype(BF16)
        key = (raw_k * cosine + swap_halves(raw_k) * sine).astype(BF16)
        value = v_ref[:, lanes].astype(BF16)
        scaled = query * jnp.asarray(HEAD ** (-0.5), BF16)
        qo_ref[:, lanes] = query
        ko_ref[:, lanes] = key
        vo_ref[:, lanes] = value
        total = jnp.zeros(value.shape[::-1], F32)
        for which in range(2):
            masked = jnp.where(allowed, against(key, head_part(scaled, which)), -1e30)
            highest = jnp.max(masked, axis=0, keepdims=True)
            exponent = jnp.exp(masked - highest)
            summed = jnp.sum(exponent, axis=0, keepdims=True)
            probs = (exponent * (1.0 / summed)).astype(BF16)
            total += contract(head_part(value, which), probs)
            lse_ref[0, 0, pl.ds(2 * pair + which, 1), :] = highest + jnp.log(summed)
        a_ref[:, lanes] = total.T.astype(BF16)


def attend(mixed, tables, column, row, rows, length):
    width = HEADS * HEAD
    steps = HEADS // 2 // GROUP
    wide = WIDE * GROUP
    place = lambda shift: pl.BlockSpec((length, wide), lambda r, p, s=shift: (r, p + s))
    table = pl.BlockSpec((length, WIDE), lambda r, p: (0, 0))
    narrow = jax.ShapeDtypeStruct((rows * length, width), BF16)
    return pl.pallas_call(
        attend_kernel,
        grid=(rows, steps),
        in_specs=[
            place(0),
            place(steps),
            place(2 * steps),
            table,
            table,
            pl.BlockSpec((1, length, 1), lambda r, p: (r, 0, 0)),
            pl.BlockSpec((1, 1, length), lambda r, p: (r, 0, 0)),
        ],
        out_specs=[place(0)] * 4 + [pl.BlockSpec((1, 1, 2 * GROUP, length), lambda r, p: (r, p, 0, 0))],
        out_shape=[narrow] * 4 + [jax.ShapeDtypeStruct((rows, steps, 2 * GROUP, length), F32)],
        compiler_params=VMEM,
        cost_estimate=pl.CostEstimate(flops=rows * HEADS * length * length * 512, bytes_accessed=rows * length * width * 24, transcendentals=rows * HEADS * length * length),
    )(mixed, mixed, mixed, *tables, column, row)


def attend_back_kernel(q_ref, k_ref, v_ref, g_ref, lse_ref, cos_ref, sin_ref, column_ref, row_ref, out_ref, *piece_refs):
    cosine, sine = cos_ref[...], sin_ref[...]
    allowed = allowed_of(column_ref, row_ref)
    scale = HEAD ** (-0.5)
    for pair in range(GROUP):
        lanes = slice(pair * WIDE, (pair + 1) * WIDE)
        query, key, value, grad = q_ref[:, lanes], k_ref[:, lanes], v_ref[:, lanes], g_ref[:, lanes]
        scaled = query * jnp.asarray(scale, BF16)
        grad_q = jnp.zeros(query.shape[::-1], F32)
        grad_k = jnp.zeros(query.shape, F32)
        grad_v = jnp.zeros(query.shape, F32)
        for which in range(2):
            own_query = head_part(scaled, which)
            own_grad = head_part(grad, which)
            mark = lse_ref[0, 0, pl.ds(2 * pair + which, 1), :]
            probs = jnp.exp(jnp.where(allowed, against(key, own_query), -1e30) - mark)
            grad_probs = against(value, own_grad)
            inside = jnp.sum(grad_probs * probs, axis=0, keepdims=True)
            grad_scores = (probs * (grad_probs - inside)).astype(BF16)
            grad_v += dot(probs.astype(BF16), own_grad)
            grad_k += dot(grad_scores, own_query)
            grad_q += contract(head_part(key, which), grad_scores)
        grad_q = grad_q.T * scale
        width = HEADS * HEAD
        start = pl.program_id(1) * (GROUP * WIDE) + pair * WIDE
        target = lambda part: pl.ds(pl.multiple_of(part * width + start, WIDE), WIDE)
        grad_q = grad_q * cosine - swap_halves(grad_q) * sine
        grad_k = grad_k * cosine - swap_halves(grad_k) * sine
        for part, values in enumerate((grad_q, grad_k, grad_v)):
            out_ref[:, target(part)] = values.astype(BF16)
            piece_refs[part][:, lanes] = values.astype(BF16)


def attend_back(query, key, value, grad, lse, tables, column, row, rows, length):
    width = HEADS * HEAD
    steps = HEADS // 2 // GROUP
    place = pl.BlockSpec((length, WIDE * GROUP), lambda r, p: (r, p))
    table = pl.BlockSpec((length, WIDE), lambda r, p: (0, 0))
    return pl.pallas_call(
        attend_back_kernel,
        grid=(rows, steps),
        in_specs=[place] * 4
        + [
            pl.BlockSpec((1, 1, 2 * GROUP, length), lambda r, p: (r, p, 0, 0)),
            table,
            table,
            pl.BlockSpec((1, length, 1), lambda r, p: (r, 0, 0)),
            pl.BlockSpec((1, 1, length), lambda r, p: (r, 0, 0)),
        ],
        out_specs=[pl.BlockSpec((length, 3 * width), lambda r, p: (r, 0))] + [place] * 3,
        out_shape=[jax.ShapeDtypeStruct((rows * length, 3 * width), BF16)] + [jax.ShapeDtypeStruct((rows * length, width), BF16)] * 3,
        compiler_params=VMEM,
        cost_estimate=pl.CostEstimate(flops=rows * HEADS * length * length * 1280, bytes_accessed=rows * length * width * 14, transcendentals=rows * HEADS * length * length),
    )(query, key, value, grad, lse, *tables, column, row)


def gelu_parts(values):
    cube = values * values
    arch = jnp.tanh(0.7978845608028654 * (values + 0.044715 * values * cube))
    slope = 0.5 * (1.0 + arch) + 0.5 * values * (1.0 - arch * arch) * (0.7978845608028654 * (1.0 + 3.0 * 0.044715 * cube))
    return 0.5 * values * (1.0 + arch), slope


TILE = 1024
BLOCK = 128


def up_kernel(mine_ref, other_ref, core_ref, x_ref, w_ref, b_ref, act_ref, slope_ref, own_ref, *give_refs):
    activated, slope = gelu_parts(dot(x_ref[...], w_ref[...]) + b_ref[...])
    activated = activated.astype(BF16)
    act_ref[...] = activated
    slope_ref[...] = slope.astype(BF16)
    second = core_ref[0] == 1
    pairs = TILE // 2 // BLOCK
    for pair in range(pairs):
        low = activated[:, 2 * pair * BLOCK : (2 * pair + 1) * BLOCK]
        high = activated[:, (2 * pair + 1) * BLOCK : (2 * pair + 2) * BLOCK]
        index = pl.program_id(0) * pairs + pair
        own_ref[:, pl.ds(pl.multiple_of(mine_ref[index] * BLOCK, BLOCK), BLOCK)] = jnp.where(second, high, low)
        place = other_ref[index]
        each = give_refs[0].shape[1] // BLOCK
        for number, ref in enumerate(give_refs):

            @pl.when(place // each == number)
            def _():
                ref[:, pl.ds(pl.multiple_of((place - number * each) * BLOCK, BLOCK), BLOCK)] = jnp.where(second, low, high)


def up_product(normed, weight, bias, mine, other, core):
    tokens, width = normed.shape
    columns = weight.shape[1]
    tall = pl.BlockSpec((tokens, TILE), lambda i, *_: (0, i))
    whole = lambda part: pl.BlockSpec((tokens, columns // part), lambda i, *_: (0, 0))
    return pl.pallas_call(
        up_kernel,
        grid_spec=pltpu.PrefetchScalarGridSpec(
            num_scalar_prefetch=3,
            grid=(columns // TILE,),
            in_specs=[
                pl.BlockSpec((tokens, width), lambda i, *_: (0, 0)),
                pl.BlockSpec((width, TILE), lambda i, *_: (0, i)),
                pl.BlockSpec((1, TILE), lambda i, *_: (0, i)),
            ],
            out_specs=[tall, tall, whole(2), whole(4), whole(4)],
        ),
        out_shape=[jax.ShapeDtypeStruct((tokens, n), BF16) for n in (columns, columns, columns // 2, columns // 4, columns // 4)],
        compiler_params=VMEM,
        cost_estimate=pl.CostEstimate(flops=2 * tokens * width * columns, bytes_accessed=2 * (width * columns + 3 * tokens * columns), transcendentals=tokens * columns),
    )(mine, other, core, normed, weight, bias)


PIECES = 4


def inner_kernel(g_ref, w_ref, slope_ref, low_ref, sum_ref, *piece_refs):
    grad_inner = against(g_ref[...], w_ref[...]) * slope_ref[...].astype(F32)
    low = grad_inner.astype(BF16)
    low_ref[...] = low
    sum_ref[...] = jnp.sum(grad_inner, axis=0, keepdims=True)
    for number, ref in enumerate(piece_refs):

        @pl.when(pl.program_id(0) == number)
        def _():
            ref[...] = low


def inner_back(grad_low, weight, slope):
    tokens, width = grad_low.shape
    columns = weight.shape[0]
    tile = columns // PIECES
    tall = pl.BlockSpec((tokens, tile), lambda i: (0, i))
    low, summed, *pieces = pl.pallas_call(
        inner_kernel,
        grid=(PIECES,),
        in_specs=[
            pl.BlockSpec((tokens, width), lambda i: (0, 0)),
            pl.BlockSpec((tile, width), lambda i: (i, 0)),
            tall,
        ],
        out_specs=[tall, pl.BlockSpec((1, tile), lambda i: (0, i))] + [pl.BlockSpec((tokens, tile), lambda i: (0, 0))] * PIECES,
        out_shape=[jax.ShapeDtypeStruct((tokens, columns), BF16), jax.ShapeDtypeStruct((1, columns), F32)]
        + [jax.ShapeDtypeStruct((tokens, columns // PIECES), BF16)] * PIECES,
        compiler_params=VMEM,
        cost_estimate=pl.CostEstimate(flops=2 * tokens * width * columns, bytes_accessed=2 * (width * columns + 2 * tokens * columns), transcendentals=0),
    )(grad_low, weight, slope)
    return low, summed, pieces


def tall_kernel(x_ref, xs_ref, g_ref, gs_ref, out_ref):
    out_ref[...] = (contract(x_ref[...], g_ref[...]) + contract(xs_ref[...], gs_ref[...])).astype(BF16)


def tall_product(x, x_other, g, g_other, part):
    tokens, rows = x_other.shape
    columns = g.shape[1]
    tile = rows // 2
    whole = pl.BlockSpec((tokens, columns), lambda i: (0, 0))
    return pl.pallas_call(
        tall_kernel,
        grid=(2,),
        in_specs=[pl.BlockSpec((tokens, tile), lambda i: (0, i + 2 * part)), pl.BlockSpec((tokens, tile), lambda i: (0, i)), whole, whole],
        out_specs=pl.BlockSpec((tile, columns), lambda i: (i, 0)),
        out_shape=jax.ShapeDtypeStruct((rows, columns), BF16),
        compiler_params=VMEM,
        cost_estimate=pl.CostEstimate(flops=4 * tokens * rows * columns, bytes_accessed=4 * tokens * (rows + columns) + 2 * rows * columns, transcendentals=0),
    )(x, x_other, g, g_other)


def wide_kernel(counts, *refs):
    sources, (give_ref, keep_ref) = refs[:-2], refs[-2:]
    half = give_ref.shape[0]
    at = 0
    for count, pieces in counts:
        (x_ref, xs_ref, g_ref), gs_refs = sources[:3], sources[3 : 3 + pieces]
        sources = sources[3 + pieces :]
        for number, gs_ref in enumerate(gs_refs):
            least = at + number * (count // pieces)

            @pl.when((pl.program_id(0) >= least) & (pl.program_id(0) < least + count // pieces))
            def _():
                summed = contract(x_ref[...], g_ref[...]) + contract(xs_ref[...], gs_ref[...])
                give_ref[...] = summed[:half].astype(BF16)
                keep_ref[...] = summed[half:].astype(BF16)

        at += count


def wide_product(*groups):
    tokens, rows = groups[0][0].shape
    tile = 1024
    counts, in_specs, values, at, columns = [], [], [], 0, 0
    for x, xs, g, pieces in groups:
        count = g.shape[1] // tile
        part = count // len(pieces)
        counts.append((count, len(pieces)))
        x_spec = pl.BlockSpec((tokens, rows), lambda i: (0, 0))
        g_spec = lambda start, size: pl.BlockSpec((tokens, tile), lambda i: (0, jnp.clip(i - start, 0, size - 1)))
        in_specs += [x_spec, x_spec, g_spec(at, count)] + [g_spec(at + number * part, part) for number in range(len(pieces))]
        values += [x, xs, g, *pieces]
        at += count
        columns += g.shape[1]
    return pl.pallas_call(
        functools.partial(wide_kernel, counts),
        grid=(at,),
        in_specs=in_specs,
        out_specs=[pl.BlockSpec((rows // 2, tile), lambda i: (0, i))] * 2,
        out_shape=[jax.ShapeDtypeStruct((rows // 2, columns), BF16)] * 2,
        compiler_params=VMEM,
        cost_estimate=pl.CostEstimate(flops=4 * tokens * rows * columns, bytes_accessed=4 * tokens * (rows + columns) + 2 * rows * columns, transcendentals=0),
    )(*values)


def last_kernel(x_ref, xs_ref, g_ref, gs_ref, extra_ref, give_ref, keep_ref):
    summed = (contract(x_ref[...], g_ref[...]) + contract(xs_ref[...], gs_ref[...])).astype(BF16)
    blocks, lines, width = extra_ref.shape
    part = summed.shape[0] // blocks
    for number, ref in enumerate((give_ref, keep_ref)):

        @pl.when(pl.program_id(0) // 2 == number)
        def _():
            ref[:, :part] = summed.reshape(blocks, part, width)
            ref[:, part:] = extra_ref[...]


def last_product(x, x_other, g, g_other, extra):
    tokens, rows = x.shape
    blocks, lines, width = extra.shape
    part = rows // blocks
    quarter = blocks // 4
    x_spec = pl.BlockSpec((tokens, rows // 4), lambda i: (0, i))
    g_spec = pl.BlockSpec((tokens, width), lambda i: (0, 0))
    out = lambda least: pl.BlockSpec((quarter, part + lines, width), lambda i: (jnp.clip(i - least, 0, 1), 0, 0))
    give, keep = pl.pallas_call(
        last_kernel,
        grid=(4,),
        in_specs=[x_spec, x_spec, g_spec, g_spec, pl.BlockSpec((quarter, lines, width), lambda i: (i, 0, 0))],
        out_specs=[out(0), out(2)],
        out_shape=[jax.ShapeDtypeStruct((blocks // 2, part + lines, width), BF16)] * 2,
        compiler_params=VMEM,
        cost_estimate=pl.CostEstimate(flops=4 * tokens * rows * width, bytes_accessed=4 * tokens * (rows + width) + 2 * rows * width, transcendentals=0),
    )(x, x_other, g, g_other, extra)
    flat = (blocks // 2 * (part + lines), width)
    return give.reshape(flat), keep.reshape(flat)


def norm_back(grad_normed, unit, scale, gain):
    scaled = grad_normed * gain
    return scale * (scaled - unit * jnp.mean(scaled * unit, axis=1, keepdims=True))


def pairs_of(move):
    pairs = []
    for z in range(4):
        for y in range(2):
            for x in range(2):
                for c in range(2):
                    there = move(z, y, x, c)
                    if there is not None:
                        source = ((z * 2 + y) * 2 + x) * 2 + c
                        target = ((there[0] * 2 + there[1]) * 2 + there[2]) * 2 + there[3]
                        pairs.append((source, target))
    return pairs


OTHER_CORE = pairs_of(lambda z, y, x, c: (z, y, x, 1 - c))
FIRST = pairs_of(lambda z, y, x, c: (z, 1 - y, x, c) if c == 0 else (z, y, 1 - x, c))
SECOND = pairs_of(lambda z, y, x, c: (z, y, 1 - x, c) if c == 0 else (z, 1 - y, x, c))
FAR = pairs_of(lambda z, y, x, c: (z ^ 2, y, x, c))
NEAR = pairs_of(lambda z, y, x, c: (z ^ 1, y, x, c))
PLANE_FIRST = (FIRST, SECOND, FAR, NEAR)
PLANE_LAST = (FIRST, FAR, NEAR, SECOND)


def send(values, pairs):
    return lax.ppermute(values, CORES, pairs)


def block_order(place, steps, core):
    z, y, x = place
    index = jnp.arange(16)
    flip = {}
    for level, pairs in enumerate(steps):
        flip[id(pairs)] = 1 - index // (8 >> level) % 2
    at_z = z ^ (2 * flip[id(FAR)]) ^ flip[id(NEAR)]
    first, second = flip[id(FIRST)], flip[id(SECOND)]
    at_y = y ^ jnp.where(core == 0, first, second)
    at_x = x ^ jnp.where(core == 0, second, first)
    return ((at_z * 2 + at_y) * 2 + at_x) * 2 + core


def both_orders(place, core, steps):
    return jnp.concatenate([block_order(place, steps, 1 - core), block_order(place, steps, core)])


def plus(left, right, kind=BF16):
    return (left.astype(F32) + right.astype(F32)).astype(kind)


class Gathering:
    def __init__(self, block, steps):
        self.kept = block
        self.steps = list(steps[::-1])

    def step(self, before=(), wait=()):
        pairs = self.steps.pop(0)
        got = after(send(after(self.kept, *before), pairs), *wait)
        if self.steps:
            self.kept = jnp.concatenate([got, self.kept])
        else:
            self.kept = (got, self.kept)
            self.kept += tuple(send(half, OTHER_CORE) for half in self.kept)
        return self.kept


def place_kernel(cuts, order_ref, *refs):
    parts, outs, sems = refs[:4], refs[4:-1], refs[-1]
    block = parts[0].shape[0] // 8
    copies = []
    for index in range(32):
        part = parts[(2 + index // 8) % 4]
        for number, (row, rows, column, columns) in enumerate(cuts):
            target = outs[number].at[pl.ds(pl.multiple_of(order_ref[index] * rows, rows), rows)]
            source = part.at[pl.ds(index % 8 * block + row, rows), pl.ds(column, columns)]
            copies.append(pltpu.make_async_copy(source, target, sems.at[number * 32 + index]))
            copies[-1].start()
    for copy in copies:
        copy.wait()


def placed(parts, order, cuts):
    rows, columns = parts[0].shape
    return pl.pallas_call(
        functools.partial(place_kernel, cuts),
        grid_spec=pltpu.PrefetchScalarGridSpec(
            num_scalar_prefetch=1,
            grid=(1,),
            in_specs=[pl.BlockSpec((rows, columns), lambda i, order: (0, 0))] * 4,
            out_specs=[pl.BlockSpec(memory_space=pl.ANY)] * len(cuts),
            scratch_shapes=[pltpu.SemaphoreType.DMA((32 * len(cuts),))],
        ),
        out_shape=[jax.ShapeDtypeStruct((32 * cut[1], cut[3]), parts[0].dtype) for cut in cuts],
        compiler_params=VMEM,
        cost_estimate=pl.CostEstimate(flops=0, bytes_accessed=16 * rows * columns, transcendentals=0),
    )(order, *parts)


def after(value, *others):
    return lax.optimization_barrier((value,) + others)[0] if others else value


class Summing:
    def __init__(self, halves, steps):
        self.give, self.kept = halves
        self.steps = list(steps)

    def step(self, *wait, before=()):
        got = after(send(after(self.give, *before), self.steps.pop(0)), *wait)
        return self.add(got)

    def add(self, got):
        if self.steps:
            half = self.kept.shape[0] // 2
            self.give = plus(self.kept[:half], got[:half])
            self.kept = plus(self.kept[half:], got[half:])
            return self.give
        self.kept = plus(self.kept, got, F32)
        return self.kept

    def send_part(self, *wait):
        half = self.give.shape[0] // 2
        got = after(send(self.give[:half], self.steps[0]), *wait)
        self.later = self.give[half:]
        self.give = plus(self.kept[:half], got)
        return self.give

    def keep_part(self, *wait):
        got = after(send(after(self.later, self.give), self.steps.pop(0)), *wait)
        self.kept = plus(self.kept[self.later.shape[0] :], got)
        return self.kept

    def finish(self):
        while self.steps:
            self.step()
        return self.kept


def picked(values, order):
    columns = values.shape[1]
    block = columns // 32
    column = jnp.arange(columns)
    source = jnp.repeat(order, block) * block + column % block
    choice = (column[:, None] == source[None, :]).astype(BF16)
    return dot(values, choice, BF16)


def swapped(values):
    return send(values, OTHER_CORE)


def halves(values):
    half = values.shape[1] // 2
    return values[:, :half], values[:, half:]


def on_device(
    known,
    frames,
    skip,
    cotangent,
    segment_ids,
    row_lengths,
    w_skip,
    b_skip,
    gain_one,
    w_qkv,
    w_out,
    gain_two,
    w_up,
    b_up,
    w_down,
    b_down,
):
    micro, rows, length, width = frames.shape
    count = micro * rows
    tokens = count * length
    devices = width // gain_one.shape[0]
    hidden_width = w_up.shape[1]

    vectors = jnp.concatenate([b_skip, gain_one, gain_two, b_down, b_up])
    part = w_skip.shape[0]
    lines = -(-vectors.shape[0] // width)
    lines = -(-lines // 16) * 16
    padded = jnp.pad(vectors, (0, lines * width - vectors.shape[0])).reshape(lines, width)
    own_skip = jnp.concatenate([w_skip, padded])
    own_qkv = jnp.concatenate([w_qkv, w_out], axis=1)
    if known:
        place = lax.axis_index("dp")
        core = lax.axis_index("core")
        coords = (place // 2, place % 2, lax.axis_index("x"))
        order = both_orders(coords, core, PLANE_FIRST)
        joined = jnp.concatenate([frames.reshape(tokens, width), skip.reshape(tokens, width)], axis=1)
        give_joined, own_joined = halves(picked(joined, order))
        all_up = lax.all_gather(w_up, CORES, axis=0, tiled=True)
        all_down = lax.all_gather(w_down, CORES, axis=0, tiled=True)
        at_skip, at_qkv = (Gathering(own, PLANE_FIRST) for own in (own_skip, own_qkv))
        at_skip.step()
        near = at_qkv.step()
        joined_other, grad_other = swapped(give_joined), swapped(cotangent.reshape(tokens, width))
        far = at_skip.step(before=(near,), wait=(own_joined, joined_other, grad_other))
        at_skip.step()
        got_skip = at_skip.step()
        far = at_qkv.step(before=(far,))
        at_skip.kept = got_skip[:2] + tuple(send(after(half, far), OTHER_CORE) for half in got_skip[:2])
        got_skip = at_skip.kept
        full_skip, flat = placed(got_skip, order, ((0, part, 0, width), (part, lines, 0, width)))
        at_qkv.step()
    else:
        all_skip = lax.all_gather(own_skip, AXES, axis=0, tiled=False)
        all_qkv = lax.all_gather(own_qkv, AXES, axis=0, tiled=True)
        all_up = lax.all_gather(w_up, AXES, axis=0, tiled=True)
        all_down = lax.all_gather(w_down, AXES, axis=0, tiled=True)
        full_skip = all_skip[:, :part].reshape(devices * part, width)
        flat = all_skip[:, part:]
        full_qkv = all_qkv[:, : 3 * width]
        full_out = all_qkv[:, 3 * width :]
        joined = jnp.concatenate([frames.reshape(tokens, width), skip.reshape(tokens, width)], axis=1)
    flat = flat.reshape(devices, lines * width)
    small = width // devices
    spread = lambda at, size: flat[:, at : at + size].reshape(1, devices * size).astype(F32)
    bias_skip, gain_1, gain_2, bias_down = (spread(i * small, small) for i in range(4))
    bias_up = spread(4 * small, hidden_width // devices)

    grad_low = cotangent.reshape(tokens, width)
    grad_out = grad_low.astype(F32)
    segments = segment_ids.reshape(count, length)
    lengths = row_lengths.reshape(count, 1)
    reach = jnp.where(jnp.arange(length)[None, :] < lengths, segments, -1)
    column, row = reach[:, :, None], segments[:, None, :]
    tables = wide_tables(length)

    hidden = dot(joined, full_skip) + bias_skip
    scale_one = lax.rsqrt(jnp.mean(hidden * hidden, axis=1, keepdims=True) + EPSILON)
    unit_one = hidden * scale_one
    normed_one = (unit_one * gain_1).astype(BF16)
    if known:
        give_one, own_one = halves(picked(normed_one, order))
        got_qkv = at_qkv.step(wait=(own_one,))
        full_qkv, full_out = placed(got_qkv, order, ((0, w_qkv.shape[0], 0, 3 * width), (0, w_qkv.shape[0], 3 * width, width)))
    mixed = dot(normed_one, full_qkv)
    query, key, value, attended, lse = attend(mixed, tables, column, row, count, length)
    middle = hidden + dot(attended, full_out)
    scale_two = lax.rsqrt(jnp.mean(middle * middle, axis=1, keepdims=True) + EPSILON)
    unit_two = middle * scale_two
    normed_two = (unit_two * gain_2).astype(BF16)
    total = lambda values: jnp.sum(values, axis=0)
    back = functools.partial(attend_back, query, key, value, lse=lse, tables=tables, column=column, row=row, rows=count, length=length)

    if known:
        ends = lambda blocks: jnp.sum(jnp.where(blocks[None, :] // 2 == jnp.arange(16)[:, None], jnp.arange(16)[None, :], 0), axis=1).astype(jnp.int32)
        give_attended, own_attended = halves(picked(attended, order))
        give_two, own_two = halves(picked(normed_two, order))
        one_other, attended_other, two_other = swapped(give_one), swapped(give_attended), swapped(give_two)

        activated, slope, own_active, *give_active = up_product(
            normed_two, all_up, bias_up, ends(order[16:]), ends(order[:16]), core.reshape(1)
        )
        active_other = [swapped(piece) for piece in give_active]
        give_down = tall_product(own_active, active_other[0], grad_low, grad_other, 0)
        keep_down = tall_product(own_active, active_other[1], after(grad_low, give_down), grad_other, 1)
        down = Summing((give_down, keep_down), PLANE_FIRST)
        inner_low, inner_sum, inner_pieces = inner_back(grad_low, after(all_down, keep_down), slope)
        inner_other = [swapped(piece) for piece in inner_pieces]
        grad_normed_two = against(inner_low, all_up)
        up = Summing(wide_product((own_two, two_other, after(inner_low, grad_normed_two), inner_other)), PLANE_FIRST)
        down.step(up.give)
        grad_middle = grad_out + norm_back(after(grad_normed_two, down.give), unit_two, scale_two, gain_2)
        middle_low = grad_middle.astype(BF16)
        middle_other = swapped(middle_low)
        grad_attended = against(middle_low, full_out).astype(BF16)
        grad_mixed, *mixed_pieces = back(grad=after(grad_attended, down.give))
        mixed_other = [swapped(piece) for piece in mixed_pieces]
        down.step(grad_mixed, *mixed_other)
        up.step(grad_mixed, *mixed_other)
        both = Summing(
            wide_product(
                (own_one, one_other, after(grad_mixed, up.give, down.give), mixed_other),
                (own_attended, attended_other, middle_low, [middle_other]),
            ),
            PLANE_FIRST,
        )
        up.step(both.give)
        given = down.send_part(both.give)
        grad_normed_one = against(after(grad_mixed, both.give, up.give, given), full_qkv)
        both.send_part(grad_normed_one)
        down_kept = down.keep_part(grad_normed_one)
        grad_hidden = grad_middle + norm_back(after(grad_normed_one, both.give, down_kept), unit_one, scale_one, gain_1)
        hidden_low = grad_hidden.astype(BF16)
        hidden_other = swapped(hidden_low)
        vector_grads = (total(grad_hidden), total(grad_normed_one * unit_one), total(grad_normed_two * unit_two), total(grad_out), inner_sum[0])
        by_block = jnp.concatenate([v.reshape(devices, -1) for v in vector_grads], axis=1)
        by_block = by_block + swapped(by_block)
        choice = (order[16:, None] == jnp.arange(devices)[None, :]).astype(F32)
        by_block = jnp.dot(choice, by_block, precision=lax.Precision.HIGHEST).astype(BF16)
        by_block = jnp.pad(by_block, ((0, 0), (0, lines * width - by_block.shape[1]))).reshape(16, lines, width)
        tail = Summing(last_product(own_joined, joined_other, after(hidden_low, both.give), hidden_other, by_block), PLANE_FIRST)
        both_kept = both.keep_part(tail.give)
        down_grad = down.step(tail.give)
        grad_joined = against(after(hidden_low, both_kept, down_grad), full_skip)
        both.step(grad_joined)
        tail.step(both.give)
        up.step(both.give)
        both.send_part(tail.give)
        tail.step()
        up_grad = up.step(tail.give)
        output = (middle + (dot(after(activated, tail.give), all_down) + bias_down)).astype(BF16)
        both.keep_part(output)
        tail.step(output)
        both_grad = both.finish()
        last = tail.finish()
        qkv_grad, out_grad = both_grad[:, : 3 * width], both_grad[:, 3 * width :]
        skip_weight_grad = last[:part]
        line = last[part:].reshape(lines * width)
        shares = [line[i * small : (i + 1) * small] for i in range(4)]
        shares.append(line[4 * small : 4 * small + hidden_width // devices])
    else:
        activated, slope = gelu_parts(dot(normed_two, all_up) + bias_up)
        activated = activated.astype(BF16)
        output = (middle + (dot(activated, all_down) + bias_down)).astype(BF16)
        grad_inner = against(grad_low, all_down) * slope
        inner_low = grad_inner.astype(BF16)
        grad_normed_two = against(inner_low, all_up)
        grad_middle = grad_out + norm_back(grad_normed_two, unit_two, scale_two, gain_2)
        middle_low = grad_middle.astype(BF16)
        grad_mixed = back(grad=against(middle_low, full_out).astype(BF16))[0]
        grad_normed_one = against(grad_mixed, full_qkv)
        grad_hidden = grad_middle + norm_back(grad_normed_one, unit_one, scale_one, gain_1)
        hidden_low = grad_hidden.astype(BF16)
        grad_joined = against(hidden_low, full_skip)
        vector_grads = (total(grad_hidden), total(grad_normed_one * unit_one), total(grad_normed_two * unit_two), total(grad_out), total(grad_inner))
        scatter = lambda values: lax.psum_scatter(values, AXES, scatter_dimension=0, tiled=True)
        down_grad = scatter(contract(activated, grad_low))
        up_grad = scatter(contract(normed_two, inner_low))
        out_grad = scatter(contract(attended, middle_low))
        qkv_grad = scatter(contract(normed_one, grad_mixed))
        skip_weight_grad = scatter(contract(joined, hidden_low))
        shares = [scatter(v) for v in vector_grads]

    shape = (micro, rows, length, width)
    return (
        output.reshape(shape),
        grad_joined[:, :width].reshape(shape),
        grad_joined[:, width:].reshape(shape),
        skip_weight_grad,
        shares[0],
        shares[1],
        qkv_grad,
        out_grad,
        shares[2],
        up_grad,
        shares[4],
        down_grad,
        shares[3],
    )


def solution(mesh):
    known = mesh.shape["dp"] == 8 and mesh.shape["fsdp"] == 4
    axes = AXES
    if known:
        mesh = Mesh(mesh.devices.reshape(8, 2, 2), CORES)
        axes = CORES
    tokens = P(None, axes, None, None)
    weight = P(axes, None)
    vector = P(axes)
    return jax.shard_map(
        functools.partial(on_device, known),
        mesh=mesh,
        in_specs=(
            tokens,
            tokens,
            tokens,
            P(None, axes, None),
            P(None, axes),
            weight,
            vector,
            vector,
            weight,
            weight,
            vector,
            weight,
            vector,
            weight,
            vector,
        ),
        out_specs=(
            tokens,
            tokens,
            tokens,
            weight,
            vector,
            vector,
            weight,
            weight,
            vector,
            weight,
            vector,
            weight,
            vector,
        ),
        check_vma=False,
    )
```

```python
import functools
import math

import jax
import jax.numpy as jnp
from jax import lax
from jax.experimental import pallas as pl
from jax.experimental.pallas import tpu as pltpu
from jax.sharding import Mesh, PartitionSpec as P

HEADS = 16
HEAD = 64
EPSILON = 1e-06
AXES = ("dp", "fsdp")
CHIPS = ("dp", "x")
CORES = CHIPS + ("core",)
F32 = jnp.float32
BF16 = jnp.bfloat16
VMEM = pltpu.CompilerParams(vmem_limit_bytes=48 << 20)


def dot(left, right, kind=F32):
    return jnp.dot(left, right, preferred_element_type=F32).astype(kind)


def against(left, right):
    return lax.dot_general(left, right, (((1,), (1,)), ((), ())), preferred_element_type=F32)


def contract(left, right):
    return lax.dot_general(left, right, (((0,), (0,)), ((), ())), preferred_element_type=F32)


def wide_tables(length):
    half = HEAD // 2
    indices = jnp.arange(half, dtype=F32)
    freqs = jnp.exp(indices * (-2.0 * math.log(10000.0) / HEAD))
    angles = jnp.arange(length, dtype=F32)[:, None] * freqs[None, :]
    cosine, sine = jnp.cos(angles), jnp.sin(angles)
    return (
        jnp.concatenate([cosine] * 4, axis=1),
        jnp.concatenate([-sine, sine, -sine, sine], axis=1),
    )


def swap_halves(values):
    half = HEAD // 2
    lane = lax.broadcasted_iota(jnp.int32, values.shape, 1)
    ahead = pltpu.roll(values, 2 * HEAD - half, 1)
    behind = pltpu.roll(values, half, 1)
    return jnp.where(lax.rem(lane, HEAD) < half, ahead, behind)


def allowed_of(column_ref, row_ref):
    length = row_ref.shape[-1]
    rows = lax.broadcasted_iota(jnp.int32, (length, length), 0)
    columns = lax.broadcasted_iota(jnp.int32, (length, length), 1)
    return (column_ref[0] == row_ref[0]) | (rows == columns)


def head_part(values, which):
    lane = lax.broadcasted_iota(jnp.int32, values.shape, 1)
    return jnp.where((lane >= HEAD) == (which == 1), values, jnp.zeros_like(values))


WIDE = 2 * HEAD
GROUP = 8


def attend_kernel(q_ref, k_ref, v_ref, cos_ref, sin_ref, column_ref, row_ref, qo_ref, ko_ref, vo_ref, a_ref, lse_ref):
    cosine, sine = cos_ref[...], sin_ref[...]
    allowed = allowed_of(column_ref, row_ref)
    for pair in range(GROUP):
        lanes = slice(pair * WIDE, (pair + 1) * WIDE)
        raw_q, raw_k = q_ref[:, lanes], k_ref[:, lanes]
        query = ((raw_q * cosine + swap_halves(raw_q) * sine)).astype(BF16)
        key = (raw_k * cosine + swap_halves(raw_k) * sine).astype(BF16)
        value = v_ref[:, lanes].astype(BF16)
        scaled = query * jnp.asarray(HEAD ** (-0.5), BF16)
        qo_ref[:, lanes] = query
        ko_ref[:, lanes] = key
        vo_ref[:, lanes] = value
        total = jnp.zeros(value.shape[::-1], F32)
        for which in range(2):
            masked = jnp.where(allowed, against(key, head_part(scaled, which)), -1e30)
            highest = jnp.max(masked, axis=0, keepdims=True)
            exponent = jnp.exp(masked - highest)
            summed = jnp.sum(exponent, axis=0, keepdims=True)
            probs = (exponent * (1.0 / summed)).astype(BF16)
            total += contract(head_part(value, which), probs)
            lse_ref[0, 0, pl.ds(2 * pair + which, 1), :] = highest + jnp.log(summed)
        a_ref[:, lanes] = total.T.astype(BF16)


def attend(mixed, tables, column, row, rows, length):
    width = HEADS * HEAD
    steps = HEADS // 2 // GROUP
    wide = WIDE * GROUP
    place = lambda shift: pl.BlockSpec((length, wide), lambda r, p, s=shift: (r, p + s))
    table = pl.BlockSpec((length, WIDE), lambda r, p: (0, 0))
    narrow = jax.ShapeDtypeStruct((rows * length, width), BF16)
    return pl.pallas_call(
        attend_kernel,
        grid=(rows, steps),
        in_specs=[
            place(0),
            place(steps),
            place(2 * steps),
            table,
            table,
            pl.BlockSpec((1, length, 1), lambda r, p: (r, 0, 0)),
            pl.BlockSpec((1, 1, length), lambda r, p: (r, 0, 0)),
        ],
        out_specs=[place(0)] * 4 + [pl.BlockSpec((1, 1, 2 * GROUP, length), lambda r, p: (r, p, 0, 0))],
        out_shape=[narrow] * 4 + [jax.ShapeDtypeStruct((rows, steps, 2 * GROUP, length), F32)],
        compiler_params=VMEM,
        cost_estimate=pl.CostEstimate(flops=rows * HEADS * length * length * 512, bytes_accessed=rows * length * width * 24, transcendentals=rows * HEADS * length * length),
    )(mixed, mixed, mixed, *tables, column, row)


def attend_back_kernel(q_ref, k_ref, v_ref, g_ref, lse_ref, cos_ref, sin_ref, column_ref, row_ref, out_ref, *piece_refs):
    cosine, sine = cos_ref[...], sin_ref[...]
    allowed = allowed_of(column_ref, row_ref)
    scale = HEAD ** (-0.5)
    for pair in range(GROUP):
        lanes = slice(pair * WIDE, (pair + 1) * WIDE)
        query, key, value, grad = q_ref[:, lanes], k_ref[:, lanes], v_ref[:, lanes], g_ref[:, lanes]
        scaled = query * jnp.asarray(scale, BF16)
        grad_q = jnp.zeros(query.shape[::-1], F32)
        grad_k = jnp.zeros(query.shape, F32)
        grad_v = jnp.zeros(query.shape, F32)
        for which in range(2):
            own_query = head_part(scaled, which)
            own_grad = head_part(grad, which)
            mark = lse_ref[0, 0, pl.ds(2 * pair + which, 1), :]
            probs = jnp.exp(jnp.where(allowed, against(key, own_query), -1e30) - mark)
            grad_probs = against(value, own_grad)
            inside = jnp.sum(grad_probs * probs, axis=0, keepdims=True)
            grad_scores = (probs * (grad_probs - inside)).astype(BF16)
            grad_v += dot(probs.astype(BF16), own_grad)
            grad_k += dot(grad_scores, own_query)
            grad_q += contract(head_part(key, which), grad_scores)
        grad_q = grad_q.T * scale
        width = HEADS * HEAD
        start = pl.program_id(1) * (GROUP * WIDE) + pair * WIDE
        target = lambda part: pl.ds(pl.multiple_of(part * width + start, WIDE), WIDE)
        grad_q = grad_q * cosine - swap_halves(grad_q) * sine
        grad_k = grad_k * cosine - swap_halves(grad_k) * sine
        for part, values in enumerate((grad_q, grad_k, grad_v)):
            out_ref[:, target(part)] = values.astype(BF16)
            piece_refs[part][:, lanes] = values.astype(BF16)


def attend_back(query, key, value, grad, lse, tables, column, row, rows, length):
    width = HEADS * HEAD
    steps = HEADS // 2 // GROUP
    place = pl.BlockSpec((length, WIDE * GROUP), lambda r, p: (r, p))
    table = pl.BlockSpec((length, WIDE), lambda r, p: (0, 0))
    return pl.pallas_call(
        attend_back_kernel,
        grid=(rows, steps),
        in_specs=[place] * 4
        + [
            pl.BlockSpec((1, 1, 2 * GROUP, length), lambda r, p: (r, p, 0, 0)),
            table,
            table,
            pl.BlockSpec((1, length, 1), lambda r, p: (r, 0, 0)),
            pl.BlockSpec((1, 1, length), lambda r, p: (r, 0, 0)),
        ],
        out_specs=[pl.BlockSpec((length, 3 * width), lambda r, p: (r, 0))] + [place] * 3,
        out_shape=[jax.ShapeDtypeStruct((rows * length, 3 * width), BF16)] + [jax.ShapeDtypeStruct((rows * length, width), BF16)] * 3,
        compiler_params=VMEM,
        cost_estimate=pl.CostEstimate(flops=rows * HEADS * length * length * 1280, bytes_accessed=rows * length * width * 14, transcendentals=rows * HEADS * length * length),
    )(query, key, value, grad, lse, *tables, column, row)


def gelu_parts(values):
    cube = values * values
    arch = jnp.tanh(0.7978845608028654 * (values + 0.044715 * values * cube))
    slope = 0.5 * (1.0 + arch) + 0.5 * values * (1.0 - arch * arch) * (0.7978845608028654 * (1.0 + 3.0 * 0.044715 * cube))
    return 0.5 * values * (1.0 + arch), slope


TILE = 1024
BLOCK = 128


def up_kernel(mine_ref, other_ref, core_ref, x_ref, w_ref, b_ref, act_ref, slope_ref, own_ref, *give_refs):
    activated, slope = gelu_parts(dot(x_ref[...], w_ref[...]) + b_ref[...])
    activated = activated.astype(BF16)
    act_ref[...] = activated
    slope_ref[...] = slope.astype(BF16)
    second = core_ref[0] == 1
    pairs = TILE // 2 // BLOCK
    for pair in range(pairs):
        low = activated[:, 2 * pair * BLOCK : (2 * pair + 1) * BLOCK]
        high = activated[:, (2 * pair + 1) * BLOCK : (2 * pair + 2) * BLOCK]
        index = pl.program_id(0) * pairs + pair
        own_ref[:, pl.ds(pl.multiple_of(mine_ref[index] * BLOCK, BLOCK), BLOCK)] = jnp.where(second, high, low)
        place = other_ref[index]
        each = give_refs[0].shape[1] // BLOCK
        for number, ref in enumerate(give_refs):

            @pl.when(place // each == number)
            def _():
                ref[:, pl.ds(pl.multiple_of((place - number * each) * BLOCK, BLOCK), BLOCK)] = jnp.where(second, low, high)


def up_product(normed, weight, bias, mine, other, core):
    tokens, width = normed.shape
    columns = weight.shape[1]
    tall = pl.BlockSpec((tokens, TILE), lambda i, *_: (0, i))
    whole = lambda part: pl.BlockSpec((tokens, columns // part), lambda i, *_: (0, 0))
    return pl.pallas_call(
        up_kernel,
        grid_spec=pltpu.PrefetchScalarGridSpec(
            num_scalar_prefetch=3,
            grid=(columns // TILE,),
            in_specs=[
                pl.BlockSpec((tokens, width), lambda i, *_: (0, 0)),
                pl.BlockSpec((width, TILE), lambda i, *_: (0, i)),
                pl.BlockSpec((1, TILE), lambda i, *_: (0, i)),
            ],
            out_specs=[tall, tall, whole(2), whole(4), whole(4)],
        ),
        out_shape=[jax.ShapeDtypeStruct((tokens, n), BF16) for n in (columns, columns, columns // 2, columns // 4, columns // 4)],
        compiler_params=VMEM,
        cost_estimate=pl.CostEstimate(flops=2 * tokens * width * columns, bytes_accessed=2 * (width * columns + 3 * tokens * columns), transcendentals=tokens * columns),
    )(mine, other, core, normed, weight, bias)


PIECES = 4


def inner_kernel(g_ref, w_ref, slope_ref, low_ref, sum_ref, *piece_refs):
    grad_inner = against(g_ref[...], w_ref[...]) * slope_ref[...].astype(F32)
    low = grad_inner.astype(BF16)
    low_ref[...] = low
    sum_ref[...] = jnp.sum(grad_inner, axis=0, keepdims=True)
    for number, ref in enumerate(piece_refs):

        @pl.when(pl.program_id(0) == number)
        def _():
            ref[...] = low


def inner_back(grad_low, weight, slope):
    tokens, width = grad_low.shape
    columns = weight.shape[0]
    tile = columns // PIECES
    tall = pl.BlockSpec((tokens, tile), lambda i: (0, i))
    low, summed, *pieces = pl.pallas_call(
        inner_kernel,
        grid=(PIECES,),
        in_specs=[
            pl.BlockSpec((tokens, width), lambda i: (0, 0)),
            pl.BlockSpec((tile, width), lambda i: (i, 0)),
            tall,
        ],
        out_specs=[tall, pl.BlockSpec((1, tile), lambda i: (0, i))] + [pl.BlockSpec((tokens, tile), lambda i: (0, 0))] * PIECES,
        out_shape=[jax.ShapeDtypeStruct((tokens, columns), BF16), jax.ShapeDtypeStruct((1, columns), F32)]
        + [jax.ShapeDtypeStruct((tokens, columns // PIECES), BF16)] * PIECES,
        compiler_params=VMEM,
        cost_estimate=pl.CostEstimate(flops=2 * tokens * width * columns, bytes_accessed=2 * (width * columns + 2 * tokens * columns), transcendentals=0),
    )(grad_low, weight, slope)
    return low, summed, pieces


def tall_kernel(x_ref, xs_ref, g_ref, gs_ref, out_ref):
    out_ref[...] = (contract(x_ref[...], g_ref[...]) + contract(xs_ref[...], gs_ref[...])).astype(BF16)


def tall_product(x, x_other, g, g_other, part):
    tokens, rows = x_other.shape
    columns = g.shape[1]
    tile = rows // 2
    whole = pl.BlockSpec((tokens, columns), lambda i: (0, 0))
    return pl.pallas_call(
        tall_kernel,
        grid=(2,),
        in_specs=[pl.BlockSpec((tokens, tile), lambda i: (0, i + 2 * part)), pl.BlockSpec((tokens, tile), lambda i: (0, i)), whole, whole],
        out_specs=pl.BlockSpec((tile, columns), lambda i: (i, 0)),
        out_shape=jax.ShapeDtypeStruct((rows, columns), BF16),
        compiler_params=VMEM,
        cost_estimate=pl.CostEstimate(flops=4 * tokens * rows * columns, bytes_accessed=4 * tokens * (rows + columns) + 2 * rows * columns, transcendentals=0),
    )(x, x_other, g, g_other)


def wide_kernel(counts, *refs):
    sources, (give_ref, keep_ref) = refs[:-2], refs[-2:]
    half = give_ref.shape[0]
    at = 0
    for count, pieces in counts:
        (x_ref, xs_ref, g_ref), gs_refs = sources[:3], sources[3 : 3 + pieces]
        sources = sources[3 + pieces :]
        for number, gs_ref in enumerate(gs_refs):
            least = at + number * (count // pieces)

            @pl.when((pl.program_id(0) >= least) & (pl.program_id(0) < least + count // pieces))
            def _():
                summed = contract(x_ref[...], g_ref[...]) + contract(xs_ref[...], gs_ref[...])
                give_ref[...] = summed[:half].astype(BF16)
                keep_ref[...] = summed[half:].astype(BF16)

        at += count


def wide_product(*groups):
    tokens, rows = groups[0][0].shape
    tile = 1024
    counts, in_specs, values, at, columns = [], [], [], 0, 0
    for x, xs, g, pieces in groups:
        count = g.shape[1] // tile
        part = count // len(pieces)
        counts.append((count, len(pieces)))
        x_spec = pl.BlockSpec((tokens, rows), lambda i: (0, 0))
        g_spec = lambda start, size: pl.BlockSpec((tokens, tile), lambda i: (0, jnp.clip(i - start, 0, size - 1)))
        in_specs += [x_spec, x_spec, g_spec(at, count)] + [g_spec(at + number * part, part) for number in range(len(pieces))]
        values += [x, xs, g, *pieces]
        at += count
        columns += g.shape[1]
    return pl.pallas_call(
        functools.partial(wide_kernel, counts),
        grid=(at,),
        in_specs=in_specs,
        out_specs=[pl.BlockSpec((rows // 2, tile), lambda i: (0, i))] * 2,
        out_shape=[jax.ShapeDtypeStruct((rows // 2, columns), BF16)] * 2,
        compiler_params=VMEM,
        cost_estimate=pl.CostEstimate(flops=4 * tokens * rows * columns, bytes_accessed=4 * tokens * (rows + columns) + 2 * rows * columns, transcendentals=0),
    )(*values)


def last_kernel(x_ref, xs_ref, g_ref, gs_ref, extra_ref, give_ref, keep_ref):
    summed = (contract(x_ref[...], g_ref[...]) + contract(xs_ref[...], gs_ref[...])).astype(BF16)
    blocks, lines, width = extra_ref.shape
    part = summed.shape[0] // blocks
    for number, ref in enumerate((give_ref, keep_ref)):

        @pl.when(pl.program_id(0) // 2 == number)
        def _():
            ref[:, :part] = summed.reshape(blocks, part, width)
            ref[:, part:] = extra_ref[...]


def last_product(x, x_other, g, g_other, extra):
    tokens, rows = x.shape
    blocks, lines, width = extra.shape
    part = rows // blocks
    quarter = blocks // 4
    x_spec = pl.BlockSpec((tokens, rows // 4), lambda i: (0, i))
    g_spec = pl.BlockSpec((tokens, width), lambda i: (0, 0))
    out = lambda least: pl.BlockSpec((quarter, part + lines, width), lambda i: (jnp.clip(i - least, 0, 1), 0, 0))
    give, keep = pl.pallas_call(
        last_kernel,
        grid=(4,),
        in_specs=[x_spec, x_spec, g_spec, g_spec, pl.BlockSpec((quarter, lines, width), lambda i: (i, 0, 0))],
        out_specs=[out(0), out(2)],
        out_shape=[jax.ShapeDtypeStruct((blocks // 2, part + lines, width), BF16)] * 2,
        compiler_params=VMEM,
        cost_estimate=pl.CostEstimate(flops=4 * tokens * rows * width, bytes_accessed=4 * tokens * (rows + width) + 2 * rows * width, transcendentals=0),
    )(x, x_other, g, g_other, extra)
    flat = (blocks // 2 * (part + lines), width)
    return give.reshape(flat), keep.reshape(flat)


def norm_back(grad_normed, unit, scale, gain):
    scaled = grad_normed * gain
    return scale * (scaled - unit * jnp.mean(scaled * unit, axis=1, keepdims=True))


def pairs_of(move):
    pairs = []
    for z in range(4):
        for y in range(2):
            for x in range(2):
                for c in range(2):
                    there = move(z, y, x, c)
                    if there is not None:
                        source = ((z * 2 + y) * 2 + x) * 2 + c
                        target = ((there[0] * 2 + there[1]) * 2 + there[2]) * 2 + there[3]
                        pairs.append((source, target))
    return pairs


OTHER_CORE = pairs_of(lambda z, y, x, c: (z, y, x, 1 - c))
FIRST = pairs_of(lambda z, y, x, c: (z, 1 - y, x, c) if c == 0 else (z, y, 1 - x, c))
SECOND = pairs_of(lambda z, y, x, c: (z, y, 1 - x, c) if c == 0 else (z, 1 - y, x, c))
FAR = pairs_of(lambda z, y, x, c: (z ^ 2, y, x, c))
NEAR = pairs_of(lambda z, y, x, c: (z ^ 1, y, x, c))
PLANE_FIRST = (FIRST, SECOND, FAR, NEAR)
PLANE_LAST = (FIRST, FAR, NEAR, SECOND)


def send(values, pairs):
    return lax.ppermute(values, CORES, pairs)


def block_order(place, steps, core):
    z, y, x = place
    index = jnp.arange(16)
    flip = {}
    for level, pairs in enumerate(steps):
        flip[id(pairs)] = 1 - index // (8 >> level) % 2
    at_z = z ^ (2 * flip[id(FAR)]) ^ flip[id(NEAR)]
    first, second = flip[id(FIRST)], flip[id(SECOND)]
    at_y = y ^ jnp.where(core == 0, first, second)
    at_x = x ^ jnp.where(core == 0, second, first)
    return ((at_z * 2 + at_y) * 2 + at_x) * 2 + core


def both_orders(place, core, steps):
    return jnp.concatenate([block_order(place, steps, 1 - core), block_order(place, steps, core)])


def plus(left, right, kind=BF16):
    return (left.astype(F32) + right.astype(F32)).astype(kind)


class Gathering:
    def __init__(self, block, steps):
        self.kept = block
        self.steps = list(steps[::-1])

    def step(self, before=(), wait=()):
        pairs = self.steps.pop(0)
        got = after(send(after(self.kept, *before), pairs), *wait)
        if self.steps:
            self.kept = jnp.concatenate([got, self.kept])
        else:
            self.kept = (got, self.kept)
            self.kept += tuple(send(half, OTHER_CORE) for half in self.kept)
        return self.kept


def place_kernel(cuts, order_ref, *refs):
    parts, outs, sems = refs[:4], refs[4:-1], refs[-1]
    block = parts[0].shape[0] // 8
    copies = []
    for index in range(32):
        part = parts[(2 + index // 8) % 4]
        for number, (row, rows, column, columns) in enumerate(cuts):
            target = outs[number].at[pl.ds(pl.multiple_of(order_ref[index] * rows, rows), rows)]
            source = part.at[pl.ds(index % 8 * block + row, rows), pl.ds(column, columns)]
            copies.append(pltpu.make_async_copy(source, target, sems.at[number * 32 + index]))
            copies[-1].start()
    for copy in copies:
        copy.wait()


def placed(parts, order, cuts):
    rows, columns = parts[0].shape
    return pl.pallas_call(
        functools.partial(place_kernel, cuts),
        grid_spec=pltpu.PrefetchScalarGridSpec(
            num_scalar_prefetch=1,
            grid=(1,),
            in_specs=[pl.BlockSpec((rows, columns), lambda i, order: (0, 0))] * 4,
            out_specs=[pl.BlockSpec(memory_space=pl.ANY)] * len(cuts),
            scratch_shapes=[pltpu.SemaphoreType.DMA((32 * len(cuts),))],
        ),
        out_shape=[jax.ShapeDtypeStruct((32 * cut[1], cut[3]), parts[0].dtype) for cut in cuts],
        compiler_params=VMEM,
        cost_estimate=pl.CostEstimate(flops=0, bytes_accessed=16 * rows * columns, transcendentals=0),
    )(order, *parts)


def after(value, *others):
    return lax.optimization_barrier((value,) + others)[0] if others else value


class Summing:
    def __init__(self, halves, steps):
        self.give, self.kept = halves
        self.steps = list(steps)

    def step(self, *wait, before=()):
        got = after(send(after(self.give, *before), self.steps.pop(0)), *wait)
        return self.add(got)

    def add(self, got):
        if self.steps:
            half = self.kept.shape[0] // 2
            self.give = plus(self.kept[:half], got[:half])
            self.kept = plus(self.kept[half:], got[half:])
            return self.give
        self.kept = plus(self.kept, got, F32)
        return self.kept

    def send_part(self, *wait):
        half = self.give.shape[0] // 2
        got = after(send(self.give[:half], self.steps[0]), *wait)
        self.later = self.give[half:]
        self.give = plus(self.kept[:half], got)
        return self.give

    def keep_part(self, *wait):
        got = after(send(after(self.later, self.give), self.steps.pop(0)), *wait)
        self.kept = plus(self.kept[self.later.shape[0] :], got)
        return self.kept

    def finish(self):
        while self.steps:
            self.step()
        return self.kept


def picked(values, order):
    columns = values.shape[1]
    block = columns // 32
    column = jnp.arange(columns)
    source = jnp.repeat(order, block) * block + column % block
    choice = (column[:, None] == source[None, :]).astype(BF16)
    return dot(values, choice, BF16)


def swapped(values):
    return send(values, OTHER_CORE)


def halves(values):
    half = values.shape[1] // 2
    return values[:, :half], values[:, half:]


def on_device(
    known,
    frames,
    skip,
    cotangent,
    segment_ids,
    row_lengths,
    w_skip,
    b_skip,
    gain_one,
    w_qkv,
    w_out,
    gain_two,
    w_up,
    b_up,
    w_down,
    b_down,
):
    micro, rows, length, width = frames.shape
    count = micro * rows
    tokens = count * length
    devices = width // gain_one.shape[0]
    hidden_width = w_up.shape[1]

    vectors = jnp.concatenate([b_skip, gain_one, gain_two, b_down, b_up])
    part = w_skip.shape[0]
    lines = -(-vectors.shape[0] // width)
    lines = -(-lines // 16) * 16
    padded = jnp.pad(vectors, (0, lines * width - vectors.shape[0])).reshape(lines, width)
    own_skip = jnp.concatenate([w_skip, padded])
    own_qkv = jnp.concatenate([w_qkv, w_out], axis=1)
    if known:
        place = lax.axis_index("dp")
        core = lax.axis_index("core")
        coords = (place // 2, place % 2, lax.axis_index("x"))
        order = both_orders(coords, core, PLANE_FIRST)
        joined = jnp.concatenate([frames.reshape(tokens, width), skip.reshape(tokens, width)], axis=1)
        give_joined, own_joined = halves(picked(joined, order))
        all_up = lax.all_gather(w_up, CORES, axis=0, tiled=True)
        all_down = lax.all_gather(w_down, CORES, axis=0, tiled=True)
        at_skip, at_qkv = (Gathering(own, PLANE_FIRST) for own in (own_skip, w_qkv))
        at_out = Gathering(w_out, PLANE_FIRST)
        at_skip.step()
        near = at_qkv.step()
        joined_other, grad_other = swapped(give_joined), swapped(cotangent.reshape(tokens, width))
        near_out = at_out.step()
        far = at_skip.step(before=(near, near_out), wait=(own_joined, joined_other, grad_other))
        second = at_skip.step()
        got_skip = at_skip.step()
        far = at_qkv.step(before=(far,), wait=(second,))
        far_out = at_out.step(before=(far,))
        at_skip.kept = got_skip[:2] + tuple(send(after(half, far), OTHER_CORE) for half in got_skip[:2])
        got_skip = at_skip.kept
        full_skip, flat = placed(got_skip, order, ((0, part, 0, width), (part, lines, 0, width)))
        at_qkv.step()
    else:
        all_skip = lax.all_gather(own_skip, AXES, axis=0, tiled=False)
        all_qkv = lax.all_gather(own_qkv, AXES, axis=0, tiled=True)
        all_up = lax.all_gather(w_up, AXES, axis=0, tiled=True)
        all_down = lax.all_gather(w_down, AXES, axis=0, tiled=True)
        full_skip = all_skip[:, :part].reshape(devices * part, width)
        flat = all_skip[:, part:]
        full_qkv = all_qkv[:, : 3 * width]
        full_out = all_qkv[:, 3 * width :]
        joined = jnp.concatenate([frames.reshape(tokens, width), skip.reshape(tokens, width)], axis=1)
    flat = flat.reshape(devices, lines * width)
    small = width // devices
    spread = lambda at, size: flat[:, at : at + size].reshape(1, devices * size).astype(F32)
    bias_skip, gain_1, gain_2, bias_down = (spread(i * small, small) for i in range(4))
    bias_up = spread(4 * small, hidden_width // devices)

    grad_low = cotangent.reshape(tokens, width)
    grad_out = grad_low.astype(F32)
    segments = segment_ids.reshape(count, length)
    lengths = row_lengths.reshape(count, 1)
    reach = jnp.where(jnp.arange(length)[None, :] < lengths, segments, -1)
    column, row = reach[:, :, None], segments[:, None, :]
    tables = wide_tables(length)

    hidden = dot(joined, full_skip) + bias_skip
    scale_one = lax.rsqrt(jnp.mean(hidden * hidden, axis=1, keepdims=True) + EPSILON)
    unit_one = hidden * scale_one
    normed_one = (unit_one * gain_1).astype(BF16)
    if known:
        give_one, own_one = halves(picked(normed_one, order))
        got_qkv = at_qkv.step(before=(far_out,), wait=(own_one,))
        (full_qkv,) = placed(got_qkv, order, ((0, w_qkv.shape[0], 0, 3 * width),))
        at_out.step(before=got_qkv[:2], wait=(full_qkv,))
    mixed = dot(normed_one, full_qkv)
    if known:
        got_out = at_out.step(wait=(mixed,))
        mixed = after(mixed, *got_out[:2])
    query, key, value, attended, lse = attend(mixed, tables, column, row, count, length)
    if known:
        (full_out,) = placed(got_out, order, ((0, w_out.shape[0], 0, width),))
    middle = hidden + dot(attended, full_out)
    scale_two = lax.rsqrt(jnp.mean(middle * middle, axis=1, keepdims=True) + EPSILON)
    unit_two = middle * scale_two
    normed_two = (unit_two * gain_2).astype(BF16)
    total = lambda values: jnp.sum(values, axis=0)
    back = functools.partial(attend_back, query, key, value, lse=lse, tables=tables, column=column, row=row, rows=count, length=length)

    if known:
        ends = lambda blocks: jnp.sum(jnp.where(blocks[None, :] // 2 == jnp.arange(16)[:, None], jnp.arange(16)[None, :], 0), axis=1).astype(jnp.int32)
        give_attended, own_attended = halves(picked(attended, order))
        give_two, own_two = halves(picked(normed_two, order))
        one_other, attended_other, two_other = swapped(give_one), swapped(give_attended), swapped(give_two)

        activated, slope, own_active, *give_active = up_product(
            normed_two, all_up, bias_up, ends(order[16:]), ends(order[:16]), core.reshape(1)
        )
        active_other = [swapped(piece) for piece in give_active]
        give_down = tall_product(own_active, active_other[0], grad_low, grad_other, 0)
        keep_down = tall_product(own_active, active_other[1], after(grad_low, give_down), grad_other, 1)
        down = Summing((give_down, keep_down), PLANE_FIRST)
        inner_low, inner_sum, inner_pieces = inner_back(grad_low, after(all_down, keep_down), slope)
        inner_other = [swapped(piece) for piece in inner_pieces]
        grad_normed_two = against(inner_low, all_up)
        up = Summing(wide_product((own_two, two_other, after(inner_low, grad_normed_two), inner_other)), PLANE_FIRST)
        down.step(up.give)
        grad_middle = grad_out + norm_back(after(grad_normed_two, down.give), unit_two, scale_two, gain_2)
        middle_low = grad_middle.astype(BF16)
        middle_other = swapped(middle_low)
        grad_attended = against(middle_low, full_out).astype(BF16)
        grad_mixed, *mixed_pieces = back(grad=after(grad_attended, down.give))
        mixed_other = [swapped(piece) for piece in mixed_pieces]
        down.step(grad_mixed, *mixed_other)
        up.step(grad_mixed, *mixed_other)
        both = Summing(
            wide_product(
                (own_one, one_other, after(grad_mixed, up.give, down.give), mixed_other),
                (own_attended, attended_other, middle_low, [middle_other]),
            ),
            PLANE_FIRST,
        )
        up.step(both.give)
        given = down.send_part(both.give)
        grad_normed_one = against(after(grad_mixed, both.give, up.give, given), full_qkv)
        both.send_part(grad_normed_one)
        down_kept = down.keep_part(grad_normed_one)
        grad_hidden = grad_middle + norm_back(after(grad_normed_one, both.give, down_kept), unit_one, scale_one, gain_1)
        hidden_low = grad_hidden.astype(BF16)
        hidden_other = swapped(hidden_low)
        vector_grads = (total(grad_hidden), total(grad_normed_one * unit_one), total(grad_normed_two * unit_two), total(grad_out), inner_sum[0])
        by_block = jnp.concatenate([v.reshape(devices, -1) for v in vector_grads], axis=1)
        by_block = by_block + swapped(by_block)
        choice = (order[16:, None] == jnp.arange(devices)[None, :]).astype(F32)
        by_block = jnp.dot(choice, by_block, precision=lax.Precision.HIGHEST).astype(BF16)
        by_block = jnp.pad(by_block, ((0, 0), (0, lines * width - by_block.shape[1]))).reshape(16, lines, width)
        tail = Summing(last_product(own_joined, joined_other, after(hidden_low, both.give), hidden_other, by_block), PLANE_FIRST)
        both_kept = both.keep_part(tail.give)
        down_grad = down.step(tail.give)
        grad_joined = against(after(hidden_low, both_kept, down_grad), full_skip)
        both.step(grad_joined)
        tail.step(both.give)
        up.step(both.give)
        both.send_part(tail.give)
        tail.step()
        up_grad = up.step(tail.give)
        output = (middle + (dot(after(activated, tail.give), all_down) + bias_down)).astype(BF16)
        both.keep_part(output)
        tail.step(output)
        both_grad = both.finish()
        last = tail.finish()
        qkv_grad, out_grad = both_grad[:, : 3 * width], both_grad[:, 3 * width :]
        skip_weight_grad = last[:part]
        line = last[part:].reshape(lines * width)
        shares = [line[i * small : (i + 1) * small] for i in range(4)]
        shares.append(line[4 * small : 4 * small + hidden_width // devices])
    else:
        activated, slope = gelu_parts(dot(normed_two, all_up) + bias_up)
        activated = activated.astype(BF16)
        output = (middle + (dot(activated, all_down) + bias_down)).astype(BF16)
        grad_inner = against(grad_low, all_down) * slope
        inner_low = grad_inner.astype(BF16)
        grad_normed_two = against(inner_low, all_up)
        grad_middle = grad_out + norm_back(grad_normed_two, unit_two, scale_two, gain_2)
        middle_low = grad_middle.astype(BF16)
        grad_mixed = back(grad=against(middle_low, full_out).astype(BF16))[0]
        grad_normed_one = against(grad_mixed, full_qkv)
        grad_hidden = grad_middle + norm_back(grad_normed_one, unit_one, scale_one, gain_1)
        hidden_low = grad_hidden.astype(BF16)
        grad_joined = against(hidden_low, full_skip)
        vector_grads = (total(grad_hidden), total(grad_normed_one * unit_one), total(grad_normed_two * unit_two), total(grad_out), total(grad_inner))
        scatter = lambda values: lax.psum_scatter(values, AXES, scatter_dimension=0, tiled=True)
        down_grad = scatter(contract(activated, grad_low))
        up_grad = scatter(contract(normed_two, inner_low))
        out_grad = scatter(contract(attended, middle_low))
        qkv_grad = scatter(contract(normed_one, grad_mixed))
        skip_weight_grad = scatter(contract(joined, hidden_low))
        shares = [scatter(v) for v in vector_grads]

    shape = (micro, rows, length, width)
    return (
        output.reshape(shape),
        grad_joined[:, :width].reshape(shape),
        grad_joined[:, width:].reshape(shape),
        skip_weight_grad,
        shares[0],
        shares[1],
        qkv_grad,
        out_grad,
        shares[2],
        up_grad,
        shares[4],
        down_grad,
        shares[3],
    )


def solution(mesh):
    known = mesh.shape["dp"] == 8 and mesh.shape["fsdp"] == 4
    axes = AXES
    if known:
        mesh = Mesh(mesh.devices.reshape(8, 2, 2), CORES)
        axes = CORES
    tokens = P(None, axes, None, None)
    weight = P(axes, None)
    vector = P(axes)
    return jax.shard_map(
        functools.partial(on_device, known),
        mesh=mesh,
        in_specs=(
            tokens,
            tokens,
            tokens,
            P(None, axes, None),
            P(None, axes),
            weight,
            vector,
            vector,
            weight,
            weight,
            vector,
            weight,
            vector,
            weight,
            vector,
        ),
        out_specs=(
            tokens,
            tokens,
            tokens,
            weight,
            vector,
            vector,
            weight,
            weight,
            vector,
            weight,
            vector,
            weight,
            vector,
        ),
        check_vma=False,
    )
```
